32 devices in a mesh: dp: 8 (over z, y), tensor: 4 (over x, core).
Axes of the slice: x: 2, y: 2, z: 4, core: 2. Of those that a mesh axis runs over, the one named last changes fastest.
Arguments:
- inputs: bfloat16 [64, 197, 512], P('dp'), may hold values from -24 to 24
- valid_mask: int32 [64, 197], P('dp'), may hold values from 0 to 1
- expert_ids: int32 [64, 197, 2], P('dp'), may hold values from 0 to 31, as said below
- slot_ids: int32 [64, 197, 2], P('dp'), may hold values from 0 to 104, as said below
- norm1_gain: bfloat16 [512], replicated, may hold values from 0.5 to 1.5
- norm1_bias: bfloat16 [512], replicated, may hold values from -3 to 3
- w_qkv: bfloat16 [512, 3, 512], P(None, None, 'tensor'), may hold values from -2 to 2
- b_qv: bfloat16 [2, 512], P(None, 'tensor'), may hold values from -3 to 3
- w_out: bfloat16 [512, 512], P('tensor'), may hold values from -1.5 to 1.5
- b_out: bfloat16 [512], replicated, may hold values from -3 to 3
- norm2_gain: bfloat16 [512], replicated, may hold values from 0.5 to 1.5
- norm2_bias: bfloat16 [512], replicated, may hold values from -3 to 3
- w_router: bfloat16 [512, 32], replicated, may hold values from -0.1875 to 0.1875
- w_in: bfloat16 [32, 512, 2048], P('dp', None, 'tensor'), may hold values from -2 to 2
- b_in: bfloat16 [32, 2048], P('dp', 'tensor'), may hold values from -1.5 to 1.5
- w_back: bfloat16 [32, 2048, 512], P('dp', 'tensor'), may hold values from -0.25 to 0.25
- b_back: bfloat16 [32, 512], replicated, may hold values from -1.5 to 1.5
- cotangent: bfloat16 [64, 197, 512], P('dp'), may hold values from -24 to 24
Outputs:
- output: float32 [64, 197, 512], P('dp')
- d_inputs: float32 [64, 197, 512], P('dp')
- g_norm1_gain: float32 [512], replicated
- g_norm1_bias: float32 [512], replicated
- g_w_qkv: float32 [512, 3, 512], P(None, None, 'tensor')
- g_b_qv: float32 [2, 512], P(None, 'tensor')
- g_w_out: float32 [512, 512], P('tensor')
- g_b_out: float32 [512], replicated
- g_norm2_gain: float32 [512], replicated
- g_norm2_bias: float32 [512], replicated
- g_w_router: float32 [512, 32], replicated
- g_w_in: float32 [32, 512, 2048], P('dp', None, 'tensor')
- g_b_in: float32 [32, 2048], P('dp', 'tensor')
- g_w_back: float32 [32, 2048, 512], P('dp', 'tensor')
- g_b_back: float32 [32, 512], replicated
- grad_norms: float32 [13], replicated
- rms_values: float32 [5], replicated
The draws below stay inside these ranges and needn't reach their ends.
Inputs may be any that keep to these rules, and one draw needn't show every extreme that they name: `expert_ids`: the two experts of a token differ. `slot_ids`: among the tokens of one block of 8 images, routes to one expert that hold a row below 104 hold different rows; 104 marks a dropped route, and every route of an invalid token is dropped. In every block some expert has all 104 rows used and some route dropped, and one expert has all rows used in every block.
All inputs are finite; a program needn't handle non-finite values.
Results may differ from the reference program's by a relative error of at most 0.025.
Values may be sent and summed in bfloat16 or wider, within the bound.
No kernel may reach another device: no remote copies, remote signals or barrier semaphores. Data moves between devices by JAX's collectives and lax.ppermute only.
A program may use at most 192 MiB of HBM per device.

```python
import math
import jax
import jax.numpy as jnp
from jax import lax

D = 512
HD = 64
FF = 2048
EXPERTS = 32
SEQ = 197
IMG_DEV = 8
CAP = 104
IMAGES = 64


def routing(key):
    blocks = IMAGES // IMG_DEV
    block_width = IMG_DEV * SEQ
    subkeys = jax.random.split(key, 5)
    orders = jax.vmap(lambda subkey: jax.random.permutation(subkey, block_width))(jax.random.split(subkeys[0], blocks))
    forced = orders <= CAP
    valid_rows = jnp.where(forced, 1, (jax.random.randint(subkeys[1], (blocks, block_width), 0, 8) > 0).astype(jnp.int32))
    favored = jax.random.randint(subkeys[2], (), 0, EXPERTS)
    labels = jnp.arange(EXPERTS, dtype=jnp.int32)
    bonuses = jax.random.randint(subkeys[3], (blocks, 1, EXPERTS), 0, 1 << 16)
    base_score = jax.random.randint(subkeys[4], (blocks, block_width, EXPERTS), 0, 1 << 16)
    boosts = jnp.where(forced[:, :, None] & (labels == favored), 1 << 18, 0)
    scores = (base_score + bonuses + boosts) * EXPERTS + labels
    chosen = lax.top_k(scores, 2)[1].astype(jnp.int32)
    matches = (chosen[:, :, :, None] == labels).astype(jnp.int32) * valid_rows[:, :, None, None]
    ordered = jnp.transpose(matches, (0, 2, 1, 3)).reshape(blocks, 2 * block_width, EXPERTS)
    before = jnp.cumsum(ordered, axis=1) - ordered
    ranks = jnp.sum(before * ordered, axis=2).reshape(blocks, 2, block_width)
    ranks = jnp.transpose(ranks, (0, 2, 1))
    slot_rows = jnp.where((valid_rows[:, :, None] > 0) & (ranks < CAP), ranks, CAP)
    return (valid_rows.reshape(IMAGES, SEQ).astype(jnp.int32), chosen.reshape(IMAGES, SEQ, 2), slot_rows.reshape(IMAGES, SEQ, 2).astype(jnp.int32))


def image_scales(image_count, top_ratio, falling):
    position = jnp.arange(image_count, dtype=jnp.float32) / max(image_count - 1, 1)
    position = jnp.abs(falling - position)
    return jnp.exp(position * math.log(top_ratio))


def draw_valid_mask(key, part):
    return routing(key)[0]


def draw_expert_ids(key, part):
    return routing(key)[1]


def draw_slot_ids(key, part):
    return routing(key)[2]


def draw_inputs(key, part):
    key = jax.random.fold_in(key, 11)
    base_key = jax.random.fold_in(key, 0)
    values = jax.random.truncated_normal(base_key, -8.0, 8.0, (IMAGES, SEQ, D), jnp.float32)
    return (values * image_scales(IMAGES, 3.0, 0.0)[:, None, None]).astype(jnp.bfloat16)


def draw_cotangent(key, part):
    key = jax.random.fold_in(key, 13)
    base_key = jax.random.fold_in(key, 0)
    values = jax.random.truncated_normal(base_key, -8.0, 8.0, (IMAGES, SEQ, D), jnp.float32)
    return (values * image_scales(IMAGES, 3.0, 1.0)[:, None, None]).astype(jnp.bfloat16)


def draw_w_qkv(key, part):
    key = jax.random.fold_in(key, 17)
    own_key, shared_key = jax.random.split(key)
    factor = D ** (-0.5)
    own = jax.random.truncated_normal(own_key, -6.0, 6.0, (D, 3, D), jnp.float32)
    shared = jax.random.truncated_normal(shared_key, -6.0, 6.0, (1, 3, D), jnp.float32)
    return ((own + shared) * factor).astype(jnp.bfloat16)


def draw_w_in(key, part):
    key = jax.random.fold_in(key, 19)
    own_key, shared_key = jax.random.split(key)
    factor = D ** (-0.5)
    own = jax.random.truncated_normal(own_key, -6.0, 6.0, (EXPERTS, D, FF), jnp.float32)
    shared = jax.random.truncated_normal(shared_key, -6.0, 6.0, (EXPERTS, 1, FF), jnp.float32)
    return ((own + 1.5 * shared) * factor).astype(jnp.bfloat16)


def shard_levels(stream_key, shape, cuts, least, largest):
    def one(axis_at, blocks):
        heights = jax.random.uniform(jax.random.fold_in(jax.random.fold_in(stream_key, 6), axis_at), (blocks,), jnp.float32, least / len(cuts), largest / len(cuts))
        return jnp.repeat(jnp.exp(heights), shape[axis_at] // blocks).reshape((-1,) + (1,) * (len(shape) - axis_at - 1))

    level = one(*cuts[0])
    for cut in cuts[1:]:
        level = level * one(*cut)
    return level


def centred(key, dims, scale, bound, shards=(), kind=jnp.bfloat16):
    array = scale * jax.random.normal(key, dims, jnp.float32)
    if shards:
        array = array * shard_levels(key, dims, shards, -0.22, 0.18)
    return jnp.clip(array, -bound, bound).astype(kind)


def setup_inputs(seed: int = 0) -> dict:
    key_list = jax.random.split(jax.random.key(seed), 19)
    return {
        "inputs": draw_inputs(jax.random.fold_in(key_list[18], 71), 0),
        "valid_mask": draw_valid_mask(jax.random.fold_in(key_list[18], 71), 0),
        "expert_ids": draw_expert_ids(jax.random.fold_in(key_list[18], 71), 0),
        "slot_ids": draw_slot_ids(jax.random.fold_in(key_list[18], 71), 0),
        "norm1_gain": jnp.clip(1.0 + 0.1 * jax.random.normal(key_list[4], (D,), jnp.float32), 0.5, 1.5).astype(jnp.bfloat16),
        "norm1_bias": centred(key_list[5], (D,), 0.2, 3.0),
        "w_qkv": draw_w_qkv(jax.random.fold_in(key_list[18], 71), 0),
        "b_qv": centred(key_list[7], (2, D), 0.2, 3.0, ((1, 4),)),
        "w_out": centred(key_list[8], (D, D), (D // 32) ** -0.5, 1.5, ((0, 4),)),
        "b_out": centred(key_list[9], (D,), 0.2, 3.0),
        "norm2_gain": jnp.clip(1.0 + 0.1 * jax.random.normal(key_list[10], (D,), jnp.float32), 0.5, 1.5).astype(jnp.bfloat16),
        "norm2_bias": centred(key_list[11], (D,), 0.2, 3.0),
        "w_router": centred(key_list[12], (D, EXPERTS), (2 * D) ** -0.5, 0.1875),
        "w_in": draw_w_in(jax.random.fold_in(key_list[18], 71), 0),
        "b_in": centred(key_list[14], (EXPERTS, FF), 0.1, 1.5, ((0, 8), (1, 4))),
        "w_back": centred(key_list[15], (EXPERTS, FF, D), (FF // 4) ** -0.5, 0.25, ((0, 8), (1, 4))),
        "b_back": centred(key_list[16], (EXPERTS, D), 0.1, 1.5),
        "cotangent": draw_cotangent(jax.random.fold_in(key_list[18], 71), 0),
    }


highest = lax.Precision.HIGHEST

@jax.custom_vjp
def low(v):
    return lax.optimization_barrier(v.astype(jnp.bfloat16)).astype(jnp.float32)

@jax.custom_vjp
def low_back(v):
    return v

def low_keep(v):
    return (low(v), None)

def low_pass(kept, grad):
    return (grad,)

def back_keep(v):
    return (v, None)

def back_low(kept, grad):
    return (low(grad),)
low.defvjp(low_keep, low_pass)
low_back.defvjp(back_keep, back_low)

def layer_norm(values, gain, shift):
    average = lax.optimization_barrier(jnp.mean(values, axis=-1, keepdims=True))
    centered = values - average
    inv_std = lax.rsqrt(lax.optimization_barrier(jnp.mean(centered * centered, axis=-1, keepdims=True)) + 1e-06)
    return centered * inv_std * gain + shift

def attend(normed, key_valid, qkv_weight, bias_full):
    images = normed.shape[0]
    heads = D // HD
    project = jnp.einsum('isd,dce->isce', normed, qkv_weight, precision=highest) + bias_full
    project = low(low_back(project))
    queries = project[:, :, 0].reshape(images, SEQ, heads, HD)
    key_rows = project[:, :, 1].reshape(images, SEQ, heads, HD)
    value_rows = project[:, :, 2].reshape(images, SEQ, heads, HD)
    scores = jnp.einsum('iqhe,ikhe->ihqk', queries, key_rows, precision=highest) * HD ** (-0.5)
    scores = low_back(scores)
    scores = jnp.where(key_valid[:, None, None, :] > 0, scores, -1e+30)
    probabilities = jax.nn.softmax(scores, axis=-1)
    mixed = jnp.einsum('ihqk,ikhe->iqhe', low(probabilities), value_rows, precision=highest)
    return mixed.reshape(images, SEQ, D)

def mix_experts(row_block, route_ids, route_slots, gate_weights, in_weight, in_bias, back_weight, back_bias):
    kept_mask = route_slots < CAP
    flat_index = jnp.where(kept_mask, route_ids * CAP + route_slots, EXPERTS * CAP)
    spread = jnp.broadcast_to(row_block[:, None, :], (row_block.shape[0], 2, D)).reshape(-1, D)
    dispatched = jnp.zeros((EXPERTS * CAP, D), jnp.float32).at[flat_index.reshape(-1)].add(spread, mode='drop')
    dispatched = dispatched.reshape(EXPERTS, CAP, D)
    pre_act = low_back(jnp.einsum('ecd,edf->ecf', dispatched, in_weight, precision=highest) + in_bias[:, None, :])
    hidden = low(jax.nn.gelu(pre_act, approximate=False))
    results = low_back(jnp.einsum('ecf,efd->ecd', hidden, back_weight, precision=highest) + back_bias[:, None, :])
    picked = jnp.take(results.reshape(EXPERTS * CAP, D), jnp.minimum(flat_index, EXPERTS * CAP - 1), axis=0)
    picked = jnp.where(kept_mask[:, :, None], picked, 0.0)
    return lax.optimization_barrier(jnp.sum(picked * gate_weights[:, :, None], axis=1))

def reference(inputs, valid_mask, expert_ids, slot_ids, norm1_gain, norm1_bias, w_qkv, b_qv, w_out, b_out, norm2_gain, norm2_bias, w_router, w_in, b_in, w_back, b_back, cotangent):
    groups = IMAGES // IMG_DEV
    block_rows = IMG_DEV * SEQ

    def forward(stream, gain_one, shift_one, qkv_weight, qv_bias, out_weight, out_bias, gain_two, shift_two, router_weight, in_weight, in_bias, back_weight, back_bias):
        normed = low(layer_norm(stream, gain_one, shift_one))
        bias_full = jnp.stack([qv_bias[0], jnp.zeros_like(qv_bias[0]), qv_bias[1]])

        def attend_group(group_data):
            return attend(group_data[0], group_data[1], qkv_weight, bias_full)
        attended = lax.map(jax.checkpoint(attend_group), (normed.reshape(groups, IMG_DEV, SEQ, D), valid_mask.reshape(groups, IMG_DEV, SEQ)))
        attended = low(low_back(attended.reshape(IMAGES, SEQ, D)))
        branch = low_back(jnp.einsum('isc,cd->isd', attended, out_weight, precision=highest) + out_bias)
        middle = stream + branch
        normed2 = low(layer_norm(middle, gain_two, shift_two))
        logits = low_back(jnp.einsum('isd,de->ise', normed2, router_weight, precision=highest))
        gate_weights = jax.nn.softmax(jnp.take_along_axis(logits, expert_ids, axis=-1), axis=-1)

        def expert_group(group_data):
            return mix_experts(group_data[0], group_data[1], group_data[2], group_data[3], in_weight, in_bias, back_weight, back_bias)
        mixture = lax.map(jax.checkpoint(expert_group), (normed2.reshape(groups, block_rows, D), expert_ids.reshape(groups, block_rows, 2), slot_ids.reshape(groups, block_rows, 2), gate_weights.reshape(groups, block_rows, 2)))
        mixture = mixture.reshape(IMAGES, SEQ, D)
        output = middle + mixture
        return (output, (middle, branch, mixture))
    params = [entry.astype(jnp.float32) for entry in (inputs, norm1_gain, norm1_bias, w_qkv, b_qv, w_out, b_out, norm2_gain, norm2_bias, w_router, w_in, b_in, w_back, b_back)]
    output, pullback, extras = jax.vjp(forward, *params, has_aux=True)
    grads = pullback(cotangent.astype(jnp.float32))
    d_inputs = grads[0]
    weight_grads = grads[1:]
    grad_norms = jnp.stack([jnp.sqrt(jnp.sum(gradient * gradient)) for gradient in weight_grads])
    weights_valid = valid_mask.astype(jnp.float32)[:, :, None]
    counted = jnp.sum(valid_mask.astype(jnp.float32))
    fields = (extras[0], extras[1], extras[2], output, d_inputs)
    rms_values = jnp.stack([jnp.sqrt(jnp.sum(field * field * weights_valid) / (counted * D)) for field in fields])
    return (output, d_inputs, weight_grads[0], weight_grads[1], weight_grads[2], weight_grads[3], weight_grads[4], weight_grads[5], weight_grads[6], weight_grads[7], weight_grads[8], weight_grads[9], weight_grads[10], weight_grads[11], weight_grads[12], grad_norms, rms_values)
```

```python
import functools

import jax
import jax.numpy as jnp
from jax import lax
from jax.experimental import pallas as pl
from jax.experimental.pallas import tpu as pltpu
from jax.sharding import PartitionSpec as P

D = 512
HD = 64
EXPERTS = 32
SEQ = 197
CAP = 104
PAD = 208
LANES = 128
F32 = jnp.float32
BF16 = jnp.bfloat16
VMEM_BYTES = 56 * 2**20


def nn(a, b):
    return lax.dot_general(a, b, (((1,), (0,)), ((), ())), preferred_element_type=F32)


def nt(a, b):
    return lax.dot_general(a, b, (((1,), (1,)), ((), ())), preferred_element_type=F32)


def tn(a, b):
    return lax.dot_general(a, b, (((0,), (0,)), ((), ())), preferred_element_type=F32)


def swap(value, axis, size, by):
    return lax.ppermute(value, axis, [(at, at ^ by) for at in range(size)])


def run(kernel, scalars, ins, outs, scratch=(), grid=(1,), own=None, out_specs=None, flops=0):
    own = own or {}
    out_specs = out_specs or {}

    def whole(shape):
        return pl.BlockSpec(shape, lambda step, s, nd=len(shape): (0,) * nd)

    in_specs = [own[i] if i in own else whole(a.shape) for i, a in enumerate(ins)]
    specs = [out_specs[i] if i in out_specs else whole(o[0]) for i, o in enumerate(outs)]
    moved = sum(a.size * a.dtype.itemsize for a in ins)
    return pl.pallas_call(
        kernel,
        grid_spec=pltpu.PrefetchScalarGridSpec(
            num_scalar_prefetch=1,
            grid=grid,
            in_specs=in_specs,
            out_specs=specs,
            scratch_shapes=list(scratch),
        ),
        out_shape=[jax.ShapeDtypeStruct(shape, dtype) for shape, dtype in outs],
        compiler_params=pltpu.CompilerParams(vmem_limit_bytes=VMEM_BYTES),
        cost_estimate=pl.CostEstimate(flops=flops, bytes_accessed=moved, transcendentals=0),
    )(scalars, *ins)


def send_cotangent_kernel(images, chunks, s_ref, flat_ref, other_ref, target_ref, cot_ref, *outs):
    target = target_ref[...]
    rows = chunks * CAP
    total = jnp.zeros((rows, D), F32)
    others = jnp.zeros((rows, SEQ), F32)
    for image in range(images):
        flat = flat_ref[image][:, :SEQ]
        other = other_ref[image][:, :SEQ]
        first = target == flat[0:1, :]
        second = target == flat[1:2, :]
        total += nn((first | second).astype(F32).astype(BF16), cot_ref[image])
        others += jnp.where(first, other[0:1, :], 0.0) + jnp.where(second, other[1:2, :], 0.0)
    other_column = jnp.sum(others, axis=1, keepdims=True)
    wide = jnp.broadcast_to(other_column, (rows, LANES))
    for chunk in range(chunks):
        outs[chunk][:, :D] = total[chunk * CAP : (chunk + 1) * CAP].astype(BF16)
        outs[chunk][:, D:] = wide[chunk * CAP : (chunk + 1) * CAP].astype(BF16)


def dispatch_kernel(groups, images, chunks, s_ref, flat_ref, target_ref, *refs):
    tokens, outs = refs[:groups], refs[groups:]
    me = s_ref[0]
    target = target_ref[...]
    total = jnp.zeros((chunks * CAP, D), F32)
    for group in range(groups):
        for image in range(images):
            flat = flat_ref[jnp.bitwise_xor(me, group) * images + image]
            hit = (target == flat[0:1, :]) | (target == flat[1:2, :])
            total += nn(
                hit.astype(F32).astype(BF16), tokens[group][image * PAD : (image + 1) * PAD, :]
            )
    for chunk in range(chunks):
        outs[chunk][...] = total[chunk * CAP : (chunk + 1) * CAP].astype(BF16)


def combine_kernel(groups, images, chunks, s_ref, flat_ref, target_ref, *refs):
    rows_in, outs, rows_wide = refs[:chunks], refs[chunks : chunks + groups], refs[-1]
    me = s_ref[0]
    for chunk in range(chunks):
        rows_wide[chunk * CAP : (chunk + 1) * CAP, :] = rows_in[chunk][...].astype(F32)
    rows = rows_wide[...].astype(BF16)
    target = target_ref[...]
    for group in range(groups):
        for image in range(images):
            flat = flat_ref[jnp.bitwise_xor(me, group) * images + image]
            hit = (flat[:, 0:1] == target) | (flat[:, 1:2] == target)
            outs[group][image * PAD : (image + 1) * PAD, :] = nn(
                hit.astype(F32).astype(BF16), rows
            ).astype(BF16)


def normalize(values):
    average = jnp.mean(values, axis=-1, keepdims=True)
    centered = values - average
    inv_std = lax.rsqrt(jnp.mean(centered * centered, axis=-1, keepdims=True) + 1e-06)
    return centered * inv_std, inv_std


def norm_pull(upstream, normal, inv_std, gain):
    scaled = upstream * gain
    inner = jnp.mean(scaled * normal, axis=-1, keepdims=True)
    return inv_std * (scaled - jnp.mean(scaled, axis=-1, keepdims=True) - normal * inner)


def load_images(images, source_ref, wide_ref):
    wide_ref[...] = jnp.zeros_like(wide_ref)
    for image in range(images):
        wide_ref[image * PAD : image * PAD + SEQ, :] = source_ref[image].astype(F32)
    return wide_ref[...]


def masked_scores(queries, key_rows, key_mask):
    scores = nt(queries, key_rows) * HD ** (-0.5)
    return jnp.where(key_mask > 0, scores, jnp.where(key_mask < 0, -2e30, -1e30))


def softmax_rows(scores):
    exps = jnp.exp(scores - jnp.max(scores, axis=-1, keepdims=True))
    return exps / jnp.sum(exps, axis=-1, keepdims=True)


def head_lanes(width, head):
    lane = lax.broadcasted_iota(jnp.int32, (1, width), 1)
    return (lane >= head * HD) & (lane < (head + 1) * HD)


def attend(images, heads, width, normed, weight, bias, mask_ref):
    projected = (nn(normed, weight) + bias.astype(F32)).astype(BF16)
    parts = []
    for image in range(images):
        rows = projected[image * PAD : (image + 1) * PAD, :]
        queries, key_rows, values = (rows[:, at * width : (at + 1) * width] for at in range(3))
        key_mask = mask_ref[image : image + 1, :]
        mixed = jnp.zeros((PAD, width), F32)
        for head in range(heads):
            lanes = head_lanes(width, head)
            own = jnp.where(lanes, queries, jnp.zeros_like(queries))
            probabilities = softmax_rows(masked_scores(own, key_rows, key_mask))
            mixed = jnp.where(lanes, nn(probabilities.astype(BF16), values), mixed)
        parts.append(mixed.astype(BF16))
    return projected, jnp.concatenate(parts, axis=0)


def first_heads_kernel(
    images, heads, width, chunks, s_ref, x_ref, gain_ref, shift_ref, mask_ref, *refs
):
    weights, outs, wide = refs[: 2 * chunks], refs[2 * chunks : -1], refs[-1]
    stream = load_images(images, x_ref, wide)
    normal, _ = normalize(stream)
    normed = (normal * gain_ref[...].astype(F32) + shift_ref[...].astype(F32)).astype(BF16)
    outs[0][...] = normed
    branch = jnp.zeros((images * PAD, D), F32)
    for chunk in range(chunks):
        weight_ref, out_ref = weights[2 * chunk], weights[2 * chunk + 1]
        projected, attended = attend(
            images, heads, width, normed, weight_ref[:D, :], weight_ref[D : D + 1, :], mask_ref
        )
        outs[2 + 2 * chunk][...] = projected
        outs[3 + 2 * chunk][...] = attended
        branch += nn(attended, out_ref[...])
    outs[1][...] = branch


def last_heads_kernel(
    images,
    heads,
    width,
    chunks,
    s_ref,
    x_ref,
    normed_ref,
    branch_ref,
    out_bias_ref,
    gain_ref,
    shift_ref,
    mask_ref,
    valid_ref,
    *refs,
):
    weights, outs, wide = refs[: 2 * chunks], refs[2 * chunks : -1], refs[-1]
    stream = load_images(images, x_ref, wide)
    normed = normed_ref[...]
    branch = branch_ref[...]
    for chunk in range(chunks):
        weight_ref, out_ref = weights[2 * chunk], weights[2 * chunk + 1]
        projected, attended = attend(
            images, heads, width, normed, weight_ref[:D, :], weight_ref[D : D + 1, :], mask_ref
        )
        outs[3 + 2 * chunk][...] = projected
        outs[4 + 2 * chunk][...] = attended
        branch += nn(attended, out_ref[...])
    branch = branch + out_bias_ref[...].astype(F32)
    middle = stream + branch
    normal, _ = normalize(middle)
    outs[0][...] = (normal * gain_ref[...].astype(F32) + shift_ref[...].astype(F32)).astype(BF16)
    outs[1][...] = middle
    valid = valid_ref[...]
    outs[2][0:1, :] = jnp.sum(middle * middle * valid, axis=0, keepdims=True)
    outs[2][1:2, :] = jnp.sum(branch * branch * valid, axis=0, keepdims=True)
    outs[2][2:8, :] = jnp.zeros((6, D), F32)


def attend_pull(images, heads, width, normed, projected_ref, d_branch, weight, out_weight, mask_ref):
    d_attended = nt(d_branch, out_weight).astype(BF16)
    parts = []
    for image in range(images):
        span = slice(image * PAD, (image + 1) * PAD)
        rows = projected_ref[span, :]
        queries, key_rows, values = (rows[:, at * width : (at + 1) * width] for at in range(3))
        key_mask = mask_ref[image : image + 1, :]
        d_mixed = d_attended[span, :]
        d_queries = jnp.zeros((PAD, width), F32)
        d_keys = jnp.zeros((PAD, width), F32)
        d_values = jnp.zeros((PAD, width), F32)
        for head in range(heads):
            lanes = head_lanes(width, head)
            own = jnp.where(lanes, queries, jnp.zeros_like(queries))
            d_own = jnp.where(lanes, d_mixed, jnp.zeros_like(d_mixed))
            probabilities = softmax_rows(masked_scores(own, key_rows, key_mask))
            d_probs = nt(d_own, values)
            row_dots = jnp.sum(d_probs * probabilities, axis=-1, keepdims=True)
            d_scores = probabilities * (d_probs - row_dots)
            d_scores = jnp.where(key_mask > 0, d_scores, 0.0).astype(BF16)
            d_values += tn(probabilities.astype(BF16), d_own)
            d_queries = jnp.where(lanes, nn(d_scores, key_rows), d_queries)
            d_keys += tn(d_scores, own)
        parts.append(
            jnp.concatenate(
                [d_queries * HD ** (-0.5), d_keys * HD ** (-0.5), d_values], axis=1
            ).astype(BF16)
        )
    d_project = jnp.concatenate(parts, axis=0)
    return d_project, tn(normed, d_project), nt(d_project, weight)


def write_pull(grad_ref, out_grad_ref, bias_ref, normed, projected_ref, attended_ref, d_branch, weight_ref, out_ref, mask_ref, dims):
    images, heads, width = dims
    d_project, grad, d_normed = attend_pull(
        images, heads, width, normed, projected_ref, d_branch, weight_ref[:D, :], out_ref[...], mask_ref
    )
    grad_ref[...] = grad.astype(BF16)
    out_grad_ref[...] = tn(attended_ref[...], d_branch).astype(BF16)
    bias_ref[...] = jnp.broadcast_to(
        jnp.sum(d_project.astype(F32), axis=0, keepdims=True), bias_ref.shape
    )
    return d_normed


def middle_pull_kernel(
    images,
    heads,
    width,
    chunks,
    s_ref,
    cot_ref,
    part_ref,
    got_ref,
    middle_ref,
    gain_ref,
    normed_ref,
    mask_ref,
    *refs,
):
    ins, outs, wide = refs[: 4 * chunks], refs[4 * chunks : -1], refs[-1]
    upstream = load_images(images, cot_ref, wide)
    normal, inv_std = normalize(middle_ref[...])
    d_normed2 = part_ref[...].astype(F32) + got_ref[...].astype(F32)
    d_middle = upstream + norm_pull(d_normed2, normal, inv_std, gain_ref[...].astype(F32))
    d_branch = d_middle.astype(BF16)
    d_low, sums, d_middle_ref, d_branch_ref = outs[0], outs[1], outs[2], outs[3]
    d_middle_ref[...] = d_middle
    d_branch_ref[...] = d_branch
    sums[0:1, :] = jnp.sum(d_normed2 * normal, axis=0, keepdims=True)
    sums[1:2, :] = jnp.sum(d_normed2, axis=0, keepdims=True)
    sums[2:3, :] = jnp.sum(d_branch.astype(F32), axis=0, keepdims=True)
    sums[3:8, :] = jnp.zeros((5, D), F32)
    normed = normed_ref[...]
    d_normed = jnp.zeros((images * PAD, D), F32)
    for chunk in range(chunks):
        weight_ref, out_ref, projected_ref, attended_ref = ins[4 * chunk : 4 * chunk + 4]
        grad_ref, out_grad_ref, bias_ref = outs[4 + 3 * chunk : 7 + 3 * chunk]
        d_normed += write_pull(
            grad_ref, out_grad_ref, bias_ref, normed, projected_ref, attended_ref, d_branch,
            weight_ref, out_ref, mask_ref, (images, heads, width),
        )
    d_low[...] = d_normed


def input_pull_kernel(
    images,
    heads,
    width,
    chunks,
    s_ref,
    x_ref,
    d_normed_ref,
    d_middle_ref,
    d_branch_ref,
    gain_ref,
    normed_ref,
    mask_ref,
    valid_ref,
    *refs,
):
    ins, outs, wide = refs[: 4 * chunks], refs[4 * chunks : -1], refs[-1]
    d_inputs_ref, sums = outs[0], outs[1]
    normed = normed_ref[...]
    d_branch = d_branch_ref[...]
    d_normed = d_normed_ref[...]
    for chunk in range(chunks):
        weight_ref, out_ref, projected_ref, attended_ref = ins[4 * chunk : 4 * chunk + 4]
        grad_ref, out_grad_ref, bias_ref = outs[2 + 3 * chunk : 5 + 3 * chunk]
        d_normed += write_pull(
            grad_ref, out_grad_ref, bias_ref, normed, projected_ref, attended_ref, d_branch,
            weight_ref, out_ref, mask_ref, (images, heads, width),
        )
    normal, inv_std = normalize(load_images(images, x_ref, wide))
    d_inputs = d_middle_ref[...] + norm_pull(d_normed, normal, inv_std, gain_ref[...].astype(F32))
    d_inputs_ref[...] = d_inputs.astype(BF16)
    sums[0:1, :] = jnp.sum(d_normed * normal, axis=0, keepdims=True)
    sums[1:2, :] = jnp.sum(d_normed, axis=0, keepdims=True)
    sums[2:3, :] = jnp.sum(d_inputs * d_inputs * valid_ref[...], axis=0, keepdims=True)
    sums[3:8, :] = jnp.zeros((5, D), F32)


def expert_kernel(chunks, pieces, hidden_width, s_ref, back_bias_ref, router_ref, *refs):
    at = 0

    def take(count):
        nonlocal at
        at += count
        return refs[at - count : at]

    rows_in, ups_in = take(chunks), take(chunks)
    in_weights, in_biases, back_weights = take(pieces), take(pieces), take(pieces)
    d_rows_out, mixed_out = take(chunks), take(chunks)
    in_grads, back_grads = take(pieces), take(pieces)
    bias_grads, back_bias_grad, router_grad, squares = take(4)
    rows_wide, ups_wide, in_weight, back_weight, in_bias, results, d_rows = take(7)
    expert, first = s_ref[1], s_ref[2]
    height = chunks * CAP
    for chunk in range(chunks):
        span = slice(chunk * CAP, (chunk + 1) * CAP)
        rows_wide[span, :] = rows_in[chunk][...].astype(F32)
        ups_wide[span, :] = ups_in[chunk][...].astype(F32)
    rows = rows_wide[...].astype(BF16)
    other = ups_wide[:, D : D + 1]
    logits = nn(rows, router_ref[...])
    label = lax.broadcasted_iota(jnp.int32, (1, EXPERTS), 1)
    mine = label == expert
    others = label.astype(F32) == other
    own_logit = jnp.sum(jnp.where(mine, logits, 0.0), axis=1, keepdims=True)
    other_logit = jnp.sum(jnp.where(others, logits, 0.0), axis=1, keepdims=True)
    peak = jnp.maximum(own_logit, other_logit)
    own_exp, other_exp = jnp.exp(own_logit - peak), jnp.exp(other_logit - peak)
    gate = own_exp / (own_exp + other_exp)
    other_gate = other_exp / (own_exp + other_exp)
    d_results_wide = (gate * ups_wide[:, :D]).astype(BF16)
    results[...] = jnp.zeros_like(results)
    d_rows[...] = jnp.zeros_like(d_rows)
    squares[...] = jnp.zeros_like(squares)

    def piece_step(piece, carry):
        for k in range(pieces):
            @pl.when(piece == k)
            def _():
                in_weight[...] = in_weights[k][...]
                back_weight[...] = back_weights[k][...]
                in_bias[...] = in_biases[k][...].astype(F32)

        pre_act = nn(rows, in_weight[...]) + in_bias[0:1, :]
        cdf = 0.5 * (1.0 + lax.erf(pre_act * (0.5**0.5)))
        hidden = (pre_act * cdf).astype(BF16)
        results[...] += nn(hidden, back_weight[...])
        slope = cdf + pre_act * jnp.exp(-0.5 * pre_act * pre_act) * 0.3989422804014327
        d_pre = (slope * nt(d_results_wide, back_weight[...])).astype(BF16)
        d_rows[...] += nt(d_pre, in_weight[...])
        in_grad = tn(rows, d_pre)
        back_grad = tn(hidden, d_results_wide)
        bias_grad = jnp.sum(d_pre.astype(F32), axis=0, keepdims=True)
        squares[0:1, :] += jnp.sum(in_grad * in_grad)
        squares[1:2, :] += jnp.sum(back_grad * back_grad)
        squares[2:3, :] += jnp.sum(bias_grad * bias_grad)
        for k in range(pieces):
            @pl.when(piece == k)
            def _():
                in_grads[k][...] = in_grad.astype(BF16)
                back_grads[k][...] = back_grad.astype(BF16)
                bias_grads[k : k + 1, :] = bias_grad

        return carry

    lax.fori_loop(0, pieces, piece_step, 0)
    total = results[...] + jnp.where(first > 0, 1.0, 0.0) * back_bias_ref[pl.ds(expert, 1), :]
    d_gate = jnp.sum(ups_wide[:, :D] * total, axis=1, keepdims=True)
    moved = gate * other_gate * d_gate
    d_logits = jnp.where(mine, moved, jnp.where(others, -moved, 0.0)).astype(BF16)
    router_grad[...] = tn(d_logits, rows)
    back_bias_grad[...] = jnp.broadcast_to(
        jnp.sum(d_results_wide.astype(F32), axis=0, keepdims=True), back_bias_grad.shape
    )
    rows_wide[...] = d_rows[...] + nt(d_logits, router_ref[...])
    results[...] = gate * total
    for chunk in range(chunks):
        span = slice(chunk * CAP, (chunk + 1) * CAP)
        d_rows_out[chunk][...] = rows_wide[span, :].astype(BF16)
        mixed_out[chunk][...] = results[span, :].astype(BF16)


def output_kernel(images, s_ref, middle_ref, part_ref, got_ref, valid_ref, out_ref, sums):
    mixture = part_ref[...].astype(F32) + got_ref[...].astype(F32)
    output = middle_ref[...] + mixture
    out_ref[...] = output.astype(BF16)
    valid = valid_ref[...]
    sums[0:1, :] = jnp.sum(mixture * mixture * valid, axis=0, keepdims=True)
    sums[1:2, :] = jnp.sum(output * output * valid, axis=0, keepdims=True)
    sums[2:8, :] = jnp.zeros((6, D), F32)


def place_tokens_kernel(groups, images, s_ref, *refs):
    out = refs[groups]
    for group in range(groups):
        @pl.when(pl.program_id(0) == group)
        def _():
            for image in range(images):
                rows = refs[group][image * PAD : (image + 1) * PAD, :].astype(F32)
                out[image] = rows[:SEQ]


def place_experts_kernel(groups, s_ref, *refs):
    outs = refs[2 * groups :]
    for group in range(groups):
        @pl.when(pl.program_id(0) == group)
        def _():
            outs[0][0] = refs[group][...].astype(F32)
            outs[1][0] = refs[groups + group][...].astype(F32)


def place_tokens(scalars, pieces, count, images):
    groups = len(pieces)
    spec = pl.BlockSpec((images, SEQ, D), lambda step, s: (jnp.bitwise_xor(s[0], step), 0, 0))
    return run(
        functools.partial(place_tokens_kernel, groups, images),
        scalars, pieces, [((count, SEQ, D), F32)], grid=(groups,), out_specs={0: spec},
    )[0]


def shards(
    inputs, valid_mask, expert_ids, slot_ids, norm1_gain, norm1_bias, w_qkv, b_qv, w_out, b_out,
    norm2_gain, norm2_bias, w_router, w_in, b_in, w_back, b_back, cotangent, dp_size, tensor_size,
):
    count = inputs.shape[0]
    groups = tensor_size
    images = count // groups
    local_width = w_qkv.shape[2]
    heads = local_width // HD
    width = -(-local_width // LANES) * LANES
    local_experts, _, hidden_width = w_in.shape
    shared = local_experts == groups
    pieces = groups if shared else 1
    chunks = dp_size
    rows = chunks * CAP
    own_tokens = images * PAD
    data_at = lax.axis_index("dp").astype(jnp.int32)
    head_at = lax.axis_index("tensor").astype(jnp.int32)
    lane_expert = head_at if shared else jnp.int32(0)
    expert_at = data_at * local_experts + lane_expert
    first = (head_at == 0).astype(jnp.int32)
    scalars = jnp.stack([head_at, expert_at, jnp.int32(1) if shared else first])

    pad_cols = [(0, 0), (0, 0), (0, width - local_width)]
    packed = jnp.pad(w_qkv, pad_cols).reshape(D, 3 * width)
    bias_rows = jnp.concatenate([b_qv[0:1], jnp.zeros_like(b_qv[0:1]), b_qv[1:2]], axis=0)
    bias_row = jnp.pad(bias_rows, [(0, 0), (0, width - local_width)]).reshape(1, 3 * width)
    packed = jnp.concatenate([packed, jnp.broadcast_to(bias_row, (16, 3 * width))], axis=0)
    out_rows = jnp.pad(w_out, [(0, width - local_width), (0, 0)])

    def gather(value):
        parts = [None] * groups
        parts[0] = value
        for r in range(2, groups, 2):
            parts[r] = swap(value, "tensor", groups, r)
        for r in range(1, groups, 2):
            parts[r] = swap(parts[r - 1], "tensor", groups, 1)
        return parts

    qkv_parts = gather(packed)
    out_parts = gather(out_rows)

    kept = slot_ids < CAP
    flat = jnp.where(kept, expert_ids * CAP + slot_ids, -1)
    flat = jnp.pad(flat, [(0, 0), (0, PAD - SEQ), (0, 0)], constant_values=-1)
    flat_rows = jnp.transpose(flat, (0, 2, 1))
    other_rows = jnp.pad(
        jnp.transpose(expert_ids[:, :, ::-1], (0, 2, 1)).astype(F32),
        [(0, 0), (0, 0), (0, PAD - SEQ)],
    )
    partners = jnp.bitwise_xor(data_at, jnp.arange(chunks, dtype=jnp.int32))
    starts = (partners * local_experts + lane_expert) * CAP
    target = (starts[:, None] + jnp.arange(CAP, dtype=jnp.int32)[None, :]).reshape(rows)
    target_column = target[:, None]
    target_row = target[None, :]
    own_mask = lax.dynamic_slice(valid_mask, (head_at * images, 0), (images, SEQ))
    key_mask = jnp.pad(own_mask, [(0, 0), (0, PAD - SEQ)], constant_values=-1)
    valid = jnp.maximum(key_mask, 0).astype(F32).reshape(own_tokens, 1)

    up_sent = run(
        functools.partial(send_cotangent_kernel, count, chunks),
        scalars, [flat_rows, other_rows, target_column, cotangent],
        [((CAP, D + LANES), BF16)] * chunks, flops=2 * rows * count * SEQ * D,
    )
    ups = [up_sent[0]] + [swap(up_sent[r], "dp", chunks, r) for r in range(1, chunks)]

    def pieces_of(weight):
        if not shared:
            return [weight[0]]
        parts = [lax.dynamic_index_in_dim(weight, head_at, 0, keepdims=False)]
        for r in range(1, groups):
            piece = lax.dynamic_index_in_dim(weight, jnp.bitwise_xor(head_at, r), 0, keepdims=False)
            parts.append(swap(piece, "tensor", groups, r))
        return parts

    in_weights = pieces_of(w_in)
    back_weights = pieces_of(w_back)
    in_biases = pieces_of(jnp.broadcast_to(b_in[:, None, :], (local_experts, 8, hidden_width)))

    row = lambda v: v.reshape(1, D)
    half = groups // 2
    own_spec = pl.BlockSpec((images, SEQ, D), lambda step, s: (s[0], 0, 0))
    heads_out = [((own_tokens, 3 * width), BF16), ((own_tokens, width), BF16)]
    heads_flops = half * own_tokens * (2 * D * 4 * width + 4 * PAD * width * heads)
    wide = pltpu.VMEM((own_tokens, D), F32)
    near = [w for r in range(half) for w in (qkv_parts[r], out_parts[r])]
    got = run(
        functools.partial(first_heads_kernel, images, heads, width, half),
        scalars, [inputs, row(norm1_gain), row(norm1_bias), key_mask, *near],
        [((own_tokens, D), BF16), ((own_tokens, D), F32)] + heads_out * half,
        scratch=[wide], own={0: own_spec}, flops=heads_flops,
    )
    normed1, branch_part = got[:2]
    kept_heads = list(got[2:])
    far = [w for r in range(half, groups) for w in (qkv_parts[r], out_parts[r])]
    got = run(
        functools.partial(last_heads_kernel, images, heads, width, groups - half),
        scalars,
        [inputs, normed1, branch_part, row(b_out), row(norm2_gain), row(norm2_bias), key_mask,
         valid, *far],
        [((own_tokens, D), BF16), ((own_tokens, D), F32), ((8, D), F32)]
        + heads_out * (groups - half),
        scratch=[wide], own={0: own_spec}, flops=heads_flops,
    )
    normed2, middle, forward_sums = got[:3]
    kept_heads += list(got[3:])

    token_parts = gather(normed2)
    sent = run(
        functools.partial(dispatch_kernel, groups, images, chunks),
        scalars, [flat_rows, target_column, *token_parts],
        [((CAP, D), BF16)] * chunks, flops=2 * rows * count * PAD * D,
    )
    dispatched = [sent[0]] + [swap(sent[r], "dp", chunks, r) for r in range(1, chunks)]
    got = run(
        functools.partial(expert_kernel, chunks, pieces, hidden_width),
        scalars,
        [b_back.astype(F32), w_router, *dispatched, *ups, *in_weights, *in_biases, *back_weights],
        [((CAP, D), BF16)] * (2 * chunks)
        + [((D, hidden_width), BF16)] * pieces
        + [((hidden_width, D), BF16)] * pieces
        + [((8, hidden_width), F32), ((8, D), F32), ((EXPERTS, D), F32), ((8, LANES), F32)],
        scratch=[
            pltpu.VMEM((rows, D), F32),
            pltpu.VMEM((rows, D + LANES), F32),
            pltpu.VMEM((D, hidden_width), BF16),
            pltpu.VMEM((hidden_width, D), BF16),
            pltpu.VMEM((8, hidden_width), F32),
            pltpu.VMEM((rows, D), F32),
            pltpu.VMEM((rows, D), F32),
        ],
        flops=12 * rows * D * hidden_width * pieces,
    )
    d_sent, mixed_sent = got[:chunks], got[chunks : 2 * chunks]
    in_grads = got[2 * chunks : 2 * chunks + pieces]
    back_grads = got[2 * chunks + pieces : 2 * chunks + 2 * pieces]
    in_bias_grads, back_bias_grad, router_grad, expert_squares = got[2 * chunks + 2 * pieces :]

    def combine(parts):
        return run(
            functools.partial(combine_kernel, groups, images, chunks),
            scalars, [flat, target_row, *parts],
            [((own_tokens, D), BF16)] * groups,
            scratch=[pltpu.VMEM((rows, D), F32)], flops=2 * rows * count * PAD * D,
        )

    def reduce_own(parts):
        near_sums = []
        for r in range(0, groups, 2):
            came = swap(parts[r + 1], "tensor", groups, 1)
            near_sums.append(parts[r].astype(F32) + came.astype(F32))
        total = near_sums[0]
        for r in range(2, groups - 2, 2):
            total = total + swap(near_sums[r // 2].astype(BF16), "tensor", groups, r).astype(F32)
        last = groups - 2
        return total, swap(near_sums[last // 2].astype(BF16), "tensor", groups, last)

    d_back = [d_sent[0]] + [swap(d_sent[r], "dp", chunks, r) for r in range(1, chunks)]
    d_total, d_came = reduce_own(combine(d_back))

    def head_ins(r_range):
        return [
            a
            for r in r_range
            for a in (qkv_parts[r], out_parts[r], kept_heads[2 * r], kept_heads[2 * r + 1])
        ]

    grads_out = [((D, 3 * width), BF16), ((width, D), BF16), ((8, 3 * width), F32)]
    got = run(
        functools.partial(middle_pull_kernel, images, heads, width, groups - half),
        scalars,
        [cotangent, d_total, d_came, middle, row(norm2_gain), normed1, key_mask,
         *head_ins(range(half, groups))],
        [((own_tokens, D), F32), ((8, D), F32), ((own_tokens, D), F32), ((own_tokens, D), BF16)]
        + grads_out * (groups - half),
        scratch=[wide], own={0: own_spec}, flops=3 * heads_flops,
    )
    d_low, norm2_sums, d_middle, d_branch = got[:4]
    far_grads = got[4:]
    got = run(
        functools.partial(input_pull_kernel, images, heads, width, half),
        scalars,
        [inputs, d_low, d_middle, d_branch, row(norm1_gain), normed1, key_mask, valid,
         *head_ins(range(half))],
        [((own_tokens, D), BF16), ((8, D), F32)] + grads_out * half,
        scratch=[wide], own={0: own_spec}, flops=3 * heads_flops,
    )
    d_own, norm1_sums = got[:2]
    head_grads = list(got[2:]) + list(far_grads)

    mixed = [mixed_sent[0]] + [swap(mixed_sent[r], "dp", chunks, r) for r in range(1, chunks)]
    mix_total, mix_came = reduce_own(combine(mixed))
    output_low, output_sums = run(
        functools.partial(output_kernel, images),
        scalars, [middle, mix_total, mix_came, valid],
        [((own_tokens, D), BF16), ((8, D), F32)],
    )
    output = place_tokens(scalars, gather(output_low), count, images)
    d_inputs = place_tokens(scalars, gather(d_own), count, images)

    if shared:

        def send_back(parts):
            return [parts[0]] + [swap(parts[r], "tensor", groups, r) for r in range(1, groups)]

        spec = lambda a, b: pl.BlockSpec(
            (1, a, b), lambda step, s: (jnp.bitwise_xor(s[0], step), 0, 0)
        )
        g_w_in, g_w_back = run(
            functools.partial(place_experts_kernel, groups),
            scalars, [*send_back(in_grads), *send_back(back_grads)],
            [((local_experts, D, hidden_width), F32), ((local_experts, hidden_width, D), F32)],
            grid=(groups,), out_specs={0: spec(D, hidden_width), 1: spec(hidden_width, D)},
        )
        bias_parts = jnp.stack(send_back([in_bias_grads[r] for r in range(groups)]))
        order = jnp.bitwise_xor(head_at, jnp.arange(groups, dtype=jnp.int32))
        g_b_in = jnp.take(bias_parts, order, axis=0)
    else:
        g_w_in = in_grads[0][None].astype(F32)
        g_w_back = back_grads[0][None].astype(F32)
        g_b_in = in_bias_grads[0:1]

    def reduce_heads(parts):
        total, came = reduce_own(parts)
        return total + came.astype(F32)

    g_qkv_own = reduce_heads(head_grads[0::3])
    g_out_own = reduce_heads(head_grads[1::3])
    dense = jnp.concatenate([g_qkv_own.reshape(-1, D), g_out_own], axis=0)
    share = dense.shape[0] // chunks
    dense = dense.astype(BF16).reshape(chunks, share, D)

    def dense_piece(r):
        at = jnp.bitwise_xor(data_at, r)
        return lax.dynamic_index_in_dim(dense, at, 0, keepdims=False)

    piece = dense_piece(0).astype(F32)
    for r in range(1, chunks):
        piece = piece + swap(dense_piece(r), "dp", chunks, r).astype(F32)
    piece = piece.astype(BF16)
    summed = [piece] + [swap(piece, "dp", chunks, r) for r in range(1, chunks)]
    summed = jnp.take(jnp.stack(summed), partners, axis=0).astype(F32).reshape(-1, D)
    qkv_rows = D * 3 * width // D
    g_w_qkv = summed[:qkv_rows].reshape(D, 3, width)[:, :, :local_width]
    g_w_out = summed[qkv_rows:][:local_width]

    order = jnp.bitwise_xor(head_at, jnp.arange(groups, dtype=jnp.int32))
    bias_rel = jnp.stack([p[0] for p in head_grads[2::3]]).reshape(groups, 3, width)
    bias_all = jnp.take(bias_rel, order, axis=0)[:, :, :local_width]
    bias_q = bias_all[:, 0].reshape(1, D)
    bias_v = bias_all[:, 2].reshape(1, D)
    once = jnp.float32(1.0) if shared else first.astype(F32)
    own_row = (jnp.arange(EXPERTS, dtype=jnp.int32) == expert_at).astype(F32)[:, None]
    g_b_back_part = own_row * back_bias_grad[0:1] * once
    scalar_terms = jnp.stack(
        [
            jnp.sum(forward_sums[0]), jnp.sum(forward_sums[1]), jnp.sum(output_sums[0]),
            jnp.sum(output_sums[1]), jnp.sum(norm1_sums[2]), jnp.sum(valid),
            expert_squares[0, 0], expert_squares[2, 0], expert_squares[1, 0],
        ]
    )
    early = lax.psum(jnp.concatenate([g_b_back_part, router_grad], axis=0), ("dp", "tensor"))
    late = jnp.concatenate(
        [norm1_sums[0:2], norm2_sums[0:3], bias_q, bias_v,
         jnp.pad(scalar_terms, (0, D - 9))[None]], axis=0,
    )
    for axis, size in (("tensor", groups), ("dp", chunks)):
        by = 1
        while by < size:
            late = late + swap(late, axis, size, by)
            by *= 2
    g_b_back = early[:EXPERTS]
    g_w_router = jnp.transpose(early[EXPERTS:])
    g_b_qv = lax.dynamic_slice(late[5:7], (0, head_at * local_width), (2, local_width))
    head_squares = jnp.stack([jnp.sum(g_w_qkv * g_w_qkv), jnp.sum(g_w_out * g_w_out)])
    by = 1
    while by < groups:
        head_squares = head_squares + swap(head_squares, "tensor", groups, by)
        by *= 2
    square = lambda v: jnp.sum(v * v)
    totals = late[7]
    squares = jnp.stack(
        [
            square(late[0]), square(late[1]), head_squares[0], square(late[5:7]), head_squares[1],
            square(late[4]), square(late[2]), square(late[3]), square(g_w_router),
            totals[6], totals[7], totals[8], square(g_b_back),
        ]
    )
    return (
        output, d_inputs, late[0], late[1], g_w_qkv, g_b_qv, g_w_out, late[4], late[2], late[3],
        g_w_router, g_w_in, g_b_in, g_w_back, g_b_back, jnp.sqrt(squares),
        jnp.sqrt(totals[:5] / (totals[5] * D)),
    )


def solution(mesh):
    placed = (
        P("dp", None, None),
        P("dp", None),
        P("dp", None, None),
        P("dp", None, None),
        P(),
        P(),
        P(None, None, "tensor"),
        P(None, "tensor"),
        P("tensor", None),
        P(),
        P(),
        P(),
        P(),
        P("dp", None, "tensor"),
        P("dp", "tensor"),
        P("dp", "tensor", None),
        P(),
        P("dp", None, None),
    )
    return jax.shard_map(
        functools.partial(shards, dp_size=mesh.shape["dp"], tensor_size=mesh.shape["tensor"]),
        mesh=mesh,
        in_specs=placed,
        out_specs=(
            P("dp", None, None),
            P("dp", None, None),
            P(),
            P(),
            P(None, None, "tensor"),
            P(None, "tensor"),
            P("tensor", None),
            P(),
            P(),
            P(),
            P(),
            P("dp", None, "tensor"),
            P("dp", "tensor"),
            P("dp", "tensor", None),
            P(),
            P(),
            P(),
        ),
        check_vma=False,
    )
```

```python
import functools

import jax
import jax.numpy as jnp
from jax import lax
from jax.experimental import pallas as pl
from jax.experimental.pallas import tpu as pltpu
from jax.sharding import PartitionSpec as P

D = 512
HD = 64
EXPERTS = 32
SEQ = 197
CAP = 104
PAD = 208
WIDE = 256
MIB_EXPERT = 58
MIB_GRADS = 58
MIB_PULL = 58
LANES = 128
F32 = jnp.float32
BF16 = jnp.bfloat16


def nn(a, b):
    return lax.dot_general(a, b, (((1,), (0,)), ((), ())), preferred_element_type=F32)


def nt(a, b):
    return lax.dot_general(a, b, (((1,), (1,)), ((), ())), preferred_element_type=F32)


def tn(a, b):
    return lax.dot_general(a, b, (((0,), (0,)), ((), ())), preferred_element_type=F32)


def swap(value, axis, size, by):
    return lax.ppermute(value, axis, [(at, at ^ by) for at in range(size)])


def after(value, *others):
    return lax.optimization_barrier((value, *others))[0]


def run(kernel, scalars, ins, outs, scratch=(), grid=(1,), out_specs=None, mib=28, left=(), kept=()):
    out_specs = out_specs or {}

    def whole(shape, stays):
        if stays:
            return pl.BlockSpec(memory_space=pl.ANY)
        return pl.BlockSpec(shape, lambda step, s, nd=len(shape): (0,) * nd)

    return pl.pallas_call(
        kernel,
        grid_spec=pltpu.PrefetchScalarGridSpec(
            num_scalar_prefetch=1,
            grid=grid,
            in_specs=[whole(a.shape, i in left) for i, a in enumerate(ins)],
            out_specs=[
                out_specs[i] if i in out_specs else whole(o[0], i in kept)
                for i, o in enumerate(outs)
            ],
            scratch_shapes=list(scratch),
        ),
        out_shape=[jax.ShapeDtypeStruct(shape, dtype) for shape, dtype in outs],
        compiler_params=pltpu.CompilerParams(vmem_limit_bytes=mib * 2**20),
        cost_estimate=pl.CostEstimate(flops=0, bytes_accessed=0, transcendentals=0),
    )(scalars, *ins)


def route_rows(ids_ref, slots_ref, image):
    ids, slots = ids_ref[image], slots_ref[image]
    return jnp.where(slots < CAP, ids * CAP + slots, -1)


def block_start(s_ref, chunk):
    return (chunk * s_ref[4] + s_ref[5]) * CAP


def target_column(s_ref, chunks):
    rows = lax.broadcasted_iota(jnp.int32, (CAP, 1), 0)
    starts = [block_start(s_ref, chunk) for chunk in range(chunks)]
    return jnp.concatenate([rows + start for start in starts], axis=0)


def target_row(s_ref, chunks):
    lanes = lax.broadcasted_iota(jnp.int32, (1, chunks * CAP), 1)
    target = lanes
    for chunk in range(chunks):
        here = (lanes >= chunk * CAP) & (lanes < (chunk + 1) * CAP)
        target = jnp.where(here, lanes + (block_start(s_ref, chunk) - chunk * CAP), target)
    return target


def spread(source_ref, wide_ref, count):
    for k in range(D // LANES):
        wide_ref[k] = source_ref[:, k * LANES : (k + 1) * LANES].astype(F32)

    def image_rows(image):
        return jnp.concatenate(
            [wide_ref[k, pl.ds(image, SEQ, stride=count), :] for k in range(D // LANES)], axis=1
        )

    return image_rows


def own_rows(images, me, image_rows, out_ref, padded):
    padded[...] = jnp.zeros_like(padded)
    for image in range(images):
        padded[image * PAD : image * PAD + SEQ, :] = image_rows(me * images + image)
    out_ref[...] = padded[...].astype(BF16)


def pack_kernel(width, s_ref, qkv_ref, out_ref, bias_ref, in_bias_ref, pack):
    pack[0 : 3 * D, :] = qkv_ref[...]
    for block in range(D // width):
        at = 3 * D + block * width
        pack[at : at + width, :] = out_ref[:, block * width : (block + 1) * width]
    bias = bias_ref[...].astype(F32)
    experts, hidden = in_bias_ref.shape
    lines = in_bias_ref[...].astype(F32)
    lines = [
        lines[e : e + 1, k * width : (k + 1) * width]
        for e in range(experts)
        for k in range(hidden // width)
    ]
    fill = -len(lines) % 16
    if fill:
        lines.append(jnp.zeros((fill, width), F32))
    pack[4 * D :, :] = jnp.concatenate(
        [bias[0:1], bias[1:2], jnp.zeros((14, width), F32), *lines], axis=0
    ).astype(BF16)


def start_kernel(dims, s_ref, ids_ref, slots_ref, cot_ref, *refs):
    count, images, chunks, shared = dims
    if shared:
        w_in, w_back, own, *sends = refs[:7]
        outs = refs[7:-4]
    else:
        own, outs = refs[0], refs[1:-4]
    wide, padded, blocks, sems = refs[-4:]
    pairs = []
    if shared:
        hidden = w_back.shape[1]
        for r, block in enumerate(sends):
            expert = jnp.bitwise_xor(s_ref[0], r)
            pairs.append((w_in.at[expert], block.at[pl.ds(0, D)]))
            pairs.append((w_back.at[expert], block.at[pl.ds(D, hidden)]))
    copies = [
        pltpu.make_async_copy(source, target, sems.at[index])
        for index, (source, target) in enumerate(pairs)
    ]
    for copy in copies:
        copy.start()
    image_rows = spread(cot_ref, wide, count)
    target = target_column(s_ref, chunks)
    rows = chunks * CAP
    total = jnp.zeros((rows, D), F32)
    others = jnp.zeros((rows, SEQ), F32)
    for image in range(count):
        flat = route_rows(ids_ref, slots_ref, image)
        ids = ids_ref[image].astype(F32)
        first = target == flat[0:1, :]
        second = target == flat[1:2, :]
        hit = (first | second).astype(F32).astype(BF16)
        total += nn(hit, image_rows(image).astype(BF16))
        others += jnp.where(first, ids[1:2, :], 0.0) + jnp.where(second, ids[0:1, :], 0.0)
    marks = jnp.broadcast_to(jnp.sum(others, axis=1, keepdims=True), (rows, LANES))
    blocks[:, :D] = total
    blocks[:, D:] = marks
    for chunk in range(chunks):
        at = pl.multiple_of(jnp.bitwise_xor(s_ref[3], chunk) * CAP, 8)
        outs[chunk][...] = blocks[pl.ds(at, CAP), :].astype(BF16)
    own_rows(images, s_ref[0], image_rows, own, padded)
    for copy in copies:
        copy.wait()


def padded_routes(ids_ref, slots_ref, image, flat_ref):
    flat_ref[...] = jnp.full(flat_ref.shape, -1, jnp.int32)
    flat_ref[0:2, 0:SEQ] = route_rows(ids_ref, slots_ref, image)
    return flat_ref[...]


def dispatch_kernel(groups, images, chunks, s_ref, ids_ref, slots_ref, *refs):
    tokens, (out, flat_ref) = refs[:groups], refs[groups:]
    me = s_ref[0]
    target = target_column(s_ref, chunks)
    total = jnp.zeros((chunks * CAP, D), F32)
    for group in range(groups):
        for image in range(images):
            at = jnp.bitwise_xor(me, group) * images + image
            flat = padded_routes(ids_ref, slots_ref, at, flat_ref)[:, :PAD]
            hit = (target == flat[0:1, :]) | (target == flat[1:2, :])
            total += nn(
                hit.astype(F32).astype(BF16), tokens[group][image * PAD : (image + 1) * PAD, :]
            )
    out[...] = total.astype(BF16)


def combine_kernel(groups, images, chunks, s_ref, ids_ref, slots_ref, rows_ref, *refs):
    outs, flat_ref = refs[:2], refs[2]
    me = s_ref[0]
    rows = rows_ref[...]
    target = target_row(s_ref, chunks)
    for group in range(groups):
        for image in range(images):
            at = jnp.bitwise_xor(me, group) * images + image
            flat = jnp.transpose(padded_routes(ids_ref, slots_ref, at, flat_ref))[:PAD, :]
            hit = (flat[:, 0:1] == target) | (flat[:, 1:2] == target)
            place = (group // 2 * images + image) * PAD
            outs[group % 2][place : place + PAD, :] = nn(
                hit.astype(F32).astype(BF16), rows
            ).astype(BF16)


def chunk_weights(packs, width):
    qkv = [p[part * D : (part + 1) * D, :] for p in packs for part in range(3)]
    biases = []
    for p in packs:
        lines = p[3 * D + D : 3 * D + D + 16, :].astype(F32)
        biases += [lines[0:1], jnp.zeros((1, width), F32), lines[1:2]]
    outs = [
        jnp.concatenate(
            [p[3 * D + b * width : 3 * D + (b + 1) * width, :] for b in range(D // width)], axis=1
        )
        for p in packs
    ]
    return (
        jnp.concatenate(qkv, axis=1),
        jnp.concatenate(biases, axis=1),
        jnp.concatenate(outs, axis=0),
    )


def normalize(values):
    average = jnp.mean(values, axis=-1, keepdims=True)
    centered = values - average
    inv_std = lax.rsqrt(jnp.mean(centered * centered, axis=-1, keepdims=True) + 1e-06)
    return centered * inv_std, inv_std


def norm_pull(upstream, normal, inv_std, gain):
    scaled = upstream * gain
    inner = jnp.mean(scaled * normal, axis=-1, keepdims=True)
    return inv_std * (scaled - jnp.mean(scaled, axis=-1, keepdims=True) - normal * inner)


def key_masks(images, me, mask_ref, pad_ref):
    pad_ref[...] = jnp.full(pad_ref.shape, -1, jnp.int32)
    for image in range(images):
        pad_ref[image : image + 1, 0:SEQ] = mask_ref[pl.ds(me * images + image, 1), :]
    return pad_ref[...]


def valid_column(images, masks):
    columns = jnp.transpose(jnp.maximum(masks, 0).astype(F32))
    return jnp.concatenate([columns[:PAD, i : i + 1] for i in range(images)], axis=0)


def masked_scores(queries, key_rows, key_mask):
    scores = nt(queries, key_rows) * HD ** (-0.5)
    return jnp.where(key_mask > 0, scores, jnp.where(key_mask < 0, -2e30, -1e30))


def softmax_rows(scores):
    exps = jnp.exp(scores - jnp.max(scores, axis=-1, keepdims=True))
    return exps / jnp.sum(exps, axis=-1, keepdims=True)


def head_lanes(width, head):
    lane = lax.broadcasted_iota(jnp.int32, (1, width), 1)
    return (lane >= head * HD) & (lane < (head + 1) * HD)


def attend(images, heads, width, chunks, normed, weight, bias, masks):
    projected = (nn(normed, weight) + bias).astype(BF16)
    parts = []
    for image in range(images):
        key_mask = masks[image : image + 1, :PAD]
        line = []
        for chunk in range(chunks):
            queries, key_rows, values = (
                projected[
                    image * PAD : (image + 1) * PAD,
                    (3 * chunk + part) * width : (3 * chunk + part + 1) * width,
                ]
                for part in range(3)
            )
            mixed = jnp.zeros((PAD, width), F32)
            for head in range(heads):
                lanes = head_lanes(width, head)
                own = jnp.where(lanes, queries, jnp.zeros_like(queries))
                probabilities = softmax_rows(masked_scores(own, key_rows, key_mask))
                mixed = jnp.where(lanes, nn(probabilities.astype(BF16), values), mixed)
            line.append(mixed.astype(BF16))
        parts.append(jnp.concatenate(line, axis=1))
    return projected, jnp.concatenate(parts, axis=0)


def first_heads_kernel(
    count, images, heads, width, chunks, s_ref, x_ref, norms_ref, mask_ref, *refs
):
    packs, outs = refs[:chunks], refs[chunks : chunks + 5]
    wide, padded, mask_pad = refs[-3:]
    x_own, normed_ref, branch_ref, projected_ref, attended_ref = outs
    own_rows(images, s_ref[0], spread(x_ref, wide, count), x_own, padded)
    normal, _ = normalize(padded[...])
    normed = (normal * norms_ref[0:1, :] + norms_ref[1:2, :]).astype(BF16)
    normed_ref[...] = normed
    masks = key_masks(images, s_ref[0], mask_ref, mask_pad)
    weight, bias, out_weight = chunk_weights(packs, width)
    projected, attended = attend(images, heads, width, chunks, normed, weight, bias, masks)
    projected_ref[...] = projected
    attended_ref[...] = attended
    branch_ref[...] = nn(attended, out_weight)


def last_heads_kernel(
    images, heads, width, chunks, s_ref, x_ref, normed_ref, branch_ref, norms_ref, mask_ref, *refs
):
    packs, outs, mask_pad = refs[:chunks], refs[chunks : chunks + 5], refs[-1]
    normed2_ref, middle_ref, sums, projected_ref, attended_ref = outs
    masks = key_masks(images, s_ref[0], mask_ref, mask_pad)
    weight, bias, out_weight = chunk_weights(packs, width)
    projected, attended = attend(
        images, heads, width, chunks, normed_ref[...], weight, bias, masks
    )
    projected_ref[...] = projected
    attended_ref[...] = attended
    branch = branch_ref[...] + nn(attended, out_weight) + norms_ref[4:5, :]
    middle = x_ref[...].astype(F32) + branch
    normal, _ = normalize(middle)
    normed2_ref[...] = (normal * norms_ref[2:3, :] + norms_ref[3:4, :]).astype(BF16)
    middle_ref[...] = middle
    valid = valid_column(images, masks)
    sums[...] = jnp.concatenate(
        [
            jnp.sum(middle * middle * valid, axis=0, keepdims=True),
            jnp.sum(branch * branch * valid, axis=0, keepdims=True),
            jnp.broadcast_to(jnp.sum(valid, axis=0, keepdims=True), (1, D)),
            jnp.zeros((5, D), F32),
        ],
        axis=0,
    )


def as_lines(rows):
    return jnp.concatenate([rows[:, k * LANES : (k + 1) * LANES] for k in range(D // LANES)], axis=0)


def as_rows(lines):
    count = lines.shape[0] // (D // LANES)
    return jnp.concatenate(
        [lines[k * count : (k + 1) * count] for k in range(D // LANES)], axis=1
    )


def attend_pull(images, heads, width, chunks, projected_ref, d_attended, masks):
    parts = []
    for image in range(images):
        span = slice(image * PAD, (image + 1) * PAD)
        key_mask = masks[image : image + 1, :PAD]
        line = []
        for chunk in range(chunks):
            queries, key_rows, values = (
                projected_ref[span, (3 * chunk + part) * width : (3 * chunk + part + 1) * width]
                for part in range(3)
            )
            d_mixed = d_attended[span, chunk * width : (chunk + 1) * width]
            d_queries = jnp.zeros((PAD, width), F32)
            d_keys = jnp.zeros((PAD, width), F32)
            d_values = jnp.zeros((PAD, width), F32)
            for head in range(heads):
                lanes = head_lanes(width, head)
                own = jnp.where(lanes, queries, jnp.zeros_like(queries))
                d_own = jnp.where(lanes, d_mixed, jnp.zeros_like(d_mixed))
                probabilities = softmax_rows(masked_scores(own, key_rows, key_mask))
                d_probs = nt(d_own, values)
                row_dots = jnp.sum(d_probs * probabilities, axis=-1, keepdims=True)
                d_scores = probabilities * (d_probs - row_dots)
                d_scores = jnp.where(key_mask > 0, d_scores, 0.0).astype(BF16)
                d_values += tn(probabilities.astype(BF16), d_own)
                d_queries = jnp.where(lanes, nn(d_scores, key_rows), d_queries)
                d_keys += tn(d_scores, own)
            line += [d_queries * HD ** (-0.5), d_keys * HD ** (-0.5), d_values]
        parts.append(jnp.concatenate(line, axis=1).astype(BF16))
    return jnp.concatenate(parts, axis=0)


def heads_pull(
    dims, s_ref, normed, projected_ref, attended_ref, d_branch, packs, masks, router_ref, grads, biases
):
    images, heads, width, chunks, start, groups = dims
    weight, _, out_weight = chunk_weights(packs, width)
    d_attended = nt(d_branch, out_weight).astype(BF16)
    d_project = attend_pull(images, heads, width, chunks, projected_ref, d_attended, masks)
    grad = tn(normed, d_project)
    out_grad = tn(attended_ref[...], d_branch)
    for chunk in range(chunks):
        for part in range(3):
            at = (3 * chunk + part) * width
            grads[chunk][part * D : (part + 1) * D, :] = grad[:, at : at + width].astype(BF16)
        for block in range(D // width):
            at = 3 * D + block * width
            grads[chunk][at : at + width, :] = out_grad[
                chunk * width : (chunk + 1) * width, block * width : (block + 1) * width
            ].astype(BF16)
        per = EXPERTS // groups
        owner = jnp.bitwise_xor(s_ref[0], start + chunk)
        router = router_ref[0:per, :]
        for g in range(1, groups):
            router = jnp.where(owner == g, router_ref[g * per : (g + 1) * per, :], router)
        router = as_lines(router)
        grads[chunk][4 * D : 4 * D + router.shape[0], :] = router.astype(BF16)
        rest = grads[chunk].shape[0] - 4 * D - router.shape[0]
        if rest:
            grads[chunk][4 * D + router.shape[0] :, :] = jnp.zeros((rest, width), BF16)
    biases[...] = jnp.broadcast_to(
        jnp.sum(d_project.astype(F32), axis=0, keepdims=True), biases.shape
    )
    return nt(d_project, weight)


def middle_pull_kernel(
    dims, s_ref, cot_ref, part_ref, near_ref, top_ref, rest_ref, middle_ref, norms_ref, normed_ref, mask_ref,
    projected_ref, attended_ref, router_ref, *refs,
):
    images, chunks = dims[0], dims[3]
    packs, outs, mask_pad = refs[:chunks], refs[chunks:-1], refs[-1]
    d_low, sums, d_middle_ref, d_branch_ref, biases = outs[:5]
    tokens = images * PAD
    normal, inv_std = normalize(middle_ref[...])
    d_normed2 = part_ref[...][:tokens].astype(F32) + near_ref[...][:tokens].astype(F32)
    d_normed2 = d_normed2 + jnp.concatenate([top_ref[...], rest_ref[...]], axis=0).astype(F32)
    d_middle = cot_ref[...].astype(F32) + norm_pull(d_normed2, normal, inv_std, norms_ref[2:3, :])
    d_branch = d_middle.astype(BF16)
    d_middle_ref[...] = d_middle
    d_branch_ref[...] = d_branch
    sums[...] = jnp.concatenate(
        [
            jnp.sum(d_normed2 * normal, axis=0, keepdims=True),
            jnp.sum(d_normed2, axis=0, keepdims=True),
            jnp.sum(d_branch.astype(F32), axis=0, keepdims=True),
            jnp.zeros((5, D), F32),
        ],
        axis=0,
    )
    masks = key_masks(images, s_ref[0], mask_ref, mask_pad)
    d_low[...] = heads_pull(
        dims, s_ref, normed_ref[...], projected_ref, attended_ref, d_branch, packs, masks, router_ref,
        outs[5:], biases,
    )


def input_pull_kernel(
    dims, s_ref, x_ref, d_normed_ref, d_middle_ref, d_branch_ref, norms_ref, normed_ref, mask_ref,
    projected_ref, attended_ref, router_ref, *refs,
):
    images, chunks = dims[0], dims[3]
    packs, outs, mask_pad = refs[:chunks], refs[chunks:-1], refs[-1]
    d_inputs_ref, sums, biases = outs[:3]
    masks = key_masks(images, s_ref[0], mask_ref, mask_pad)
    d_normed = d_normed_ref[...] + heads_pull(
        dims, s_ref, normed_ref[...], projected_ref, attended_ref, d_branch_ref[...], packs, masks,
        router_ref, outs[3:], biases,
    )
    normal, inv_std = normalize(x_ref[...].astype(F32))
    d_inputs = d_middle_ref[...] + norm_pull(d_normed, normal, inv_std, norms_ref[0:1, :])
    d_inputs_ref[...] = d_inputs.astype(BF16)
    sums[...] = jnp.concatenate(
        [
            jnp.sum(d_normed * normal, axis=0, keepdims=True),
            jnp.sum(d_normed, axis=0, keepdims=True),
            jnp.sum(d_inputs * d_inputs * valid_column(images, masks), axis=0, keepdims=True),
            jnp.zeros((5, D), F32),
        ],
        axis=0,
    )


def expert_kernel(dims, begins, ends, s_ref, *refs):
    chunks, pieces, hidden_width, width, bias_at = dims
    at = 0

    def take(count):
        nonlocal at
        at += count
        return refs[at - count : at]

    rows_in, ups_in, packs, router_ref = take(1)[0], take(chunks), take(pieces), take(1)[0]
    weight_refs = take(max(pieces, 2))
    if not begins:
        d_before, marks_before, results_before, d_rows_before = take(4)
    if ends:
        back_bias_ref = take(1)[0]
    hidden_out, d_pre_out = take(2)
    if ends:
        d_rows_out, mixed_out, router_grad, back_bias_out = take(4)
    if begins:
        d_left = take(1)[0]
    if not ends:
        marks_left, results_left, d_rows_left = take(3)
    ups_wide, in_weight, back_weight, in_bias, results, d_rows = take(6)
    if pieces == 1:
        weights = [((weight_refs[0], 0), (weight_refs[1], 0))]
    else:
        weights = [((ref, 0), (ref, D)) for ref in weight_refs]
    expert, first = s_ref[1], s_ref[2]
    for chunk in range(chunks):
        at = pl.multiple_of(jnp.bitwise_xor(s_ref[3], chunk) * CAP, 8)
        ups_wide[pl.ds(at, CAP), :] = ups_in[chunk][...].astype(F32)
    lines = hidden_width // width
    for k in range(pieces):
        block = packs[k][bias_at:, :].astype(F32)
        bias_rows = block[0:lines]
        for e in range(1, block.shape[0] // lines):
            bias_rows = jnp.where(s_ref[0] == e, block[e * lines : (e + 1) * lines], bias_rows)
        for line in range(lines):
            in_bias[k : k + 1, line * width : (line + 1) * width] = bias_rows[line : line + 1]
    rows = rows_in[...]
    label = lax.broadcasted_iota(jnp.int32, (1, EXPERTS), 1)
    mine = label == expert
    if begins:
        other = ups_wide[:, D : D + 1]
        logits = nt(rows, router_ref[...])
        others = label.astype(F32) == other
        own_logit = jnp.sum(jnp.where(mine, logits, 0.0), axis=1, keepdims=True)
        other_logit = jnp.sum(jnp.where(others, logits, 0.0), axis=1, keepdims=True)
        peak = jnp.maximum(own_logit, other_logit)
        own_exp, other_exp = jnp.exp(own_logit - peak), jnp.exp(other_logit - peak)
        gate = own_exp / (own_exp + other_exp)
        other_gate = other_exp / (own_exp + other_exp)
        d_results = (gate * ups_wide[:, :D]).astype(BF16)
        d_left[...] = d_results
        results[...] = jnp.zeros_like(results)
        d_rows[...] = jnp.zeros_like(d_rows)
    else:
        d_results = d_before[...]
        gate, other_gate = marks_before[:, 0:1], marks_before[:, 1:2]
        other = marks_before[:, 2:3]
        others = label.astype(F32) == other
        results[...] = results_before[...]
        d_rows[...] = d_rows_before[...]

    def piece_step(piece, carry):
        for k in range(pieces):
            @pl.when(piece == k)
            def _():
                (in_ref, _), (back_ref, start) = weights[k]
                in_weight[...] = in_ref[0:D, :]
                back_weight[...] = back_ref[start:, :]

        pre_act = nn(rows, in_weight[...]) + in_bias[pl.ds(piece, 1), :]
        cdf = 0.5 * (1.0 + lax.erf(pre_act * (0.5**0.5)))
        hidden = (pre_act * cdf).astype(BF16)
        hidden_out[piece] = hidden
        results[...] += nn(hidden, back_weight[...])
        slope = cdf + pre_act * jnp.exp(-0.5 * pre_act * pre_act) * 0.3989422804014327
        d_pre = (slope * nt(d_results, back_weight[...])).astype(BF16)
        d_pre_out[piece] = d_pre
        d_rows[...] += nt(d_pre, in_weight[...])
        return carry

    lax.fori_loop(0, pieces, piece_step, 0)
    if not ends:
        lane = lax.broadcasted_iota(jnp.int32, (1, LANES), 1)
        marks_left[...] = jnp.where(lane == 0, gate, jnp.where(lane == 1, other_gate, other))
        results_left[...] = results[...]
        d_rows_left[...] = d_rows[...]
        return
    bias = jnp.where(first > 0, 1.0, 0.0) * back_bias_ref[...].astype(F32)
    pick = (lax.broadcasted_iota(jnp.int32, (EXPERTS, 1), 0) == expert).astype(F32)
    total = results[...] + jnp.sum(pick * bias, axis=0, keepdims=True)
    d_gate = jnp.sum(ups_wide[:, :D] * total, axis=1, keepdims=True)
    moved = gate * other_gate * d_gate
    d_logits = jnp.where(mine, moved, jnp.where(others, -moved, 0.0)).astype(BF16)
    router_grad[...] = tn(d_logits, rows)
    back_bias_out[...] = jnp.broadcast_to(
        jnp.sum(d_results.astype(F32), axis=0, keepdims=True), back_bias_out.shape
    )
    d_rows_out[...] = (d_rows[...] + nn(d_logits, router_ref[...])).astype(BF16)
    mixed_out[...] = (gate * total).astype(BF16)


def expert_grads_kernel(s_ref, rows_ref, d_ref, hiddens, d_pres, *refs):
    grads, sums = refs[:-1], refs[-1]
    hidden_width = hiddens.shape[2]
    sums[...] = jnp.zeros_like(sums)
    rows, d_results = rows_ref[...], d_ref[...]
    for k in range(hiddens.shape[0]):
        d_pre = d_pres[k]
        in_grad = tn(rows, d_pre)
        back_grad = tn(hiddens[k], d_results)
        bias_grad = jnp.sum(d_pre.astype(F32), axis=0, keepdims=True)
        sums[1:2, :] += jnp.sum(in_grad * in_grad)
        sums[2:3, :] += jnp.sum(bias_grad * bias_grad)
        sums[3:4, :] += jnp.sum(back_grad * back_grad)
        grads[2 * k][0:D, :] = in_grad.astype(BF16)
        grads[2 * k][D:, :] = jnp.broadcast_to(bias_grad, (16, hidden_width)).astype(BF16)
        grads[2 * k + 1][...] = back_grad.astype(BF16)


def output_kernel(
    images, s_ref, middle_ref, part_ref, near_ref, top_ref, rest_ref, mask_ref, *refs
):
    out_ref, sums, mask_pad = refs
    tokens = images * PAD
    mixture = part_ref[...][:tokens].astype(F32) + near_ref[...][:tokens].astype(F32)
    mixture = mixture + jnp.concatenate([top_ref[...], rest_ref[...]], axis=0).astype(F32)
    output = middle_ref[...] + mixture
    out_ref[...] = output.astype(BF16)
    valid = valid_column(images, key_masks(images, s_ref[0], mask_ref, mask_pad))
    sums[...] = jnp.concatenate(
        [
            jnp.sum(mixture * mixture * valid, axis=0, keepdims=True),
            jnp.sum(output * output * valid, axis=0, keepdims=True),
            jnp.zeros((6, D), F32),
        ],
        axis=0,
    )


def place_tokens_kernel(count, groups, images, s_ref, *refs):
    out, wide = refs[groups:]
    for group in range(groups):
        for image in range(images):
            rows = refs[group][image * PAD : (image + 1) * PAD, :].astype(F32)[:SEQ]
            at = jnp.bitwise_xor(s_ref[0], group) * images + image
            for k in range(D // LANES):
                wide[k, pl.ds(at, SEQ, stride=count), :] = rows[:, k * LANES : (k + 1) * LANES]
    for k in range(D // LANES):
        out[:, k * LANES : (k + 1) * LANES] = wide[k]


def place_experts_kernel(biased, s_ref, *refs):
    ins, outs = refs[:4], refs[4:]
    for group, source in enumerate(ins):
        @pl.when(pl.program_id(0) == group)
        def _():
            height = outs[0].shape[1]
            outs[0][0] = source[0:height, :].astype(F32)
            if biased:
                bias = source[height:, :].astype(F32)[0:1, :]
                outs[1][pl.ds(jnp.bitwise_xor(s_ref[0], group), 1), :] = bias


def split_kernel(chunks, s_ref, part_ref, near_ref, far_ref, out_ref):
    total = part_ref[...].astype(F32) + near_ref[...].astype(F32) + far_ref[...].astype(F32)
    share = total.shape[0] // chunks
    for chunk in range(chunks):
        out_ref[chunk] = total[chunk * share : (chunk + 1) * share].astype(BF16)


def join_kernel(dims, s_ref, pieces_ref, *refs):
    chunks, groups, half, width, small = dims
    norm1, norm2, forward, outputs, expert, back_bias, near_bias, far_bias = refs[:8]
    message, lines = refs[8:]
    total = pieces_ref[0].astype(F32)
    for chunk in range(1, chunks):
        total += pieces_ref[chunk].astype(F32)
    share = total.shape[0]
    row = lax.broadcasted_iota(jnp.int32, (share, 1), 0) + s_ref[3] * share
    squares = total * total
    lines[...] = jnp.zeros_like(lines)
    at = 0
    for source, index in ((norm1, 0), (norm1, 1), (norm2, 0), (norm2, 1), (norm2, 2)):
        lines[at : at + D // LANES, :] = as_lines(source[index : index + 1, :])
        at += D // LANES
    for part in (0, 2):
        for group in range(groups):
            biases, chunk = (near_bias, group) if group < half else (far_bias, group - half)
            line = biases[0:1, (3 * chunk + part) * width : (3 * chunk + part) * width + LANES]
            lines[pl.ds(at + jnp.bitwise_xor(s_ref[0], group), 1), :] = line
        at += groups
    lane = lax.broadcasted_iota(jnp.int32, (1, LANES), 1)
    terms = [
        jnp.sum(forward[0:1, :]),
        jnp.sum(forward[1:2, :]),
        jnp.sum(outputs[0:1, :]),
        jnp.sum(outputs[1:2, :]),
        jnp.sum(norm1[2:3, :]),
        jnp.sum(forward[2:3, :]) * (1.0 / D),
        jnp.sum(jnp.where(row < 3 * D, squares, 0.0)),
        jnp.sum(jnp.where((row >= 3 * D) & (row < 4 * D), squares, 0.0)),
        expert[1:2, 0:1],
        expert[2:3, 0:1],
        expert[3:4, 0:1],
    ]
    scalars = jnp.zeros((1, LANES), F32)
    for index, term in enumerate(terms):
        scalars = jnp.where(lane == index, term, scalars)
    lines[at : at + 1, :] = scalars
    lines[small - 8 : small - 8 + D // LANES, :] = as_lines(back_bias[0:1, :])
    values = lines[...]
    high = values.astype(BF16)
    low = (values - high.astype(F32)).astype(BF16)
    for chunk in range(chunks):
        message[chunk, 0:share, :] = total.astype(BF16)
        message[chunk, share : share + small, :] = high
        message[chunk, share + small :, :] = low


def spread_kernel(dims, s_ref, messages, qkv_out, out_out, sums, total):
    chunks, groups, width, small = dims
    share = messages.shape[1] - 2 * small
    summed = jnp.zeros((small, LANES), F32)
    at = small - 8
    for chunk in range(chunks):
        total[chunk * share : (chunk + 1) * share, :] = messages[chunk, 0:share, :].astype(F32)
        lines = messages[chunk, share : share + small, :].astype(F32) + messages[
            chunk, share + small :, :
        ].astype(F32)
        summed += lines
        sums[at : at + D // LANES, :] = lines[small - 8 : small - 8 + D // LANES]
        at += D // LANES
    sums[0 : small - 8, :] = summed[0 : small - 8]
    per = EXPERTS // groups * (D // LANES)
    sums[at : at + per, :] = total[4 * D : 4 * D + per, :]
    qkv_out[...] = total[0 : 3 * D, :]
    for block in range(D // width):
        out_out[:, block * width : (block + 1) * width] = total[
            3 * D + block * width : 3 * D + (block + 1) * width, :
        ]


def finish_kernel(dims, s_ref, mine_ref, came_ref, *refs):
    chunks, groups, half, small, shared = dims
    gain1, shift1, gain2, shift2, out_bias, bias_out, router_out, back_out, norms_out, rms_out = refs
    per = D // LANES
    top = small - 8
    summed = mine_ref[0:top, :] + came_ref[0:top, :]
    squares = []
    for index, out in enumerate((gain1, shift1, gain2, shift2, out_bias)):
        block = summed[index * per : (index + 1) * per]
        squares.append(jnp.sum(block * block))
        out[...] = as_rows(block)
    at = 5 * per
    biases = summed[at : at + 2 * groups]
    place = lax.broadcasted_iota(jnp.int32, (groups, 1), 0) == s_ref[0]
    for part in range(2):
        lines = biases[part * groups : (part + 1) * groups]
        bias_out[part : part + 1, :] = jnp.sum(
            jnp.where(place, lines, 0.0), axis=0, keepdims=True
        )
    scalars = summed[at + 2 * groups : at + 2 * groups + 1]
    lane = lax.broadcasted_iota(jnp.int32, (1, LANES), 1)

    def scalar(index):
        return jnp.sum(jnp.where(lane == index, scalars, 0.0))

    share = EXPERTS // groups
    size = chunks * per + share * per
    for group in range(groups):
        source = mine_ref if group < half else came_ref
        start = top + (group if group < half else group - half) * size
        owner = jnp.bitwise_xor(s_ref[0], group)
        lane_expert = owner if shared else 0
        for chunk in range(chunks):
            line = as_rows(source[start + chunk * per : start + (chunk + 1) * per, :])
            back_out[pl.ds(chunk * s_ref[4] + lane_expert, 1), :] = line
        start += chunks * per
        router_rows = as_rows(source[start : start + share * per, :])
        for g in range(groups):
            @pl.when(owner == g)
            def _():
                router_out[g * share : (g + 1) * share, :] = router_rows
    router, back_bias = router_out[...], back_out[...]
    ordered = [
        squares[0], squares[1], scalar(6), jnp.sum(biases * biases), scalar(7), squares[4],
        squares[2], squares[3], jnp.sum(router * router), scalar(8), scalar(9), scalar(10),
        jnp.sum(back_bias * back_bias),
    ]
    norms = jnp.zeros((1, LANES), F32)
    for index, value in enumerate(ordered):
        norms = jnp.where(lane == index, value, norms)
    norms_out[...] = jnp.sqrt(norms)
    rms_out[...] = jnp.sqrt(scalars / (scalar(5) * D))


def shards(
    inputs, valid_mask, expert_ids, slot_ids, norm1_gain, norm1_bias, w_qkv, b_qv, w_out, b_out,
    norm2_gain, norm2_bias, w_router, w_in, b_in, w_back, b_back, cotangent, dp_size, tensor_size,
):
    count = inputs.shape[0]
    groups = tensor_size
    images = count // groups
    local_width = w_qkv.shape[2]
    heads = local_width // HD
    width = -(-local_width // LANES) * LANES
    local_experts, _, hidden_width = w_in.shape
    shared = local_experts == groups == 4
    pieces = groups if shared else 1
    chunks = dp_size
    rows = chunks * CAP
    own_tokens = images * PAD
    half = groups // 2
    data_at = lax.axis_index("dp").astype(jnp.int32)
    head_at = lax.axis_index("tensor").astype(jnp.int32)
    lane_expert = head_at if shared else jnp.int32(0)
    expert_at = data_at * local_experts + lane_expert
    first = jnp.int32(1) if shared else (head_at == 0).astype(jnp.int32)
    scalars = jnp.stack(
        [head_at, expert_at, first, data_at, jnp.int32(local_experts), lane_expert]
    )
    x_lines = jnp.transpose(inputs, (1, 0, 2)).reshape(SEQ * count, D)
    cot_lines = jnp.transpose(cotangent, (1, 0, 2)).reshape(SEQ * count, D)
    ids = jnp.transpose(expert_ids, (0, 2, 1))
    slots = jnp.transpose(slot_ids, (0, 2, 1))
    norms = jnp.stack([norm1_gain, norm1_bias, norm2_gain, norm2_bias, b_out]).astype(F32)
    router = jnp.transpose(w_router)
    last = [None]

    def call(kernel, ins, outs, **options):
        at = scalars if last[0] is None else after(scalars, last[0])
        got = run(kernel, at, ins, outs, **options)
        last[0] = got[0]
        return got

    def over(axis, size, value, by, *others):
        return swap(after(value, *others) if others else value, axis, size, by)

    def core(value, *others):
        return over("tensor", groups, value, 1, *others)

    def gather(value):
        parts = [value] + [None] * (groups - 1)
        for r in range(2, groups, 2):
            parts[r] = over("tensor", groups, value, r)
        for r in range(1, groups, 2):
            parts[r] = core(parts[r - 1])
        return parts

    def exchange(value, *others):
        value = after(value, *others) if others else value
        return lax.all_to_all(value.reshape(chunks, CAP, -1), "dp", 0, 0).reshape(rows, -1)

    fill = width - local_width
    qkv = jnp.pad(jnp.transpose(w_qkv, (1, 0, 2)), [(0, 0), (0, 0), (0, fill)])
    qkv = qkv.reshape(3 * D, width)
    out_rows = jnp.pad(w_out, [(0, fill), (0, 0)])
    qv_bias = jnp.pad(b_qv, [(0, 0), (0, fill)])
    bias_at = 4 * D + 16
    bias_lines = -(-(local_experts * hidden_width // width) // 16) * 16
    pack = call(
        functools.partial(pack_kernel, width),
        [qkv, out_rows, qv_bias, b_in], [((bias_at + bias_lines, width), BF16)], mib=58,
    )[0]
    packs = [pack, core(pack)] + [None] * (groups - 2)
    for r in range(2, groups, 2):
        packs[r] = over("tensor", groups, pack, r)

    block = D + hidden_width
    tall = D // LANES, SEQ * count, LANES
    got = call(
        functools.partial(start_kernel, (count, images, chunks, shared)),
        [ids, slots, cot_lines] + ([w_in, w_back] if shared else []),
        [((own_tokens, D), BF16)]
        + (
            [((block, D), BF16)] * pieces if shared else []
        )
        + [((CAP, D + LANES), BF16)] * chunks,
        left=(3, 4), mib=58,
        scratch=[
            pltpu.VMEM(tall, F32), pltpu.VMEM((own_tokens, D), F32),
            pltpu.VMEM((rows, D + LANES), F32),
            pltpu.SemaphoreType.DMA((8,)),
        ],
    )
    cot_own, up_sent = got[0], got[-chunks:]
    if shared:
        weights_sent = got[1 : 1 + pieces]
    merged = chunks // 2
    ups = list(up_sent)

    def send_ups(turn, *others):
        for r in turn:
            ups[r] = over("dp", chunks, up_sent[r], r, *others)
        return [ups[r] for r in turn]

    turn = send_ups(range(merged, chunks))
    for r in range(2, groups, 2):
        packs[r + 1] = core(packs[r], cot_own)

    def heads_out(parts):
        return [((own_tokens, parts * 3 * width), BF16), ((own_tokens, parts * width), BF16)]

    mask_pad = pltpu.VMEM((8, WIDE), jnp.int32)
    x_own, normed1, branch_part, projected_near, attended_near = call(
        functools.partial(first_heads_kernel, count, images, heads, width, half),
        [x_lines, norms, valid_mask, *packs[:half]],
        [((own_tokens, D), BF16), ((own_tokens, D), BF16), ((own_tokens, D), F32)]
        + heads_out(half),
        scratch=[pltpu.VMEM(tall, F32), pltpu.VMEM((own_tokens, D), F32), mask_pad],
    )
    normed2, middle, forward_sums, projected_far, attended_far = call(
        functools.partial(last_heads_kernel, images, heads, width, groups - half),
        [x_own, normed1, branch_part, norms, valid_mask, *packs[half:]],
        [((own_tokens, D), BF16), ((own_tokens, D), F32), ((8, D), F32)]
        + heads_out(groups - half),
        scratch=[mask_pad],
    )

    normed2 = after(normed2, *turn)
    tokens = [normed2, core(normed2)] + [None] * (groups - 2)
    weights = list(weights_sent) if shared else []
    turn = []
    if shared:
        weights[1] = core(weights[1], normed2)
        turn.append(weights[1])
    for r in range(2, groups, 2):
        tokens[r] = over("tensor", groups, normed2, r)
    for r in range(2, groups, 2):
        tokens[r + 1] = core(tokens[r], *turn)
    if shared:
        weights[2] = over("tensor", groups, weights[2], 2, tokens[2])
        weights[3] = over("tensor", groups, weights[3], 3, tokens[3])
    flat_pad = pltpu.VMEM((8, WIDE), jnp.int32)
    sent = call(
        functools.partial(dispatch_kernel, groups, images, chunks),
        [ids, slots, *tokens], [((rows, D), BF16)], scratch=[flat_pad],
    )[0]
    send_ups(range(1, merged), sent)
    dispatched = exchange(sent)

    def expert(begins, ends, count, weights, before=()):
        outs = [((count, rows, hidden_width), BF16)] * 2
        if ends:
            outs += [((rows, D), BF16)] * 2 + [((EXPERTS, D), F32), ((8, D), F32)]
        if begins:
            outs += [((rows, D), BF16)]
        if not ends:
            outs += [((rows, LANES), F32), ((rows, D), F32), ((rows, D), F32)]
        dims = chunks, count, hidden_width, width, bias_at
        held = packs[:count] if begins else packs[-count:]
        return call(
            functools.partial(expert_kernel, dims, begins, ends),
            [dispatched, *ups, *held, router, *weights, *before] + ([b_back] if ends else []),
            outs,
            scratch=[
                pltpu.VMEM((rows, D + LANES), F32),
                pltpu.VMEM((D, hidden_width), BF16),
                pltpu.VMEM((hidden_width, D), BF16),
                pltpu.VMEM((8, hidden_width), F32),
                pltpu.VMEM((rows, D), F32),
                pltpu.VMEM((rows, D), F32),
            ],
            mib=MIB_EXPERT,
        )

    if shared:
        hidden_one, d_pre_one, d_results, *left = expert(True, False, 2, weights[:2])
        hidden_two, d_pre_two, d_sent, mixed_sent, router_part, back_bias = expert(
            False, True, 2, weights[2:], [d_results, *left]
        )
        hiddens, d_pres = [hidden_one, hidden_two], [d_pre_one, d_pre_two]
    else:
        hidden, d_pre, d_sent, mixed_sent, router_part, back_bias, d_results = expert(
            True, True, 1, [w_in[0], w_back[0]]
        )
        hiddens, d_pres = [hidden], [d_pre]
    d_back = exchange(d_sent)
    grads, expert_sums = [], []
    for hidden, d_pre in zip(reversed(hiddens), reversed(d_pres)):
        pair = [((D + 16, hidden_width), BF16), ((hidden_width, D), BF16)]
        *some, sums = call(
            expert_grads_kernel, [dispatched, d_results, hidden, d_pre],
            pair * hidden.shape[0] + [((8, LANES), F32)], mib=58,
        )
        grads = some + grads
        expert_sums.append(sums)

    def combine(value):
        return call(
            functools.partial(combine_kernel, groups, images, chunks),
            [ids, slots, value],
            [((half * own_tokens, D), BF16)] * 2, scratch=[flat_pad],
        )

    def reduce_own(keep, send, size, *others):
        came = core(send)
        far = [None, None]
        for r in range(2, groups, 2):
            for part in range(2):
                start = r // 2 * size + part * (size // 2)
                span = slice(start, start + size // 2)
                out = (keep[span].astype(F32) + came[span].astype(F32)).astype(BF16)
                term = over("tensor", groups, out, r, *others)
                if far[part] is not None:
                    term = far[part].astype(F32) + term.astype(F32)
                far[part] = term
        return keep, came, far

    if shared:
        in_last = over("tensor", groups, grads[6], 2)
        d_back = after(d_back, in_last)
    d_keep, d_near, d_far = reduce_own(*combine(d_back), own_tokens)
    if shared:
        back_last = over("tensor", groups, grads[7], 2, *d_far)
    mixed = exchange(mixed_sent, d_far[0])

    router_lines = EXPERTS // groups * (D // LANES)
    share = -(-(4 * D + router_lines) // (16 * chunks)) * 16

    def grads_out(parts):
        return [((8, parts * 3 * width), F32)] + [((chunks * share, width), BF16)] * parts

    got = call(
        functools.partial(
            middle_pull_kernel, (images, heads, width, groups - half, half, groups)
        ),
        [cot_own, d_keep, d_near, *d_far, middle, norms, normed1, valid_mask, projected_far,
         attended_far, router_part, *packs[half:]],
        [((own_tokens, D), F32), ((8, D), F32), ((own_tokens, D), F32), ((own_tokens, D), BF16)]
        + grads_out(groups - half),
        scratch=[mask_pad], mib=MIB_PULL,
    )
    d_low, norm2_sums, d_middle, d_branch, far_bias = got[:5]
    far_grads = list(got[5:])

    def add_odd(grads):
        return (grads[0].astype(F32) + core(grads[1]).astype(F32)).astype(BF16)

    if shared:
        far_grads[1] = after(far_grads[1], back_last)
    far = None
    for r in range(0, groups - half, 2):
        out = add_odd(far_grads[r : r + 2])
        d_low = after(d_low, out)
        term = over("tensor", groups, out, half + r)
        far = term if far is None else far.astype(F32) + term.astype(F32)
    got = call(
        functools.partial(input_pull_kernel, (images, heads, width, half, 0, groups)),
        [x_own, d_low, d_middle, d_branch, norms, normed1, valid_mask, projected_near,
         attended_near, router_part, *packs[:half]],
        [((own_tokens, D), BF16), ((8, D), F32)] + grads_out(half),
        scratch=[mask_pad], mib=MIB_PULL,
    )
    d_own, norm1_sums, near_bias = got[:3]
    head_grads = list(got[3:])
    for r in range(2, half, 2):
        term = over("tensor", groups, add_odd(head_grads[r : r + 2]), r)
        far = far.astype(F32) + term.astype(F32)
    near = core(head_grads[1], far)
    d_tokens = gather(d_own)
    split = call(
        functools.partial(split_kernel, chunks),
        [head_grads[0], near, far], [((chunks, share, width), BF16)],
    )[0]
    pieces_in = lax.all_to_all(split, "dp", 0, 0)

    mix_keep, mix_near, mix_far = reduce_own(*combine(after(mixed, d_tokens[2])), own_tokens)
    output_own, output_sums = call(
        functools.partial(output_kernel, images),
        [middle, mix_keep, mix_near, *mix_far, valid_mask],
        [((own_tokens, D), BF16), ((8, D), F32)], scratch=[mask_pad],
    )
    out_tokens = gather(output_own)

    def place_tokens(parts):
        placed = call(
            functools.partial(place_tokens_kernel, count, groups, images),
            parts, [((SEQ * count, D), F32)],
            scratch=[pltpu.VMEM(tall, F32)],
        )[0]
        return jnp.transpose(placed.reshape(SEQ, count, D), (1, 0, 2))

    def place_experts(parts, shape, bias):
        spec = pl.BlockSpec((1, *shape), lambda step, s: (jnp.bitwise_xor(s[0], step), 0, 0))
        return call(
            functools.partial(place_experts_kernel, bool(bias)), parts,
            [((local_experts, *shape), F32)] + bias, grid=(groups,), out_specs={0: spec},
        )

    small = -(-(5 * D // LANES + 2 * groups + 1) // 8) * 8 + 8
    small = -(-small // 16) * 16
    message = call(
        functools.partial(join_kernel, (chunks, groups, half, width, small)),
        [pieces_in, after(norm1_sums, d_tokens[groups - 1]), norm2_sums, forward_sums, output_sums,
         sum(expert_sums), back_bias, near_bias, far_bias],
        [((chunks, share + 2 * small, width), BF16)], scratch=[pltpu.VMEM((small, LANES), F32)],
        mib=58,
    )[0]
    messages = lax.all_to_all(message, "dp", 0, 0)
    d_inputs = place_tokens(d_tokens)
    output = place_tokens(out_tokens)
    if shared:
        in_far = over("tensor", groups, grads[4], 2, out_tokens[2])
        back_far = over("tensor", groups, grads[5], 2, in_far)
        g_w_in, g_b_in = place_experts(
            [grads[0], core(grads[2]), in_far, core(in_last)], (D, hidden_width),
            [((local_experts, hidden_width), F32)],
        )
    top = small - 8
    qkv_sum, out_sum, sums = call(
        functools.partial(spread_kernel, (chunks, groups, width, small)),
        [messages],
        [((3 * D, width), F32), ((width, D), F32),
         ((top + chunks * (D // LANES) + router_lines, LANES), F32)],
        scratch=[pltpu.VMEM((chunks * share, width), F32)],
    )
    by = 1
    while True:
        came = over("tensor", groups, sums, by)
        by *= 2
        if by == groups:
            break
        sums = jnp.concatenate([sums[:top] + came[:top], sums[top:], came[top:]], axis=0)

    if shared:
        (g_w_back,) = place_experts(
            [grads[1], core(grads[3]), back_far, core(back_last)], (hidden_width, D), []
        )
    else:
        g_w_in = grads[0][None, :D].astype(F32)
        g_w_back = grads[1][None].astype(F32)
        g_b_in = grads[0][D : D + 1].astype(F32)

    vector = [((1, D), F32)]
    (
        g_norm1_gain, g_norm1_bias, g_norm2_gain, g_norm2_bias, g_b_out, g_b_qv, router_grad,
        g_b_back, grad_norms, rms_values,
    ) = call(
        functools.partial(finish_kernel, (chunks, groups, half, small, shared)),
        [sums, came],
        vector * 5
        + [((2, LANES), F32), ((EXPERTS, D), F32), ((EXPERTS, D), F32)]
        + [((1, LANES), F32)] * 2,
    )
    g_w_qkv = jnp.transpose(qkv_sum.reshape(3, D, width), (1, 0, 2))[:, :, :local_width]
    return (
        output, d_inputs, g_norm1_gain[0], g_norm1_bias[0], g_w_qkv, g_b_qv[:, :local_width],
        out_sum[:local_width], g_b_out[0], g_norm2_gain[0], g_norm2_bias[0],
        jnp.transpose(router_grad), g_w_in, g_b_in, g_w_back, g_b_back,
        grad_norms[0, :13], rms_values[0, :5],
    )


def solution(mesh):
    placed = (
        P("dp", None, None),
        P("dp", None),
        P("dp", None, None),
        P("dp", None, None),
        P(),
        P(),
        P(None, None, "tensor"),
        P(None, "tensor"),
        P("tensor", None),
        P(),
        P(),
        P(),
        P(),
        P("dp", None, "tensor"),
        P("dp", "tensor"),
        P("dp", "tensor", None),
        P(),
        P("dp", None, None),
    )
    return jax.shard_map(
        functools.partial(shards, dp_size=mesh.shape["dp"], tensor_size=mesh.shape["tensor"]),
        mesh=mesh,
        in_specs=placed,
        out_specs=(
            P("dp", None, None),
            P("dp", None, None),
            P(),
            P(),
            P(None, None, "tensor"),
            P(None, "tensor"),
            P("tensor", None),
            P(),
            P(),
            P(),
            P(),
            P("dp", None, "tensor"),
            P("dp", "tensor"),
            P("dp", "tensor", None),
            P(),
            P(),
            P(),
        ),
        check_vma=False,
    )
```

```python
import functools

import jax
import jax.numpy as jnp
from jax import lax
from jax.experimental import pallas as pl
from jax.experimental.pallas import tpu as pltpu
from jax.sharding import PartitionSpec as P

D = 512
HD = 64
EXPERTS = 32
SEQ = 197
CAP = 104
PAD = 208
WIDE = 256
MIB_HEADS = 58
MIB_EXPERT = 58
MIB_GRADS = 58
MIB_PULL = 58
LANES = 128
F32 = jnp.float32
BF16 = jnp.bfloat16


def nn(a, b):
    return lax.dot_general(a, b, (((1,), (0,)), ((), ())), preferred_element_type=F32)


def nt(a, b):
    return lax.dot_general(a, b, (((1,), (1,)), ((), ())), preferred_element_type=F32)


def tn(a, b):
    return lax.dot_general(a, b, (((0,), (0,)), ((), ())), preferred_element_type=F32)


def swap(value, axis, size, by):
    return lax.ppermute(value, axis, [(at, at ^ by) for at in range(size)])


def after(value, *others):
    return lax.optimization_barrier((value, *others))[0]


class Held:
    def __init__(self, ref, copy):
        self.ref, self.copy, self.there = ref, copy, False
        self.shape, self.dtype = ref.shape, ref.dtype

    def __getitem__(self, index):
        if not self.there:
            self.copy.wait()
            self.there = True
        return self.ref[index]


class Sent:
    def __init__(self, ref, copy):
        self.ref, self.copy, self.left = ref, copy, False
        self.shape, self.dtype = ref.shape, ref.dtype

    def __getitem__(self, index):
        return self.ref[index]

    def __setitem__(self, index, value):
        self.ref[index] = value

    def send(self):
        if not self.left:
            self.copy.start()
            self.left = True


def streamed(kernel, ins, outs, scratch):
    shapes = [(a.shape, a.dtype) for a in ins] + list(outs)

    def body(s_ref, *refs):
        far, refs = refs[: len(shapes)], refs[len(shapes) :]
        near, refs, sems = refs[: len(shapes)], refs[len(shapes) : -1], refs[-1]
        held = []
        for i in range(len(ins)):
            copy = pltpu.make_async_copy(far[i], near[i], sems.at[i])
            copy.start()
            held.append(Held(near[i], copy))
        sent = [
            Sent(near[i], pltpu.make_async_copy(near[i], far[i], sems.at[i]))
            for i in range(len(ins), len(shapes))
        ]
        kernel(s_ref, *held, *sent, *refs)
        for value in held:
            if not value.there:
                value.copy.wait()
        for value in sent:
            value.send()
        for value in sent:
            value.copy.wait()

    buffers = [pltpu.VMEM(shape, dtype) for shape, dtype in shapes]
    return body, [*buffers, *scratch, pltpu.SemaphoreType.DMA((len(shapes),))]


def run(
    kernel, scalars, ins, outs, scratch=(), grid=(1,), in_specs=None, out_specs=None, mib=28, left=(),
    stream=False,
):
    in_specs, out_specs = in_specs or {}, out_specs or {}
    if stream:
        kernel, scratch = streamed(kernel, ins, outs, scratch)
        left = range(len(ins))
        out_specs = {i: pl.BlockSpec(memory_space=pl.ANY) for i in range(len(outs))}

    def whole(shape, stays=False):
        if stays:
            return pl.BlockSpec(memory_space=pl.ANY)
        return pl.BlockSpec(shape, lambda step, s, nd=len(shape): (0,) * nd)

    return pl.pallas_call(
        kernel,
        grid_spec=pltpu.PrefetchScalarGridSpec(
            num_scalar_prefetch=1,
            grid=grid,
            in_specs=[
                in_specs[i] if i in in_specs else whole(a.shape, i in left)
                for i, a in enumerate(ins)
            ],
            out_specs=[out_specs[i] if i in out_specs else whole(o[0]) for i, o in enumerate(outs)],
            scratch_shapes=list(scratch),
        ),
        out_shape=[jax.ShapeDtypeStruct(shape, dtype) for shape, dtype in outs],
        compiler_params=pltpu.CompilerParams(vmem_limit_bytes=mib * 2**20),
        cost_estimate=pl.CostEstimate(flops=0, bytes_accessed=0, transcendentals=0),
    )(scalars, *ins)


def route_rows(ids_ref, slots_ref, image):
    ids, slots = ids_ref[image], slots_ref[image]
    return jnp.where(slots < CAP, ids * CAP + slots, -1)


def block_start(s_ref, chunk):
    return (chunk * s_ref[4] + s_ref[5]) * CAP


def target_column(s_ref, chunks):
    rows = lax.broadcasted_iota(jnp.int32, (CAP, 1), 0)
    starts = [block_start(s_ref, chunk) for chunk in range(chunks)]
    return jnp.concatenate([rows + start for start in starts], axis=0)


def target_row(s_ref, chunks):
    lanes = lax.broadcasted_iota(jnp.int32, (1, chunks * CAP), 1)
    target = lanes
    for chunk in range(chunks):
        here = (lanes >= chunk * CAP) & (lanes < (chunk + 1) * CAP)
        target = jnp.where(here, lanes + (block_start(s_ref, chunk) - chunk * CAP), target)
    return target


def spread(source_ref, wide_ref, count):
    for k in range(D // LANES):
        wide_ref[k] = source_ref[:, k * LANES : (k + 1) * LANES].astype(F32)

    def image_rows(image):
        return jnp.concatenate(
            [wide_ref[k, pl.ds(image, SEQ, stride=count), :] for k in range(D // LANES)], axis=1
        )

    return image_rows


def own_rows(images, me, image_rows, out_ref, padded):
    padded[...] = jnp.zeros_like(padded)
    for image in range(images):
        padded[image * PAD : image * PAD + SEQ, :] = image_rows(me * images + image)
    out_ref[...] = padded[...].astype(BF16)


def pack_kernel(width, s_ref, qkv_ref, out_ref, bias_ref, in_bias_ref, pack):
    pack[0 : 3 * D, :] = qkv_ref[...]
    for block in range(D // width):
        at = 3 * D + block * width
        pack[at : at + width, :] = out_ref[:, block * width : (block + 1) * width]
    bias = bias_ref[...].astype(F32)
    experts, hidden = in_bias_ref.shape
    lines = in_bias_ref[...].astype(F32)
    lines = [
        lines[e : e + 1, k * width : (k + 1) * width]
        for e in range(experts)
        for k in range(hidden // width)
    ]
    fill = -len(lines) % 16
    if fill:
        lines.append(jnp.zeros((fill, width), F32))
    pack[4 * D :, :] = jnp.concatenate(
        [bias[0:1], bias[1:2], jnp.zeros((14, width), F32), *lines], axis=0
    ).astype(BF16)


def weight_copies(s_ref, w_in, w_back, blocks, sems):
    copies = []
    for index, (r, block) in enumerate(blocks):
        expert = jnp.bitwise_xor(s_ref[0], r)
        for side, (source, target) in enumerate(
            (
                (w_in.at[expert], block.at[pl.ds(0, D)]),
                (w_back.at[expert], block.at[pl.ds(D, w_back.shape[1])]),
            )
        ):
            copies.append(pltpu.make_async_copy(source, target, sems.at[2 * index + side]))
    return copies


def start_kernel(dims, s_ref, ids_ref, slots_ref, cot_ref, *refs):
    count, images, chunks, shared = dims
    copies = []
    if shared:
        w_in, w_back, *refs = refs
    own, *refs = refs
    near_outs, far_out, refs = refs[: chunks // 2], refs[chunks // 2], refs[chunks // 2 + 1 :]
    if shared:
        laid, refs = refs[:3], refs[3:]
    wide, padded, blocks, wholes, sems = refs
    if shared:
        copies = weight_copies(s_ref, w_in, w_back, list(enumerate(laid, 1)), sems)
    for copy in copies:
        copy.start()
    image_rows = spread(cot_ref, wide, count)
    target = target_column(s_ref, chunks)
    rows = chunks * CAP
    blocks[...] = jnp.zeros_like(blocks)

    def step(pair, carry):
        total = jnp.zeros((rows, D), F32)
        others = jnp.zeros((rows, SEQ), F32)
        for image in (2 * pair, 2 * pair + 1):
            flat = route_rows(ids_ref, slots_ref, image)
            ids = ids_ref[image].astype(F32)
            first = target == flat[0:1, :]
            second = target == flat[1:2, :]
            hit = (first | second).astype(F32).astype(BF16)
            total += nn(hit, image_rows(image).astype(BF16))
            others += jnp.where(first, ids[1:2, :], 0.0) + jnp.where(second, ids[0:1, :], 0.0)
        blocks[:, :D] += total
        blocks[:, D:] += jnp.broadcast_to(jnp.sum(others, axis=1, keepdims=True), (rows, LANES))
        return carry

    lax.fori_loop(0, count // 2, step, 0)
    for chunk in range(chunks):
        at = pl.multiple_of(jnp.bitwise_xor(s_ref[3], chunk) * CAP, 8)
        wholes[chunk * CAP : (chunk + 1) * CAP, :] = blocks[pl.ds(at, CAP), :]
    for chunk, near_out in enumerate(near_outs):
        near_out[...] = wholes[chunk * CAP : (chunk + 1) * CAP, :].astype(BF16)
    far_out[...] = wholes[rows // 2 :, :].astype(BF16)
    own_rows(images, s_ref[0], image_rows, own, padded)
    for copy in copies:
        copy.wait()


def padded_routes(ids_ref, slots_ref, image, flat_ref):
    flat_ref[...] = jnp.full(flat_ref.shape, -1, jnp.int32)
    flat_ref[0:2, 0:SEQ] = route_rows(ids_ref, slots_ref, image)
    return flat_ref[...]


def dispatch_kernel(groups, images, chunks, s_ref, ids_ref, slots_ref, *refs):
    tokens, (far, late, out, *passed, flat_ref) = refs[:groups], refs[groups:]
    for chunk, on in enumerate(passed, 1):
        on[0:CAP, :] = far[chunk * CAP : (chunk + 1) * CAP, :]
    passed[-1][CAP:, :] = late[...]
    me = s_ref[0]
    target = target_column(s_ref, chunks)
    total = jnp.zeros((chunks * CAP, D), F32)
    for group in range(groups):
        for image in range(images):
            at = jnp.bitwise_xor(me, group) * images + image
            flat = padded_routes(ids_ref, slots_ref, at, flat_ref)[:, :PAD]
            hit = (target == flat[0:1, :]) | (target == flat[1:2, :])
            total += nn(
                hit.astype(F32).astype(BF16), tokens[group][image * PAD : (image + 1) * PAD, :]
            )
    out[...] = total.astype(BF16)


def combine_kernel(groups, images, chunks, s_ref, ids_ref, slots_ref, rows_ref, *refs):
    outs, flat_ref = refs[:2], refs[2]
    me = s_ref[0]
    rows = rows_ref[...]
    target = target_row(s_ref, chunks)
    for group in range(groups):
        for image in range(images):
            at = jnp.bitwise_xor(me, group) * images + image
            flat = jnp.transpose(padded_routes(ids_ref, slots_ref, at, flat_ref))[:PAD, :]
            hit = (flat[:, 0:1] == target) | (flat[:, 1:2] == target)
            place = (group // 2 * images + image) * PAD
            outs[group % 2][place : place + PAD, :] = nn(
                hit.astype(F32).astype(BF16), rows
            ).astype(BF16)


def chunk_weights(packs, width):
    qkv = [p[part * D : (part + 1) * D, :] for p in packs for part in range(3)]
    biases = []
    for p in packs:
        lines = p[3 * D + D : 3 * D + D + 16, :].astype(F32)
        biases += [lines[0:1], jnp.zeros((1, width), F32), lines[1:2]]
    outs = [
        jnp.concatenate(
            [p[3 * D + b * width : 3 * D + (b + 1) * width, :] for b in range(D // width)], axis=1
        )
        for p in packs
    ]
    return (
        jnp.concatenate(qkv, axis=1),
        jnp.concatenate(biases, axis=1),
        jnp.concatenate(outs, axis=0),
    )


def normalize(values):
    average = jnp.mean(values, axis=-1, keepdims=True)
    centered = values - average
    inv_std = lax.rsqrt(jnp.mean(centered * centered, axis=-1, keepdims=True) + 1e-06)
    return centered * inv_std, inv_std


def norm_pull(upstream, normal, inv_std, gain):
    scaled = upstream * gain
    inner = jnp.mean(scaled * normal, axis=-1, keepdims=True)
    return inv_std * (scaled - jnp.mean(scaled, axis=-1, keepdims=True) - normal * inner)


def key_masks(images, me, mask_ref, pad_ref):
    pad_ref[...] = jnp.full(pad_ref.shape, -1, jnp.int32)
    for image in range(images):
        pad_ref[image : image + 1, 0:SEQ] = mask_ref[pl.ds(me * images + image, 1), :]
    return pad_ref[...]


def valid_column(images, masks):
    columns = jnp.transpose(jnp.maximum(masks, 0).astype(F32))
    return jnp.concatenate([columns[:PAD, i : i + 1] for i in range(images)], axis=0)


def probabilities_of(queries, key_rows, key_mask):
    shift = jnp.where(key_mask > 0, 0.0, jnp.where(key_mask < 0, -2e30, -1e30))
    scores = nt(queries * jnp.asarray(HD ** (-0.5), BF16), key_rows) + shift
    exps = jnp.exp(scores - jnp.max(scores, axis=-1, keepdims=True))
    return exps * (1.0 / jnp.sum(exps, axis=-1, keepdims=True))


def by_head(rows, heads):
    zeros = jnp.zeros_like(rows)
    width = rows.shape[1]
    return jnp.concatenate(
        [jnp.where(head_lanes(width, head), rows, zeros) for head in range(heads)], axis=0
    )


def own_lanes(stacked, heads):
    result = stacked[:PAD]
    for head in range(1, heads):
        lanes = head_lanes(stacked.shape[1], head)
        result = jnp.where(lanes, stacked[head * PAD : (head + 1) * PAD], result)
    return result


def head_lanes(width, head):
    lane = lax.broadcasted_iota(jnp.int32, (1, width), 1)
    return (lane >= head * HD) & (lane < (head + 1) * HD)


def attend(images, heads, width, chunks, normed, weight, bias, masks, projected_ref):
    projected = (nn(normed, weight) + bias).astype(BF16)
    projected_ref[...] = projected
    projected_ref.send()
    parts = []
    for image in range(images):
        key_mask = masks[image : image + 1, :PAD]
        line = []
        for chunk in range(chunks):
            queries, key_rows, values = (
                projected[
                    image * PAD : (image + 1) * PAD,
                    (3 * chunk + part) * width : (3 * chunk + part + 1) * width,
                ]
                for part in range(3)
            )
            own = by_head(queries, heads)
            probabilities = probabilities_of(own, key_rows, key_mask)
            mixed = own_lanes(nn(probabilities.astype(BF16), values), heads)
            line.append(mixed.astype(BF16))
        parts.append(jnp.concatenate(line, axis=1))
    return projected, jnp.concatenate(parts, axis=0)


def heads_kernel(count, images, heads, width, chunks, s_ref, x_ref, norms_ref, mask_ref, *refs):
    packs, outs = refs[:chunks], refs[chunks : chunks + 7]
    wide, padded, mask_pad = refs[-3:]
    x_own, normed_ref, normed2_ref, middle_ref, sums, projected_ref, attended_ref = outs
    own_rows(images, s_ref[0], spread(x_ref, wide, count), x_own, padded)
    x_own.send()
    stream = padded[...]
    normal, _ = normalize(stream)
    normed = (normal * norms_ref[0:1, :] + norms_ref[1:2, :]).astype(BF16)
    normed_ref[...] = normed
    normed_ref.send()
    masks = key_masks(images, s_ref[0], mask_ref, mask_pad)
    weight, bias, out_weight = chunk_weights(packs, width)
    projected, attended = attend(
        images, heads, width, chunks, normed, weight, bias, masks, projected_ref
    )
    attended_ref[...] = attended
    attended_ref.send()
    branch = nn(attended, out_weight) + norms_ref[4:5, :]
    middle = stream + branch
    normal, _ = normalize(middle)
    normed2_ref[...] = (normal * norms_ref[2:3, :] + norms_ref[3:4, :]).astype(BF16)
    normed2_ref.send()
    middle_ref[...] = middle.astype(BF16)
    middle_ref.send()
    valid = valid_column(images, masks)
    sums[...] = jnp.concatenate(
        [
            jnp.sum(middle * middle * valid, axis=0, keepdims=True),
            jnp.sum(branch * branch * valid, axis=0, keepdims=True),
            jnp.broadcast_to(jnp.sum(valid, axis=0, keepdims=True), (1, D)),
            jnp.zeros((5, D), F32),
        ],
        axis=0,
    )


def as_lines(rows):
    return jnp.concatenate([rows[:, k * LANES : (k + 1) * LANES] for k in range(D // LANES)], axis=0)


def as_rows(lines):
    count = lines.shape[0] // (D // LANES)
    return jnp.concatenate(
        [lines[k * count : (k + 1) * count] for k in range(D // LANES)], axis=1
    )


def attend_pull(images, heads, width, chunks, projected_ref, d_attended, masks):
    parts = []
    for image in range(images):
        span = slice(image * PAD, (image + 1) * PAD)
        key_mask = masks[image : image + 1, :PAD]
        line = []
        for chunk in range(chunks):
            queries, key_rows, values = (
                projected_ref[span, (3 * chunk + part) * width : (3 * chunk + part + 1) * width]
                for part in range(3)
            )
            d_mixed = d_attended[span, chunk * width : (chunk + 1) * width]
            own = by_head(queries, heads)
            d_own = by_head(d_mixed, heads)
            probabilities = probabilities_of(own, key_rows, key_mask)
            d_probs = nt(d_own, values)
            row_dots = jnp.sum(d_probs * probabilities, axis=-1, keepdims=True)
            d_scores = probabilities * (d_probs - row_dots)
            d_scores = jnp.where(key_mask > 0, d_scores, 0.0).astype(BF16)
            d_values = tn(probabilities.astype(BF16), d_own)
            d_queries = own_lanes(nn(d_scores, key_rows), heads)
            d_keys = tn(d_scores, own)
            line += [d_queries * HD ** (-0.5), d_keys * HD ** (-0.5), d_values]
        parts.append(jnp.concatenate(line, axis=1).astype(BF16))
    return jnp.concatenate(parts, axis=0)


def heads_pull(
    dims, s_ref, normed, projected_ref, attended_ref, d_branch, packs, masks, router_ref, grads, biases
):
    images, heads, width, chunks, start, groups = dims
    weight, _, out_weight = chunk_weights(packs, width)
    d_attended = nt(d_branch, out_weight).astype(BF16)
    d_project = attend_pull(images, heads, width, chunks, projected_ref, d_attended, masks)
    grad = tn(normed, d_project)
    out_grad = tn(attended_ref[...], d_branch)
    for chunk in range(chunks):
        for part in range(3):
            at = (3 * chunk + part) * width
            grads[chunk][part * D : (part + 1) * D, :] = grad[:, at : at + width].astype(BF16)
        for block in range(D // width):
            at = 3 * D + block * width
            grads[chunk][at : at + width, :] = out_grad[
                chunk * width : (chunk + 1) * width, block * width : (block + 1) * width
            ].astype(BF16)
        per = EXPERTS // groups
        owner = jnp.bitwise_xor(s_ref[0], start + chunk)
        router = router_ref[0:per, :]
        for g in range(1, groups):
            router = jnp.where(owner == g, router_ref[g * per : (g + 1) * per, :], router)
        router = as_lines(router)
        grads[chunk][4 * D : 4 * D + router.shape[0], :] = router.astype(BF16)
        rest = grads[chunk].shape[0] - 4 * D - router.shape[0]
        if rest:
            grads[chunk][4 * D + router.shape[0] :, :] = jnp.zeros((rest, width), BF16)
    biases[...] = jnp.broadcast_to(
        jnp.sum(d_project.astype(F32), axis=0, keepdims=True), biases.shape
    )
    return nt(d_project, weight)


def middle_pull_kernel(
    dims, s_ref, cot_ref, part_ref, near_ref, top_ref, rest_ref, middle_ref, norms_ref, normed_ref, mask_ref,
    projected_ref, attended_ref, router_ref, *refs,
):
    images, chunks = dims[0], dims[3]
    packs, outs, mask_pad = refs[:chunks], refs[chunks:-1], refs[-1]
    d_low, sums, d_branch_ref, biases = outs[:4]
    tokens = images * PAD
    normal, inv_std = normalize(middle_ref[...].astype(F32))
    d_normed2 = part_ref[...][:tokens].astype(F32) + near_ref[...][:tokens].astype(F32)
    d_normed2 = d_normed2 + jnp.concatenate([top_ref[...], rest_ref[...]], axis=0).astype(F32)
    d_middle = cot_ref[...].astype(F32) + norm_pull(d_normed2, normal, inv_std, norms_ref[2:3, :])
    d_branch = d_middle.astype(BF16)
    d_branch_ref[...] = d_branch
    sums[...] = jnp.concatenate(
        [
            jnp.sum(d_normed2 * normal, axis=0, keepdims=True),
            jnp.sum(d_normed2, axis=0, keepdims=True),
            jnp.sum(d_branch.astype(F32), axis=0, keepdims=True),
            jnp.zeros((5, D), F32),
        ],
        axis=0,
    )
    masks = key_masks(images, s_ref[0], mask_ref, mask_pad)
    d_low[...] = heads_pull(
        dims, s_ref, normed_ref[...], projected_ref, attended_ref, d_branch, packs, masks, router_ref,
        outs[4:], biases,
    ).astype(BF16)


def input_pull_kernel(
    dims, s_ref, x_ref, d_normed_ref, d_branch_ref, norms_ref, normed_ref, mask_ref,
    projected_ref, attended_ref, router_ref, *refs,
):
    images, chunks = dims[0], dims[3]
    packs, outs, mask_pad = refs[:chunks], refs[chunks:-1], refs[-1]
    d_inputs_ref, sums, biases = outs[:3]
    masks = key_masks(images, s_ref[0], mask_ref, mask_pad)
    d_normed = d_normed_ref[...].astype(F32) + heads_pull(
        dims, s_ref, normed_ref[...], projected_ref, attended_ref, d_branch_ref[...], packs, masks,
        router_ref, outs[3:], biases,
    )
    normal, inv_std = normalize(x_ref[...].astype(F32))
    d_inputs = d_branch_ref[...].astype(F32) + norm_pull(d_normed, normal, inv_std, norms_ref[0:1, :])
    d_inputs_ref[...] = d_inputs.astype(BF16)
    sums[...] = jnp.concatenate(
        [
            jnp.sum(d_normed * normal, axis=0, keepdims=True),
            jnp.sum(d_normed, axis=0, keepdims=True),
            jnp.sum(d_inputs * d_inputs * valid_column(images, masks), axis=0, keepdims=True),
            jnp.zeros((5, D), F32),
        ],
        axis=0,
    )


def expert_kernel(dims, s_ref, rows_in, *refs):
    chunks, pieces, hidden_width, width = dims
    ups_in, refs = refs[: chunks - 1], refs[chunks - 1 :]
    biases, refs = refs[:pieces], refs[pieces:]
    half = chunks // 2
    router_ref, back_bias_ref, w_in, w_back, *blocks = refs[: 3 + pieces]
    hidden_out, d_pre_out, d_results, d_rows_out, mixed_out, router_grad, back_bias_out = refs[
        3 + pieces : 10 + pieces
    ]
    (
        ups_wide, marks, in_weight, back_weight, in_bias, results, d_rows, sems
    ) = refs[10 + pieces :]
    piece = pl.program_id(0)

    def weight_copies_of(k):
        slot = k % 2
        if k == 0:
            sources = w_in.at[s_ref[5]], w_back.at[s_ref[5]]
        else:
            block = blocks[k - 1]
            sources = block.at[pl.ds(0, D)], block.at[pl.ds(D, hidden_width)]
        return [
            pltpu.make_async_copy(sources[0], in_weight.at[slot], sems.at[0, slot]),
            pltpu.make_async_copy(sources[1], back_weight.at[slot], sems.at[1, slot]),
        ]

    def start(k):
        for copy in weight_copies_of(k):
            copy.start()

    expert, first = s_ref[1], s_ref[2]
    rows = rows_in[...]
    label = lax.broadcasted_iota(jnp.int32, (1, EXPERTS), 1)
    mine = label == expert

    @pl.when(piece == 0)
    def _():
        start(0)
        for chunk in range(chunks):
            at = pl.multiple_of(jnp.bitwise_xor(s_ref[3], chunk) * CAP, 8)
            if chunk == half - 1:
                came = ups_in[-1][CAP:, :]
            else:
                came = ups_in[chunk if chunk < half else chunk - 1][0:CAP, :]
            ups_wide[pl.ds(at, CAP), :] = came.astype(F32)
        lines = hidden_width // width
        for k in range(pieces):
            block = biases[k][...].astype(F32)
            bias_rows = block[0:lines]
            for e in range(1, block.shape[0] // lines):
                here = block[e * lines : (e + 1) * lines]
                bias_rows = jnp.where(s_ref[0] == e, here, bias_rows)
            for line in range(lines):
                in_bias[k : k + 1, line * width : (line + 1) * width] = bias_rows[line : line + 1]
        other = ups_wide[:, D : D + 1]
        logits = nt(rows, router_ref[...])
        others = label.astype(F32) == other
        own_logit = jnp.sum(jnp.where(mine, logits, 0.0), axis=1, keepdims=True)
        other_logit = jnp.sum(jnp.where(others, logits, 0.0), axis=1, keepdims=True)
        peak = jnp.maximum(own_logit, other_logit)
        own_exp, other_exp = jnp.exp(own_logit - peak), jnp.exp(other_logit - peak)
        gate = own_exp / (own_exp + other_exp)
        other_gate = other_exp / (own_exp + other_exp)
        lane = lax.broadcasted_iota(jnp.int32, (1, LANES), 1)
        marks[...] = jnp.where(lane == 0, gate, other_gate)
        d_results[...] = (gate * ups_wide[:, :D]).astype(BF16)
        results[...] = jnp.zeros_like(results)
        d_rows[...] = jnp.zeros_like(d_rows)

    for k in range(pieces):
        @pl.when(piece == k)
        def _():
            for copy in weight_copies_of(k):
                copy.wait()
            if k + 1 < pieces:
                start(k + 1)

    slot = lax.rem(piece, 2)
    in_now, back_now = in_weight[slot], back_weight[slot]
    pre_act = nn(rows, in_now) + in_bias[pl.ds(piece, 1), :]
    cdf = 0.5 * (1.0 + lax.erf(pre_act * (0.5**0.5)))
    hidden = (pre_act * cdf).astype(BF16)
    hidden_out[0] = hidden
    results[...] += nn(hidden, back_now)
    slope = cdf + pre_act * jnp.exp(-0.5 * pre_act * pre_act) * 0.3989422804014327
    d_pre = (slope * nt(d_results[...], back_now)).astype(BF16)
    d_pre_out[0] = d_pre
    d_rows[...] += nt(d_pre, in_now)

    @pl.when(piece == pieces - 1)
    def _():
        gate, other_gate = marks[:, 0:1], marks[:, 1:2]
        others = label.astype(F32) == ups_wide[:, D : D + 1]
        bias = jnp.where(first > 0, 1.0, 0.0) * back_bias_ref[...].astype(F32)
        pick = (lax.broadcasted_iota(jnp.int32, (EXPERTS, 1), 0) == expert).astype(F32)
        total = results[...] + jnp.sum(pick * bias, axis=0, keepdims=True)
        d_gate = jnp.sum(ups_wide[:, :D] * total, axis=1, keepdims=True)
        moved = gate * other_gate * d_gate
        d_logits = jnp.where(mine, moved, jnp.where(others, -moved, 0.0)).astype(BF16)
        router_grad[...] = tn(d_logits, rows)
        back_bias_out[...] = jnp.broadcast_to(
            jnp.sum(d_results[...].astype(F32), axis=0, keepdims=True), back_bias_out.shape
        )
        d_rows_out[...] = (d_rows[...] + nn(d_logits, router_ref[...])).astype(BF16)
        mixed_out[...] = (gate * total).astype(BF16)


def expert_grads_kernel(pieces, cuts, s_ref, rows_ref, d_ref, hiddens, d_pres, *refs):
    grads, sums = refs[:-1], refs[-1]
    hidden_width = hiddens.shape[2]
    sums[...] = jnp.zeros_like(sums)
    rows, d_results = rows_ref[...], d_ref[...]
    for index, piece in enumerate(pieces):
        d_pre = d_pres[piece]
        in_grad = tn(rows, d_pre)
        back_grad = tn(hiddens[piece], d_results)
        bias_grad = jnp.sum(d_pre.astype(F32), axis=0, keepdims=True)
        sums[1:2, :] += jnp.sum(in_grad * in_grad)
        sums[2:3, :] += jnp.sum(bias_grad * bias_grad)
        sums[3:4, :] += jnp.sum(back_grad * back_grad)
        parts = (in_grad, jnp.broadcast_to(bias_grad, (16, hidden_width)), back_grad)
        at = 0
        for part in parts:
            done = 0
            while done < part.shape[0]:
                place, start = 0, at
                while start >= cuts[place]:
                    start -= cuts[place]
                    place += 1
                size = min(part.shape[0] - done, cuts[place] - start)
                grads[index * len(cuts) + place][start : start + size, :] = part[
                    done : done + size
                ].astype(BF16)
                done += size
                at += size


def mixture_kernel(s_ref, middle_ref, part_ref, near_ref, out_ref):
    tokens = middle_ref.shape[0]
    total = part_ref[...].astype(F32) + near_ref[...].astype(F32)
    out_ref[0:tokens, :] = (total[0:tokens] + middle_ref[...].astype(F32)).astype(BF16)
    out_ref[tokens:, :] = total[tokens:].astype(BF16)


def output_kernel(images, groups, s_ref, middle_ref, part_ref, mask_ref, *refs):
    fars, (out_ref, sums, mask_pad) = refs[: groups // 2 - 1], refs[groups // 2 - 1 :]
    tokens = images * PAD
    for r in range(0, groups, 2):
        total = part_ref[r // 2 * tokens : (r // 2 + 1) * tokens, :].astype(F32)
        for far, ref in enumerate(fars, 1):
            at = ((r // 2) ^ far) * tokens
            total = total + ref[at : at + tokens, :].astype(F32)
        out_ref[r // 2 * tokens : (r // 2 + 1) * tokens, :] = total.astype(BF16)
        if r == 0:
            output = total
    mixture = output - middle_ref[...].astype(F32)
    valid = valid_column(images, key_masks(images, s_ref[0], mask_ref, mask_pad))
    sums[...] = jnp.concatenate(
        [
            jnp.sum(mixture * mixture * valid, axis=0, keepdims=True),
            jnp.sum(output * output * valid, axis=0, keepdims=True),
            jnp.zeros((6, D), F32),
        ],
        axis=0,
    )


def place_tokens_kernel(count, images, places, s_ref, *refs):
    out, wide = refs[-2:]
    for group, (index, place) in enumerate(places):
        for image in range(images):
            start = (place * images + image) * PAD
            rows = refs[index][start : start + PAD, :].astype(F32)[:SEQ]
            at = jnp.bitwise_xor(s_ref[0], group) * images + image
            for k in range(D // LANES):
                wide[k, pl.ds(at, SEQ, stride=count), :] = rows[:, k * LANES : (k + 1) * LANES]
    for k in range(D // LANES):
        out[:, k * LANES : (k + 1) * LANES] = wide[k]


def place_experts_kernel(counts, first_row, biased, s_ref, *refs):
    ins, outs = refs[: sum(counts)], refs[sum(counts) :]
    height = outs[0].shape[1]
    at = 0
    for group, count in enumerate(counts):
        parts, at = ins[at : at + count], at + count

        @pl.when(pl.program_id(0) == group)
        def _():
            row = 0
            for part in parts:
                begin, end = max(first_row, row), min(first_row + height, row + part.shape[0])
                if begin < end:
                    outs[0][0, begin - first_row : end - first_row, :] = part[
                        begin - row : end - row, :
                    ].astype(F32)
                row += part.shape[0]
            if biased:
                bias = parts[0][height : height + 16, :].astype(F32)[0:1, :]
                outs[1][pl.ds(jnp.bitwise_xor(s_ref[0], group), 1), :] = bias


def split_kernel(chunks, s_ref, part_ref, near_ref, far_ref, out_ref):
    total = part_ref[...].astype(F32) + near_ref[...].astype(F32) + far_ref[...].astype(F32)
    share = total.shape[0] // chunks
    for chunk in range(chunks):
        out_ref[chunk] = total[chunk * share : (chunk + 1) * share].astype(BF16)


def join_kernel(dims, s_ref, pieces_ref, *refs):
    chunks, groups, half, width, small = dims
    norm1, norm2, forward, outputs, expert, back_bias, near_bias, far_bias = refs[:8]
    message, lines = refs[8:]
    total = pieces_ref[0].astype(F32)
    for chunk in range(1, chunks):
        total += pieces_ref[chunk].astype(F32)
    share = total.shape[0]
    row = lax.broadcasted_iota(jnp.int32, (share, 1), 0) + s_ref[3] * share
    squares = total * total
    lines[...] = jnp.zeros_like(lines)
    at = 0
    for source, index in ((norm1, 0), (norm1, 1), (norm2, 0), (norm2, 1), (norm2, 2)):
        lines[at : at + D // LANES, :] = as_lines(source[index : index + 1, :])
        at += D // LANES
    for part in (0, 2):
        for group in range(groups):
            biases, chunk = (near_bias, group) if group < half else (far_bias, group - half)
            line = biases[0:1, (3 * chunk + part) * width : (3 * chunk + part) * width + LANES]
            lines[pl.ds(at + jnp.bitwise_xor(s_ref[0], group), 1), :] = line
        at += groups
    lane = lax.broadcasted_iota(jnp.int32, (1, LANES), 1)
    terms = [
        jnp.sum(forward[0:1, :]),
        jnp.sum(forward[1:2, :]),
        jnp.sum(outputs[0:1, :]),
        jnp.sum(outputs[1:2, :]),
        jnp.sum(norm1[2:3, :]),
        jnp.sum(forward[2:3, :]) * (1.0 / D),
        jnp.sum(jnp.where(row < 3 * D, squares, 0.0)),
        jnp.sum(jnp.where((row >= 3 * D) & (row < 4 * D), squares, 0.0)),
        expert[1:2, 0:1],
        expert[2:3, 0:1],
        expert[3:4, 0:1],
    ]
    scalars = jnp.zeros((1, LANES), F32)
    for index, term in enumerate(terms):
        scalars = jnp.where(lane == index, term, scalars)
    lines[at : at + 1, :] = scalars
    lines[small - 8 : small - 8 + D // LANES, :] = as_lines(back_bias[0:1, :])
    values = lines[...]
    high = values.astype(BF16)
    low = (values - high.astype(F32)).astype(BF16)
    for chunk in range(chunks):
        message[chunk, 0:share, :] = total.astype(BF16)
        message[chunk, share : share + small, :] = high
        message[chunk, share + small :, :] = low


def spread_kernel(dims, s_ref, messages, qkv_out, out_out, sums, total):
    chunks, groups, width, small = dims
    share = messages.shape[1] - 2 * small
    summed = jnp.zeros((small, LANES), F32)
    at = small - 8
    for chunk in range(chunks):
        total[chunk * share : (chunk + 1) * share, :] = messages[chunk, 0:share, :].astype(F32)
        lines = messages[chunk, share : share + small, :].astype(F32) + messages[
            chunk, share + small :, :
        ].astype(F32)
        summed += lines
        sums[at : at + D // LANES, :] = lines[small - 8 : small - 8 + D // LANES]
        at += D // LANES
    sums[0 : small - 8, :] = summed[0 : small - 8]
    per = EXPERTS // groups * (D // LANES)
    sums[at : at + per, :] = total[4 * D : 4 * D + per, :]
    qkv_out[...] = total[0 : 3 * D, :]
    for block in range(D // width):
        out_out[:, block * width : (block + 1) * width] = total[
            3 * D + block * width : 3 * D + (block + 1) * width, :
        ]


def finish_kernel(dims, s_ref, mine_ref, came_ref, *refs):
    chunks, groups, half, small, shared = dims
    gain1, shift1, gain2, shift2, out_bias, bias_out, router_out, back_out, norms_out, rms_out = refs
    per = D // LANES
    top = small - 8
    summed = mine_ref[0:top, :] + came_ref[0:top, :]
    squares = []
    for index, out in enumerate((gain1, shift1, gain2, shift2, out_bias)):
        block = summed[index * per : (index + 1) * per]
        squares.append(jnp.sum(block * block))
        out[...] = as_rows(block)
    at = 5 * per
    biases = summed[at : at + 2 * groups]
    place = lax.broadcasted_iota(jnp.int32, (groups, 1), 0) == s_ref[0]
    for part in range(2):
        lines = biases[part * groups : (part + 1) * groups]
        bias_out[part : part + 1, :] = jnp.sum(
            jnp.where(place, lines, 0.0), axis=0, keepdims=True
        )
    scalars = summed[at + 2 * groups : at + 2 * groups + 1]
    lane = lax.broadcasted_iota(jnp.int32, (1, LANES), 1)

    def scalar(index):
        return jnp.sum(jnp.where(lane == index, scalars, 0.0))

    share = EXPERTS // groups
    size = chunks * per + share * per
    for group in range(groups):
        source = mine_ref if group < half else came_ref
        start = top + (group if group < half else group - half) * size
        owner = jnp.bitwise_xor(s_ref[0], group)
        lane_expert = owner if shared else 0
        for chunk in range(chunks):
            line = as_rows(source[start + chunk * per : start + (chunk + 1) * per, :])
            back_out[pl.ds(chunk * s_ref[4] + lane_expert, 1), :] = line
        start += chunks * per
        router_rows = as_rows(source[start : start + share * per, :])
        for g in range(groups):
            @pl.when(owner == g)
            def _():
                router_out[g * share : (g + 1) * share, :] = router_rows
    router, back_bias = router_out[...], back_out[...]
    ordered = [
        squares[0], squares[1], scalar(6), jnp.sum(biases * biases), scalar(7), squares[4],
        squares[2], squares[3], jnp.sum(router * router), scalar(8), scalar(9), scalar(10),
        jnp.sum(back_bias * back_bias),
    ]
    norms = jnp.zeros((1, LANES), F32)
    for index, value in enumerate(ordered):
        norms = jnp.where(lane == index, value, norms)
    norms_out[...] = jnp.sqrt(norms)
    rms_out[...] = jnp.sqrt(scalars / (scalar(5) * D))


def shards(
    inputs, valid_mask, expert_ids, slot_ids, norm1_gain, norm1_bias, w_qkv, b_qv, w_out, b_out,
    norm2_gain, norm2_bias, w_router, w_in, b_in, w_back, b_back, cotangent, dp_size, tensor_size,
):
    count = inputs.shape[0]
    groups = tensor_size
    images = count // groups
    local_width = w_qkv.shape[2]
    heads = local_width // HD
    width = -(-local_width // LANES) * LANES
    local_experts, _, hidden_width = w_in.shape
    shared = local_experts == groups == 4
    pieces = groups if shared else 1
    chunks = dp_size
    rows = chunks * CAP
    own_tokens = images * PAD
    half = groups // 2
    data_at = lax.axis_index("dp").astype(jnp.int32)
    head_at = lax.axis_index("tensor").astype(jnp.int32)
    lane_expert = head_at if shared else jnp.int32(0)
    expert_at = data_at * local_experts + lane_expert
    first = jnp.int32(1) if shared else (head_at == 0).astype(jnp.int32)
    scalars = jnp.stack(
        [head_at, expert_at, first, data_at, jnp.int32(local_experts), lane_expert]
    )
    x_lines = jnp.transpose(inputs, (1, 0, 2)).reshape(SEQ * count, D)
    cot_lines = jnp.transpose(cotangent, (1, 0, 2)).reshape(SEQ * count, D)
    ids = jnp.transpose(expert_ids, (0, 2, 1))
    slots = jnp.transpose(slot_ids, (0, 2, 1))
    norms = jnp.stack([norm1_gain, norm1_bias, norm2_gain, norm2_bias, b_out]).astype(F32)
    router = jnp.transpose(w_router)
    last = [None]

    def call(kernel, ins, outs, **options):
        at = scalars if last[0] is None else after(scalars, last[0])
        got = run(kernel, at, ins, outs, **options)
        last[0] = got[0]
        return got

    def over(axis, size, value, by, *others):
        return swap(after(value, *others) if others else value, axis, size, by)

    def core(value, *others):
        return over("tensor", groups, value, 1, *others)

    def gather(value):
        parts = [value] + [None] * (groups - 1)
        for r in range(2, groups, 2):
            parts[r] = over("tensor", groups, value, r)
        for r in range(1, groups, 2):
            parts[r] = core(parts[r - 1])
        return parts

    def exchange(value, *others):
        value = after(value, *others) if others else value
        return lax.all_to_all(value.reshape(chunks, CAP, -1), "dp", 0, 0).reshape(rows, -1)

    fill = width - local_width
    qkv = jnp.pad(jnp.transpose(w_qkv, (1, 0, 2)), [(0, 0), (0, 0), (0, fill)])
    qkv = qkv.reshape(3 * D, width)
    out_rows = jnp.pad(w_out, [(0, fill), (0, 0)])
    qv_bias = jnp.pad(b_qv, [(0, 0), (0, fill)])
    bias_at = 4 * D + 16
    bias_lines = -(-(local_experts * hidden_width // width) // 16) * 16
    pack = call(
        functools.partial(pack_kernel, width),
        [qkv, out_rows, qv_bias, b_in], [((bias_at + bias_lines, width), BF16)], mib=58,
    )[0]
    packs = [pack, core(pack)] + [None] * (groups - 2)
    for r in range(2, groups, 2):
        packs[r] = over("tensor", groups, pack, r)

    block = D + hidden_width
    tall = D // LANES, SEQ * count, LANES
    got = call(
        functools.partial(start_kernel, (count, images, chunks, shared)),
        [ids, slots, cot_lines] + ([w_in, w_back] if shared else []),
        [((own_tokens, D), BF16)] + [((CAP, D + LANES), BF16)] * (chunks // 2)
        + [((rows // 2, D + LANES), BF16)]
        + ([((block, D), BF16)] * (pieces - 1) if shared else []),
        left=(3, 4), mib=58,
        scratch=[
            pltpu.VMEM(tall, F32), pltpu.VMEM((own_tokens, D), F32),
            pltpu.VMEM((rows, D + LANES), F32), pltpu.VMEM((rows, D + LANES), F32),
            pltpu.SemaphoreType.DMA((6,)),
        ],
    )
    cot_own, ups, up_far = got[0], got[1 : 1 + chunks // 2], got[1 + chunks // 2]
    up_far = over("dp", chunks, up_far, chunks // 2)
    if shared:
        weights = [None, got[-3], over("tensor", groups, got[-2], 2), got[-1]]
    for r in range(2, groups, 2):
        packs[r + 1] = core(packs[r], cot_own)

    mask_pad = pltpu.VMEM((8, WIDE), jnp.int32)
    x_own, normed1, normed2, middle, forward_sums, projected, attended = call(
        functools.partial(heads_kernel, count, images, heads, width, groups),
        [x_lines, norms, valid_mask, *packs],
        [((own_tokens, D), BF16)] * 4 + [((8, D), F32)]
        + [((own_tokens, groups * 3 * width), BF16), ((own_tokens, groups * width), BF16)],
        scratch=[pltpu.VMEM(tall, F32), pltpu.VMEM((own_tokens, D), F32), mask_pad], mib=MIB_HEADS,
        stream=True,
    )
    half_heads = {
        which: [
            pl.BlockSpec((own_tokens, half * size * width), lambda step, s, at=which: (0, at))
            for size in (3, 1)
        ]
        for which in (0, 1)
    }

    tokens = [normed2, core(normed2)] + [None] * (groups - 2)
    early = chunks // 2 - 1
    ups = list(ups)
    for r in range(1, early):
        ups[r] = over("dp", chunks, ups[r], r, normed2)
    for r in range(2, groups, 2):
        tokens[r] = over("tensor", groups, normed2, r)
    turn = [up_far, *ups[1:early]]
    if shared:
        turn.append(weights[2])
    for r in range(2, groups, 2):
        tokens[r + 1] = core(tokens[r], *turn)
    if shared:
        weights[3] = over("tensor", groups, weights[3], 3, tokens[2])
        weights[1] = core(weights[1], tokens[2])
    flat_pad = pltpu.VMEM((8, WIDE), jnp.int32)
    sent, *passed = call(
        functools.partial(dispatch_kernel, groups, images, chunks),
        [ids, slots, *tokens, up_far, ups[early]],
        [((rows, D), BF16)] + [((CAP, D + LANES), BF16)] * (early - 1)
        + [((2 * CAP, D + LANES), BF16)],
        scratch=[flat_pad],
    )
    dispatched = exchange(sent)
    passed = [over("dp", chunks, value, r) for r, value in enumerate(passed, 1)]
    ups = [*ups[:early], up_far, *passed]

    by_piece = pl.BlockSpec((1, rows, hidden_width), lambda step, s: (step, 0, 0))
    bias_spec = pl.BlockSpec((bias_lines, width), lambda step, s: (bias_at // bias_lines, 0))
    first_rows = pl.BlockSpec((CAP, D + LANES), lambda step, s: (0, 0))
    before = chunks
    hidden, d_pre, d_results, d_sent, mixed_sent, router_part, back_bias = call(
        functools.partial(expert_kernel, (chunks, pieces, hidden_width, width)),
        [dispatched, *ups, *packs[:pieces], router, b_back, w_in, w_back]
        + (weights[1:] if shared else []),
        [((pieces, rows, hidden_width), BF16)] * 2 + [((rows, D), BF16)] * 3
        + [((EXPERTS, D), F32), ((8, D), F32)],
        grid=(pieces,),
        in_specs={chunks // 2: first_rows, **{before + k: bias_spec for k in range(pieces)}},
        out_specs={0: by_piece, 1: by_piece},
        scratch=[
            pltpu.VMEM((rows, D + LANES), F32),
            pltpu.VMEM((rows, LANES), F32),
            pltpu.VMEM((2, D, hidden_width), BF16),
            pltpu.VMEM((2, hidden_width, D), BF16),
            pltpu.VMEM((8, hidden_width), F32),
            pltpu.VMEM((rows, D), F32),
            pltpu.VMEM((rows, D), F32),
            pltpu.SemaphoreType.DMA((2, 2)),
        ],
        left=range(before + pieces + 2, before + pieces + 4 + pieces), mib=61,
    )
    d_back = exchange(d_sent)
    tall_grad = D + 16 + hidden_width
    first_cut = -(-2 * tall_grad // 48) * 16
    plans = [((3,), (first_cut, tall_grad - first_cut)), ((2, 0, 1), (tall_grad,))]
    if not shared:
        plans = [((0,), (D + 16, hidden_width))]
    lane_counts = (D, D) if shared else (hidden_width, D)
    grads, expert_sums = {}, []
    for kept, cuts in plans:
        part = pl.BlockSpec(
            (1 if len(kept) == 1 else 3, rows, hidden_width),
            lambda step, s, at=kept[0] if len(kept) == 1 else 0: (at, 0, 0),
        )
        held = tuple(range(len(kept))) if len(kept) == 1 else kept
        *some, sums = call(
            functools.partial(expert_grads_kernel, held, cuts),
            [dispatched, d_results, hidden, d_pre],
            [((cut, wide), BF16) for cut, wide in zip(cuts, lane_counts)] * len(kept)
            + [((8, LANES), F32)],
            in_specs={2: part, 3: part}, mib=58,
        )
        for index, piece in enumerate(kept):
            grads[piece] = some[index * len(cuts) : (index + 1) * len(cuts)]
        expert_sums.append(sums)

    def combine(value):
        return call(
            functools.partial(combine_kernel, groups, images, chunks),
            [ids, slots, value],
            [((half * own_tokens, D), BF16)] * 2, scratch=[flat_pad],
        )

    def reduce_own(keep, send, size, *others):
        came = core(send)
        far = [None, None]
        for r in range(2, groups, 2):
            for part in range(2):
                start = r // 2 * size + part * (size // 2)
                span = slice(start, start + size // 2)
                out = (keep[span].astype(F32) + came[span].astype(F32)).astype(BF16)
                term = over("tensor", groups, out, r, *others)
                if far[part] is not None:
                    term = far[part].astype(F32) + term.astype(F32)
                far[part] = term
        return keep, came, far

    if shared:
        last_top = over("tensor", groups, grads[3][0], 2)
        d_back = after(d_back, last_top)
    d_keep, d_near, d_far = reduce_own(*combine(d_back), own_tokens)
    if shared:
        last_rest = over("tensor", groups, grads[3][1], 2, *d_far)
    mixed = exchange(mixed_sent, d_back)

    router_lines = EXPERTS // groups * (D // LANES)
    share = -(-(4 * D + router_lines) // (16 * chunks)) * 16

    def grads_out(parts):
        return [((8, parts * 3 * width), F32)] + [((chunks * share, width), BF16)] * parts

    first_half = pl.BlockSpec((own_tokens, D), lambda step, s: (0, 0))
    got = call(
        functools.partial(
            middle_pull_kernel, (images, heads, width, groups - half, half, groups)
        ),
        [cot_own, d_keep, d_near, *d_far, middle, norms, normed1, valid_mask, projected,
         attended, router_part, *packs[half:]],
        [((own_tokens, D), BF16), ((8, D), F32), ((own_tokens, D), BF16)]
        + grads_out(groups - half),
        scratch=[mask_pad], mib=MIB_PULL, in_specs={**dict(zip((9, 10), half_heads[1])), 1: first_half, 2: first_half},
    )
    d_low, norm2_sums, d_branch, far_bias = got[:4]
    far_grads = list(got[4:])

    def add_odd(grads):
        return (grads[0].astype(F32) + core(grads[1]).astype(F32)).astype(BF16)

    if shared:
        far_grads[1] = after(far_grads[1], last_rest)
    far = None
    for r in range(0, groups - half, 2):
        out = add_odd(far_grads[r : r + 2])
        d_low = after(d_low, out)
        term = over("tensor", groups, out, half + r)
        far = term if far is None else far.astype(F32) + term.astype(F32)
    got = call(
        functools.partial(input_pull_kernel, (images, heads, width, half, 0, groups)),
        [x_own, d_low, d_branch, norms, normed1, valid_mask, projected, attended,
         router_part, *packs[:half]],
        [((own_tokens, D), BF16), ((8, D), F32)] + grads_out(half),
        scratch=[mask_pad], mib=MIB_PULL, in_specs=dict(zip((6, 7), half_heads[0])),
    )
    d_own, norm1_sums, near_bias = got[:3]
    head_grads = list(got[3:])
    for r in range(2, half, 2):
        term = over("tensor", groups, add_odd(head_grads[r : r + 2]), r)
        far = far.astype(F32) + term.astype(F32)
    near = core(head_grads[1], far)
    split = call(
        functools.partial(split_kernel, chunks),
        [head_grads[0], near, far], [((chunks, share, width), BF16)],
    )[0]
    pieces_in = lax.all_to_all(split, "dp", 0, 0)
    mix_keep, mix_send = combine(mixed)
    mix_near = core(mix_send)

    mix = call(
        mixture_kernel, [middle, mix_keep, mix_near], [((half * own_tokens, D), BF16)]
    )[0]
    d_tokens = [d_own, core(d_own)] + [None] * (groups - 2)
    for r in range(2, groups, 2):
        d_tokens[r] = over("tensor", groups, d_own, r)
    mix = after(mix, d_tokens[2])
    mix_far = [over("tensor", groups, mix, r) for r in range(2, groups, 2)]
    output_own, output_sums = call(
        functools.partial(output_kernel, images, groups),
        [middle, mix, valid_mask, *mix_far],
        [((half * own_tokens, D), BF16), ((8, D), F32)], scratch=[mask_pad],
    )
    out_near = core(output_own)

    def place_tokens(parts, places):
        placed = call(
            functools.partial(place_tokens_kernel, count, images, places),
            parts, [((SEQ * count, D), F32)],
            scratch=[pltpu.VMEM(tall, F32)],
        )[0]
        return jnp.transpose(placed.reshape(SEQ, count, D), (1, 0, 2))

    def place_experts(came, first_row, shape, bias):
        spec = pl.BlockSpec((1, *shape), lambda step, s: (jnp.bitwise_xor(s[0], step), 0, 0))
        counts = tuple(len(parts) for parts in came)
        return call(
            functools.partial(place_experts_kernel, counts, first_row, bool(bias)),
            [a for parts in came for a in parts],
            [((local_experts, *shape), F32)] + bias, grid=(groups,), out_specs={0: spec},
        )

    small = -(-(5 * D // LANES + 2 * groups + 1) // 8) * 8 + 8
    small = -(-small // 16) * 16
    message = call(
        functools.partial(join_kernel, (chunks, groups, half, width, small)),
        [pieces_in, norm1_sums, norm2_sums, forward_sums, output_sums,
         sum(expert_sums), back_bias, near_bias, far_bias],
        [((chunks, share + 2 * small, width), BF16)], scratch=[pltpu.VMEM((small, LANES), F32)],
        mib=58,
    )[0]
    messages = lax.all_to_all(message, "dp", 0, 0)
    for r in range(2, groups, 2):
        d_tokens[r + 1] = core(d_tokens[r], message)
    d_inputs = place_tokens(d_tokens, [(r, 0) for r in range(groups)])
    output = place_tokens([output_own, out_near], [(r % 2, r // 2) for r in range(groups)])
    top = small - 8
    qkv_sum, out_sum, sums = call(
        functools.partial(spread_kernel, (chunks, groups, width, small)),
        [messages],
        [((3 * D, width), F32), ((width, D), F32),
         ((top + chunks * (D // LANES) + router_lines, LANES), F32)],
        scratch=[pltpu.VMEM((chunks * share, width), F32)],
    )
    by = 1
    while True:
        came = over("tensor", groups, sums, by)
        by *= 2
        if by == groups:
            break
        sums = jnp.concatenate([sums[:top] + came[:top], sums[top:], came[top:]], axis=0)

    if shared:
        arrived = [
            grads[0], [core(grads[1][0])], [over("tensor", groups, grads[2][0], 2, *mix_far)],
            [core(last_top), core(last_rest)],
        ]
        g_w_in, g_b_in = place_experts(
            arrived, 0, (D, hidden_width), [((local_experts, hidden_width), F32)]
        )
        (g_w_back,) = place_experts(arrived, D + 16, (hidden_width, D), [])
    else:
        g_w_in = grads[0][0][None, :D].astype(F32)
        g_w_back = grads[0][1][None].astype(F32)
        g_b_in = grads[0][0][D : D + 1].astype(F32)

    vector = [((1, D), F32)]
    (
        g_norm1_gain, g_norm1_bias, g_norm2_gain, g_norm2_bias, g_b_out, g_b_qv, router_grad,
        g_b_back, grad_norms, rms_values,
    ) = call(
        functools.partial(finish_kernel, (chunks, groups, half, small, shared)),
        [sums, came],
        vector * 5
        + [((2, LANES), F32), ((EXPERTS, D), F32), ((EXPERTS, D), F32)]
        + [((1, LANES), F32)] * 2,
    )
    g_w_qkv = jnp.transpose(qkv_sum.reshape(3, D, width), (1, 0, 2))[:, :, :local_width]
    return (
        output, d_inputs, g_norm1_gain[0], g_norm1_bias[0], g_w_qkv, g_b_qv[:, :local_width],
        out_sum[:local_width], g_b_out[0], g_norm2_gain[0], g_norm2_bias[0],
        jnp.transpose(router_grad), g_w_in, g_b_in, g_w_back, g_b_back,
        grad_norms[0, :13], rms_values[0, :5],
    )


def solution(mesh):
    placed = (
        P("dp", None, None),
        P("dp", None),
        P("dp", None, None),
        P("dp", None, None),
        P(),
        P(),
        P(None, None, "tensor"),
        P(None, "tensor"),
        P("tensor", None),
        P(),
        P(),
        P(),
        P(),
        P("dp", None, "tensor"),
        P("dp", "tensor"),
        P("dp", "tensor", None),
        P(),
        P("dp", None, None),
    )
    return jax.shard_map(
        functools.partial(shards, dp_size=mesh.shape["dp"], tensor_size=mesh.shape["tensor"]),
        mesh=mesh,
        in_specs=placed,
        out_specs=(
            P("dp", None, None),
            P("dp", None, None),
            P(),
            P(),
            P(None, None, "tensor"),
            P(None, "tensor"),
            P("tensor", None),
            P(),
            P(),
            P(),
            P(),
            P("dp", None, "tensor"),
            P("dp", "tensor"),
            P("dp", "tensor", None),
            P(),
            P(),
            P(),
        ),
        check_vma=False,
    )
```

```python
import functools

import jax
import jax.numpy as jnp
from jax import lax
from jax.experimental import pallas as pl
from jax.experimental.pallas import tpu as pltpu
from jax.sharding import PartitionSpec as P

D = 512
HD = 64
EXPERTS = 32
SEQ = 197
CAP = 104
PAD = 208
WIDE = 256
MIB_HEADS = 58
MIB_EXPERT = 58
MIB_GRADS = 58
MIB_PULL = 58
LANES = 128
F32 = jnp.float32
BF16 = jnp.bfloat16


def nn(a, b):
    return lax.dot_general(a, b, (((1,), (0,)), ((), ())), preferred_element_type=F32)


def nt(a, b):
    return lax.dot_general(a, b, (((1,), (1,)), ((), ())), preferred_element_type=F32)


def tn(a, b):
    return lax.dot_general(a, b, (((0,), (0,)), ((), ())), preferred_element_type=F32)


def swap(value, axis, size, by):
    return lax.ppermute(value, axis, [(at, at ^ by) for at in range(size)])


def after(value, *others):
    return lax.optimization_barrier((value, *others))[0]


class Held:
    def __init__(self, ref, copy):
        self.ref, self.copy, self.there = ref, copy, False
        self.shape, self.dtype = ref.shape, ref.dtype

    def __getitem__(self, index):
        if not self.there:
            self.copy.wait()
            self.there = True
        return self.ref[index]


class Sent:
    def __init__(self, ref, copy):
        self.ref, self.copy, self.left = ref, copy, False
        self.shape, self.dtype = ref.shape, ref.dtype

    def __getitem__(self, index):
        return self.ref[index]

    def __setitem__(self, index, value):
        self.ref[index] = value

    def send(self):
        if not self.left:
            self.copy.start()
            self.left = True


def streamed(kernel, ins, outs, scratch):
    shapes = [(a.shape, a.dtype) for a in ins] + list(outs)

    def body(s_ref, *refs):
        far, refs = refs[: len(shapes)], refs[len(shapes) :]
        near, refs, sems = refs[: len(shapes)], refs[len(shapes) : -1], refs[-1]
        held = []
        for i in range(len(ins)):
            copy = pltpu.make_async_copy(far[i], near[i], sems.at[i])
            copy.start()
            held.append(Held(near[i], copy))
        sent = [
            Sent(near[i], pltpu.make_async_copy(near[i], far[i], sems.at[i]))
            for i in range(len(ins), len(shapes))
        ]
        kernel(s_ref, *held, *sent, *refs)
        for value in held:
            if not value.there:
                value.copy.wait()
        for value in sent:
            value.send()
        for value in sent:
            value.copy.wait()

    buffers = [pltpu.VMEM(shape, dtype) for shape, dtype in shapes]
    return body, [*buffers, *scratch, pltpu.SemaphoreType.DMA((len(shapes),))]


def run(
    kernel, scalars, ins, outs, scratch=(), grid=(1,), in_specs=None, out_specs=None, mib=28, left=(),
    stream=False, aliases=None,
):
    in_specs, out_specs = in_specs or {}, out_specs or {}
    if stream:
        kernel, scratch = streamed(kernel, ins, outs, scratch)
        left = range(len(ins))
        out_specs = {i: pl.BlockSpec(memory_space=pl.ANY) for i in range(len(outs))}

    def whole(shape, stays=False):
        if stays:
            return pl.BlockSpec(memory_space=pl.ANY)
        return pl.BlockSpec(shape, lambda step, s, nd=len(shape): (0,) * nd)

    return pl.pallas_call(
        kernel,
        grid_spec=pltpu.PrefetchScalarGridSpec(
            num_scalar_prefetch=1,
            grid=grid,
            in_specs=[
                in_specs[i] if i in in_specs else whole(a.shape, i in left)
                for i, a in enumerate(ins)
            ],
            out_specs=[out_specs[i] if i in out_specs else whole(o[0]) for i, o in enumerate(outs)],
            scratch_shapes=list(scratch),
        ),
        out_shape=[jax.ShapeDtypeStruct(shape, dtype) for shape, dtype in outs],
        input_output_aliases={i + 1: o for i, o in (aliases or {}).items()},
        compiler_params=pltpu.CompilerParams(vmem_limit_bytes=mib * 2**20),
        cost_estimate=pl.CostEstimate(flops=0, bytes_accessed=0, transcendentals=0),
    )(scalars, *ins)


def route_rows(ids_ref, slots_ref, image):
    ids, slots = ids_ref[image], slots_ref[image]
    return jnp.where(slots < CAP, ids * CAP + slots, -1)


def block_start(s_ref, chunk):
    return (chunk * s_ref[4] + s_ref[5]) * CAP


def target_column(s_ref, chunks):
    rows = lax.broadcasted_iota(jnp.int32, (CAP, 1), 0)
    starts = [block_start(s_ref, chunk) for chunk in range(chunks)]
    return jnp.concatenate([rows + start for start in starts], axis=0)


def target_row(s_ref, chunks):
    lanes = lax.broadcasted_iota(jnp.int32, (1, chunks * CAP), 1)
    target = lanes
    for chunk in range(chunks):
        here = (lanes >= chunk * CAP) & (lanes < (chunk + 1) * CAP)
        target = jnp.where(here, lanes + (block_start(s_ref, chunk) - chunk * CAP), target)
    return target


def spread(source_ref, wide_ref, count):
    for k in range(D // LANES):
        wide_ref[k] = source_ref[:, k * LANES : (k + 1) * LANES].astype(F32)

    def image_rows(image):
        return jnp.concatenate(
            [wide_ref[k, pl.ds(image, SEQ, stride=count), :] for k in range(D // LANES)], axis=1
        )

    return image_rows


def own_rows(images, me, image_rows, out_ref, padded):
    padded[...] = jnp.zeros_like(padded)
    for image in range(images):
        padded[image * PAD : image * PAD + SEQ, :] = image_rows(me * images + image)
    out_ref[...] = padded[...].astype(BF16)


def pack_kernel(width, s_ref, qkv_ref, out_ref, bias_ref, in_bias_ref, pack):
    pack[0 : 3 * D, :] = qkv_ref[...]
    for block in range(D // width):
        at = 3 * D + block * width
        pack[at : at + width, :] = out_ref[:, block * width : (block + 1) * width]
    bias = bias_ref[...].astype(F32)
    experts, hidden = in_bias_ref.shape
    lines = in_bias_ref[...].astype(F32)
    lines = [
        lines[e : e + 1, k * width : (k + 1) * width]
        for e in range(experts)
        for k in range(hidden // width)
    ]
    fill = -len(lines) % 16
    if fill:
        lines.append(jnp.zeros((fill, width), F32))
    pack[4 * D :, :] = jnp.concatenate(
        [bias[0:1], bias[1:2], jnp.zeros((14, width), F32), *lines], axis=0
    ).astype(BF16)


def weight_copies(s_ref, w_in, w_back, blocks, sems):
    copies = []
    for index, (r, block) in enumerate(blocks):
        expert = jnp.bitwise_xor(s_ref[0], r)
        for side, (source, target) in enumerate(
            (
                (w_in.at[expert], block.at[pl.ds(0, D)]),
                (w_back.at[expert], block.at[pl.ds(D, w_back.shape[1])]),
            )
        ):
            copies.append(pltpu.make_async_copy(source, target, sems.at[2 * index + side]))
    return copies


def start_kernel(dims, s_ref, ids_ref, slots_ref, cot_ref, *refs):
    count, images, chunks, shared = dims
    copies = []
    if shared:
        w_in, w_back, *refs = refs
    own, *refs = refs
    near_outs, far_out, refs = refs[: chunks // 2], refs[chunks // 2], refs[chunks // 2 + 1 :]
    if shared:
        laid, refs = refs[:3], refs[3:]
    wide, padded, blocks, wholes, sems = refs
    if shared:
        copies = weight_copies(s_ref, w_in, w_back, list(enumerate(laid, 1)), sems)
    for copy in copies:
        copy.start()
    image_rows = spread(cot_ref, wide, count)
    target = target_column(s_ref, chunks)
    rows = chunks * CAP
    blocks[...] = jnp.zeros_like(blocks)

    def step(pair, carry):
        total = jnp.zeros((rows, D), F32)
        others = jnp.zeros((rows, SEQ), F32)
        for image in (2 * pair, 2 * pair + 1):
            flat = route_rows(ids_ref, slots_ref, image)
            ids = ids_ref[image].astype(F32)
            first = target == flat[0:1, :]
            second = target == flat[1:2, :]
            hit = (first | second).astype(F32).astype(BF16)
            total += nn(hit, image_rows(image).astype(BF16))
            others += jnp.where(first, ids[1:2, :], 0.0) + jnp.where(second, ids[0:1, :], 0.0)
        blocks[:, :D] += total
        blocks[:, D:] += jnp.broadcast_to(jnp.sum(others, axis=1, keepdims=True), (rows, LANES))
        return carry

    lax.fori_loop(0, count // 2, step, 0)
    for chunk in range(chunks):
        at = pl.multiple_of(jnp.bitwise_xor(s_ref[3], chunk) * CAP, 8)
        wholes[chunk * CAP : (chunk + 1) * CAP, :] = blocks[pl.ds(at, CAP), :]
    for chunk, near_out in enumerate(near_outs):
        near_out[...] = wholes[chunk * CAP : (chunk + 1) * CAP, :].astype(BF16)
    far_out[...] = wholes[rows // 2 :, :].astype(BF16)
    own_rows(images, s_ref[0], image_rows, own, padded)
    for copy in copies:
        copy.wait()


def padded_routes(ids_ref, slots_ref, image, flat_ref):
    flat_ref[...] = jnp.full(flat_ref.shape, -1, jnp.int32)
    flat_ref[0:2, 0:SEQ] = route_rows(ids_ref, slots_ref, image)
    return flat_ref[...]


def dispatch_kernel(groups, images, chunks, s_ref, ids_ref, slots_ref, *refs):
    tokens, (far, late, out, *passed, flat_ref) = refs[:groups], refs[groups:]
    for chunk, on in enumerate(passed, 1):
        on[0:CAP, :] = far[chunk * CAP : (chunk + 1) * CAP, :]
    passed[-1][CAP:, :] = late[...]
    me = s_ref[0]
    target = target_column(s_ref, chunks)
    total = jnp.zeros((chunks * CAP, D), F32)
    for group in range(groups):
        for image in range(images):
            at = jnp.bitwise_xor(me, group) * images + image
            flat = padded_routes(ids_ref, slots_ref, at, flat_ref)[:, :PAD]
            hit = (target == flat[0:1, :]) | (target == flat[1:2, :])
            total += nn(
                hit.astype(F32).astype(BF16), tokens[group][image * PAD : (image + 1) * PAD, :]
            )
    out[...] = total.astype(BF16)


def combine_kernel(groups, images, chunks, s_ref, ids_ref, slots_ref, rows_ref, *refs):
    outs, flat_ref = refs[:2], refs[2]
    me = s_ref[0]
    rows = rows_ref[...]
    target = target_row(s_ref, chunks)
    for group in range(groups):
        for image in range(images):
            at = jnp.bitwise_xor(me, group) * images + image
            flat = jnp.transpose(padded_routes(ids_ref, slots_ref, at, flat_ref))[:PAD, :]
            hit = (flat[:, 0:1] == target) | (flat[:, 1:2] == target)
            place = (group // 2 * images + image) * PAD
            outs[group % 2][place : place + PAD, :] = nn(
                hit.astype(F32).astype(BF16), rows
            ).astype(BF16)


def chunk_weights(packs, width):
    qkv = [p[part * D : (part + 1) * D, :] for p in packs for part in range(3)]
    biases = []
    for p in packs:
        lines = p[3 * D + D : 3 * D + D + 16, :].astype(F32)
        biases += [lines[0:1], jnp.zeros((1, width), F32), lines[1:2]]
    outs = [
        jnp.concatenate(
            [p[3 * D + b * width : 3 * D + (b + 1) * width, :] for b in range(D // width)], axis=1
        )
        for p in packs
    ]
    return (
        jnp.concatenate(qkv, axis=1),
        jnp.concatenate(biases, axis=1),
        jnp.concatenate(outs, axis=0),
    )


def normalize(values):
    average = jnp.mean(values, axis=-1, keepdims=True)
    centered = values - average
    inv_std = lax.rsqrt(jnp.mean(centered * centered, axis=-1, keepdims=True) + 1e-06)
    return centered * inv_std, inv_std


def norm_pull(upstream, normal, inv_std, gain):
    scaled = upstream * gain
    inner = jnp.mean(scaled * normal, axis=-1, keepdims=True)
    return inv_std * (scaled - jnp.mean(scaled, axis=-1, keepdims=True) - normal * inner)


def key_masks(images, me, mask_ref, pad_ref):
    pad_ref[...] = jnp.full(pad_ref.shape, -1, jnp.int32)
    for image in range(images):
        pad_ref[image : image + 1, 0:SEQ] = mask_ref[pl.ds(me * images + image, 1), :]
    return pad_ref[...]


def valid_column(images, masks):
    columns = jnp.transpose(jnp.maximum(masks, 0).astype(F32))
    return jnp.concatenate([columns[:PAD, i : i + 1] for i in range(images)], axis=0)


def probabilities_of(queries, key_rows, key_mask):
    shift = jnp.where(key_mask > 0, 0.0, jnp.where(key_mask < 0, -2e30, -1e30))
    scores = nt(queries * jnp.asarray(HD ** (-0.5), BF16), key_rows) + shift
    exps = jnp.exp(scores - jnp.max(scores, axis=-1, keepdims=True))
    return exps * (1.0 / jnp.sum(exps, axis=-1, keepdims=True))


def by_head(rows, heads):
    zeros = jnp.zeros_like(rows)
    width = rows.shape[1]
    return jnp.concatenate(
        [jnp.where(head_lanes(width, head), rows, zeros) for head in range(heads)], axis=0
    )


def own_lanes(stacked, heads):
    result = stacked[:PAD]
    for head in range(1, heads):
        lanes = head_lanes(stacked.shape[1], head)
        result = jnp.where(lanes, stacked[head * PAD : (head + 1) * PAD], result)
    return result


def head_lanes(width, head):
    lane = lax.broadcasted_iota(jnp.int32, (1, width), 1)
    return (lane >= head * HD) & (lane < (head + 1) * HD)


def attend(images, heads, width, chunks, normed, weight, bias, masks, projected_ref):
    projected = (nn(normed, weight) + bias).astype(BF16)
    projected_ref[...] = projected
    projected_ref.send()
    parts = []
    for image in range(images):
        key_mask = masks[image : image + 1, :PAD]
        line = []
        for chunk in range(chunks):
            queries, key_rows, values = (
                projected[
                    image * PAD : (image + 1) * PAD,
                    (3 * chunk + part) * width : (3 * chunk + part + 1) * width,
                ]
                for part in range(3)
            )
            own = by_head(queries, heads)
            probabilities = probabilities_of(own, key_rows, key_mask)
            mixed = own_lanes(nn(probabilities.astype(BF16), values), heads)
            line.append(mixed.astype(BF16))
        parts.append(jnp.concatenate(line, axis=1))
    return projected, jnp.concatenate(parts, axis=0)


def heads_kernel(count, images, heads, width, chunks, s_ref, x_ref, norms_ref, mask_ref, *refs):
    packs, outs = refs[:chunks], refs[chunks : chunks + 7]
    wide, padded, mask_pad = refs[-3:]
    x_own, normed_ref, normed2_ref, middle_ref, sums, projected_ref, attended_ref = outs
    own_rows(images, s_ref[0], spread(x_ref, wide, count), x_own, padded)
    x_own.send()
    stream = padded[...]
    normal, _ = normalize(stream)
    normed = (normal * norms_ref[0:1, :] + norms_ref[1:2, :]).astype(BF16)
    normed_ref[...] = normed
    normed_ref.send()
    masks = key_masks(images, s_ref[0], mask_ref, mask_pad)
    weight, bias, out_weight = chunk_weights(packs, width)
    projected, attended = attend(
        images, heads, width, chunks, normed, weight, bias, masks, projected_ref
    )
    attended_ref[...] = attended
    attended_ref.send()
    branch = nn(attended, out_weight) + norms_ref[4:5, :]
    middle = stream + branch
    normal, _ = normalize(middle)
    normed2_ref[...] = (normal * norms_ref[2:3, :] + norms_ref[3:4, :]).astype(BF16)
    normed2_ref.send()
    middle_ref[...] = middle.astype(BF16)
    middle_ref.send()
    valid = valid_column(images, masks)
    sums[...] = jnp.concatenate(
        [
            jnp.sum(middle * middle * valid, axis=0, keepdims=True),
            jnp.sum(branch * branch * valid, axis=0, keepdims=True),
            jnp.broadcast_to(jnp.sum(valid, axis=0, keepdims=True), (1, D)),
            jnp.zeros((5, D), F32),
        ],
        axis=0,
    )


def as_lines(rows):
    return jnp.concatenate([rows[:, k * LANES : (k + 1) * LANES] for k in range(D // LANES)], axis=0)


def as_rows(lines):
    count = lines.shape[0] // (D // LANES)
    return jnp.concatenate(
        [lines[k * count : (k + 1) * count] for k in range(D // LANES)], axis=1
    )


def attend_pull(images, heads, width, chunks, projected_ref, d_attended, masks):
    parts = []
    for image in range(images):
        span = slice(image * PAD, (image + 1) * PAD)
        key_mask = masks[image : image + 1, :PAD]
        line = []
        for chunk in range(chunks):
            queries, key_rows, values = (
                projected_ref[span, (3 * chunk + part) * width : (3 * chunk + part + 1) * width]
                for part in range(3)
            )
            d_mixed = d_attended[span, chunk * width : (chunk + 1) * width]
            own = by_head(queries, heads)
            d_own = by_head(d_mixed, heads)
            probabilities = probabilities_of(own, key_rows, key_mask)
            d_probs = nt(d_own, values)
            row_dots = jnp.sum(d_probs * probabilities, axis=-1, keepdims=True)
            d_scores = probabilities * (d_probs - row_dots)
            d_scores = jnp.where(key_mask > 0, d_scores, 0.0).astype(BF16)
            d_values = tn(probabilities.astype(BF16), d_own)
            d_queries = own_lanes(nn(d_scores, key_rows), heads)
            d_keys = tn(d_scores, own)
            line += [d_queries * HD ** (-0.5), d_keys * HD ** (-0.5), d_values]
        parts.append(jnp.concatenate(line, axis=1).astype(BF16))
    return jnp.concatenate(parts, axis=0)


def heads_pull(
    dims, s_ref, normed, projected_ref, attended_ref, d_branch, packs, masks, router_ref, grads, biases
):
    images, heads, width, chunks, start, groups = dims
    weight, _, out_weight = chunk_weights(packs, width)
    d_attended = nt(d_branch, out_weight).astype(BF16)
    d_project = attend_pull(images, heads, width, chunks, projected_ref, d_attended, masks)
    grad = tn(normed, d_project)
    out_grad = tn(attended_ref[...], d_branch)
    for chunk in range(chunks):
        for part in range(3):
            at = (3 * chunk + part) * width
            grads[chunk][part * D : (part + 1) * D, :] = grad[:, at : at + width].astype(BF16)
        for block in range(D // width):
            at = 3 * D + block * width
            grads[chunk][at : at + width, :] = out_grad[
                chunk * width : (chunk + 1) * width, block * width : (block + 1) * width
            ].astype(BF16)
        per = EXPERTS // groups
        owner = jnp.bitwise_xor(s_ref[0], start + chunk)
        router = router_ref[0:per, :]
        for g in range(1, groups):
            router = jnp.where(owner == g, router_ref[g * per : (g + 1) * per, :], router)
        router = as_lines(router)
        grads[chunk][4 * D : 4 * D + router.shape[0], :] = router.astype(BF16)
        rest = grads[chunk].shape[0] - 4 * D - router.shape[0]
        if rest:
            grads[chunk][4 * D + router.shape[0] :, :] = jnp.zeros((rest, width), BF16)
    biases[...] = jnp.broadcast_to(
        jnp.sum(d_project.astype(F32), axis=0, keepdims=True), biases.shape
    )
    return nt(d_project, weight)


def middle_pull_kernel(
    dims, s_ref, cot_ref, part_ref, near_ref, top_ref, rest_ref, middle_ref, norms_ref, normed_ref, mask_ref,
    projected_ref, attended_ref, router_ref, *refs,
):
    images, chunks = dims[0], dims[3]
    packs, outs, mask_pad = refs[:chunks], refs[chunks:-1], refs[-1]
    d_low, sums, d_branch_ref, biases = outs[:4]
    tokens = images * PAD
    normal, inv_std = normalize(middle_ref[...].astype(F32))
    d_normed2 = part_ref[...][:tokens].astype(F32) + near_ref[...][:tokens].astype(F32)
    d_normed2 = d_normed2 + jnp.concatenate([top_ref[...], rest_ref[...]], axis=0).astype(F32)
    d_middle = cot_ref[...].astype(F32) + norm_pull(d_normed2, normal, inv_std, norms_ref[2:3, :])
    d_branch = d_middle.astype(BF16)
    d_branch_ref[...] = d_branch
    sums[...] = jnp.concatenate(
        [
            jnp.sum(d_normed2 * normal, axis=0, keepdims=True),
            jnp.sum(d_normed2, axis=0, keepdims=True),
            jnp.sum(d_branch.astype(F32), axis=0, keepdims=True),
            jnp.zeros((5, D), F32),
        ],
        axis=0,
    )
    masks = key_masks(images, s_ref[0], mask_ref, mask_pad)
    d_low[...] = heads_pull(
        dims, s_ref, normed_ref[...], projected_ref, attended_ref, d_branch, packs, masks, router_ref,
        outs[4:], biases,
    ).astype(BF16)


def input_pull_kernel(
    dims, s_ref, x_ref, d_normed_ref, d_branch_ref, norms_ref, normed_ref, mask_ref,
    projected_ref, attended_ref, router_ref, *refs,
):
    images, chunks = dims[0], dims[3]
    packs, outs, mask_pad = refs[:chunks], refs[chunks:-1], refs[-1]
    d_inputs_ref, sums, biases = outs[:3]
    masks = key_masks(images, s_ref[0], mask_ref, mask_pad)
    d_normed = d_normed_ref[...].astype(F32) + heads_pull(
        dims, s_ref, normed_ref[...], projected_ref, attended_ref, d_branch_ref[...], packs, masks,
        router_ref, outs[3:], biases,
    )
    normal, inv_std = normalize(x_ref[...].astype(F32))
    d_inputs = d_branch_ref[...].astype(F32) + norm_pull(d_normed, normal, inv_std, norms_ref[0:1, :])
    d_inputs_ref[...] = d_inputs.astype(BF16)
    sums[...] = jnp.concatenate(
        [
            jnp.sum(d_normed * normal, axis=0, keepdims=True),
            jnp.sum(d_normed, axis=0, keepdims=True),
            jnp.sum(d_inputs * d_inputs * valid_column(images, masks), axis=0, keepdims=True),
            jnp.zeros((5, D), F32),
        ],
        axis=0,
    )


def expert_kernel(dims, s_ref, rows_in, *refs):
    chunks, pieces, hidden_width, width = dims
    ups_in, refs = refs[: chunks - 1], refs[chunks - 1 :]
    biases, refs = refs[:pieces], refs[pieces:]
    half = chunks // 2
    router_ref, back_bias_ref, w_in, w_back, *blocks = refs[: 3 + pieces]
    hidden_out, d_pre_out, d_results, d_rows_out, mixed_out, router_grad, back_bias_out = refs[
        3 + pieces : 10 + pieces
    ]
    (
        ups_wide, marks, in_weight, back_weight, in_bias, results, d_rows, sems
    ) = refs[10 + pieces :]
    piece = pl.program_id(0)

    def weight_copies_of(k):
        slot = k % 2
        if k == 0:
            sources = w_in.at[s_ref[5]], w_back.at[s_ref[5]]
        else:
            block = blocks[k - 1]
            sources = block.at[pl.ds(0, D)], block.at[pl.ds(D, hidden_width)]
        return [
            pltpu.make_async_copy(sources[0], in_weight.at[slot], sems.at[0, slot]),
            pltpu.make_async_copy(sources[1], back_weight.at[slot], sems.at[1, slot]),
        ]

    def start(k):
        for copy in weight_copies_of(k):
            copy.start()

    expert, first = s_ref[1], s_ref[2]
    rows = rows_in[...]
    label = lax.broadcasted_iota(jnp.int32, (1, EXPERTS), 1)
    mine = label == expert

    @pl.when(piece == 0)
    def _():
        start(0)
        for chunk in range(chunks):
            at = pl.multiple_of(jnp.bitwise_xor(s_ref[3], chunk) * CAP, 8)
            if chunk == half - 1:
                came = ups_in[-1][CAP:, :]
            else:
                came = ups_in[chunk if chunk < half else chunk - 1][0:CAP, :]
            ups_wide[pl.ds(at, CAP), :] = came.astype(F32)
        lines = hidden_width // width
        for k in range(pieces):
            block = biases[k][...].astype(F32)
            bias_rows = block[0:lines]
            for e in range(1, block.shape[0] // lines):
                here = block[e * lines : (e + 1) * lines]
                bias_rows = jnp.where(s_ref[5] == e, here, bias_rows)
            for line in range(lines):
                in_bias[k : k + 1, line * width : (line + 1) * width] = bias_rows[line : line + 1]
        other = ups_wide[:, D : D + 1]
        logits = nt(rows, router_ref[...])
        others = label.astype(F32) == other
        own_logit = jnp.sum(jnp.where(mine, logits, 0.0), axis=1, keepdims=True)
        other_logit = jnp.sum(jnp.where(others, logits, 0.0), axis=1, keepdims=True)
        peak = jnp.maximum(own_logit, other_logit)
        own_exp, other_exp = jnp.exp(own_logit - peak), jnp.exp(other_logit - peak)
        gate = own_exp / (own_exp + other_exp)
        other_gate = other_exp / (own_exp + other_exp)
        lane = lax.broadcasted_iota(jnp.int32, (1, LANES), 1)
        marks[...] = jnp.where(lane == 0, gate, other_gate)
        d_results[...] = (gate * ups_wide[:, :D]).astype(BF16)
        results[...] = jnp.zeros_like(results)
        d_rows[...] = jnp.zeros_like(d_rows)

    for k in range(pieces):
        @pl.when(piece == k)
        def _():
            for copy in weight_copies_of(k):
                copy.wait()
            if k + 1 < pieces:
                start(k + 1)

    slot = lax.rem(piece, 2)
    in_now, back_now = in_weight[slot], back_weight[slot]
    pre_act = nn(rows, in_now) + in_bias[pl.ds(piece, 1), :]
    cdf = 0.5 * (1.0 + lax.erf(pre_act * (0.5**0.5)))
    hidden = (pre_act * cdf).astype(BF16)
    hidden_out[0] = hidden
    results[...] += nn(hidden, back_now)
    slope = cdf + pre_act * jnp.exp(-0.5 * pre_act * pre_act) * 0.3989422804014327
    d_pre = (slope * nt(d_results[...], back_now)).astype(BF16)
    d_pre_out[0] = d_pre
    d_rows[...] += nt(d_pre, in_now)

    @pl.when(piece == pieces - 1)
    def _():
        gate, other_gate = marks[:, 0:1], marks[:, 1:2]
        others = label.astype(F32) == ups_wide[:, D : D + 1]
        bias = jnp.where(first > 0, 1.0, 0.0) * back_bias_ref[...].astype(F32)
        pick = (lax.broadcasted_iota(jnp.int32, (EXPERTS, 1), 0) == expert).astype(F32)
        total = results[...] + jnp.sum(pick * bias, axis=0, keepdims=True)
        d_gate = jnp.sum(ups_wide[:, :D] * total, axis=1, keepdims=True)
        moved = gate * other_gate * d_gate
        d_logits = jnp.where(mine, moved, jnp.where(others, -moved, 0.0)).astype(BF16)
        router_grad[...] = tn(d_logits, rows)
        back_bias_out[...] = jnp.broadcast_to(
            jnp.sum(d_results[...].astype(F32), axis=0, keepdims=True), back_bias_out.shape
        )
        d_rows_out[...] = (d_rows[...] + nn(d_logits, router_ref[...])).astype(BF16)
        mixed_out[...] = (gate * total).astype(BF16)


def expert_grads_kernel(pieces, cuts, s_ref, rows_ref, d_ref, hiddens, d_pres, *refs):
    grads, sums = refs[:-1], refs[-1]
    hidden_width = hiddens.shape[2]
    sums[...] = jnp.zeros_like(sums)
    rows, d_results = rows_ref[...], d_ref[...]
    for index, piece in enumerate(pieces):
        d_pre = d_pres[piece]
        in_grad = tn(rows, d_pre)
        back_grad = tn(hiddens[piece], d_results)
        bias_grad = jnp.sum(d_pre.astype(F32), axis=0, keepdims=True)
        sums[1:2, :] += jnp.sum(in_grad * in_grad)
        sums[2:3, :] += jnp.sum(bias_grad * bias_grad)
        sums[3:4, :] += jnp.sum(back_grad * back_grad)
        parts = (in_grad, jnp.broadcast_to(bias_grad, (16, hidden_width)), back_grad)
        at = 0
        for part in parts:
            done = 0
            while done < part.shape[0]:
                place, start = 0, at
                while start >= cuts[place]:
                    start -= cuts[place]
                    place += 1
                size = min(part.shape[0] - done, cuts[place] - start)
                grads[index * len(cuts) + place][start : start + size, :] = part[
                    done : done + size
                ].astype(BF16)
                done += size
                at += size


def mixture_kernel(s_ref, middle_ref, part_ref, near_ref, out_ref):
    tokens = middle_ref.shape[0]
    total = part_ref[...].astype(F32) + near_ref[...].astype(F32)
    out_ref[0:tokens, :] = (total[0:tokens] + middle_ref[...].astype(F32)).astype(BF16)
    out_ref[tokens:, :] = total[tokens:].astype(BF16)


def output_kernel(images, groups, s_ref, middle_ref, part_ref, mask_ref, *refs):
    fars, (out_ref, sums, mask_pad) = refs[: groups // 2 - 1], refs[groups // 2 - 1 :]
    tokens = images * PAD
    for r in range(0, groups, 2):
        total = part_ref[r // 2 * tokens : (r // 2 + 1) * tokens, :].astype(F32)
        for far, ref in enumerate(fars, 1):
            at = ((r // 2) ^ far) * tokens
            total = total + ref[at : at + tokens, :].astype(F32)
        out_ref[r // 2 * tokens : (r // 2 + 1) * tokens, :] = total.astype(BF16)
        if r == 0:
            output = total
    mixture = output - middle_ref[...].astype(F32)
    valid = valid_column(images, key_masks(images, s_ref[0], mask_ref, mask_pad))
    lane = lax.broadcasted_iota(jnp.int32, sums.shape, 1)
    sums[...] = jnp.where(
        lane == 2, jnp.sum(mixture * mixture * valid),
        jnp.where(lane == 3, jnp.sum(output * output * valid), 0.0),
    )


def place_tokens_kernel(count, images, places, s_ref, *refs):
    out, wide = refs[-2:]
    for group, (index, place) in enumerate(places):
        for image in range(images):
            start = (place * images + image) * PAD
            rows = refs[index][start : start + PAD, :].astype(F32)[:SEQ]
            at = jnp.bitwise_xor(s_ref[0], group) * images + image
            for k in range(D // LANES):
                wide[k, pl.ds(at, SEQ, stride=count), :] = rows[:, k * LANES : (k + 1) * LANES]
    for k in range(D // LANES):
        out[:, k * LANES : (k + 1) * LANES] = wide[k]


def place_experts_kernel(counts, first_row, s_ref, *refs):
    ins, outs = refs[: sum(counts)], refs[-1 if first_row else -2 :]
    height = outs[0].shape[1]
    at = 0
    for step, count in enumerate(counts):
        parts, at = ins[at : at + count], at + count

        @pl.when(pl.program_id(0) == step)
        def _():
            row = 0
            for part in parts:
                begin, end = max(first_row, row), min(first_row + height, row + part.shape[0])
                if begin < end:
                    outs[0][0, begin - first_row : end - first_row, :] = part[
                        begin - row : end - row, :
                    ].astype(F32)
                row += part.shape[0]
            if not first_row:
                bias = parts[0][height : height + 16, :].astype(F32)[0:1, :]
                outs[1][...] = jnp.broadcast_to(bias, outs[1].shape)


def split_kernel(chunks, s_ref, part_ref, near_ref, far_ref, out_ref):
    total = part_ref[...].astype(F32) + near_ref[...].astype(F32) + far_ref[...].astype(F32)
    share = total.shape[0] // chunks
    for chunk in range(chunks):
        out_ref[chunk] = total[chunk * share : (chunk + 1) * share].astype(BF16)


def join_kernel(dims, s_ref, pieces_ref, *refs):
    chunks, groups, half, width, small = dims
    norm1, norm2, forward, expert, back_bias, near_bias, far_bias = refs[:7]
    message, lines = refs[7:]
    total = pieces_ref[0].astype(F32)
    for chunk in range(1, chunks):
        total += pieces_ref[chunk].astype(F32)
    share = total.shape[0]
    row = lax.broadcasted_iota(jnp.int32, (share, 1), 0) + s_ref[3] * share
    squares = total * total
    lines[...] = jnp.zeros_like(lines)
    at = 0
    for source, index in ((norm1, 0), (norm1, 1), (norm2, 0), (norm2, 1), (norm2, 2)):
        lines[at : at + D // LANES, :] = as_lines(source[index : index + 1, :])
        at += D // LANES
    for part in (0, 2):
        for group in range(groups):
            biases, chunk = (near_bias, group) if group < half else (far_bias, group - half)
            line = biases[0:1, (3 * chunk + part) * width : (3 * chunk + part) * width + LANES]
            lines[pl.ds(at + jnp.bitwise_xor(s_ref[0], group), 1), :] = line
        at += groups
    lane = lax.broadcasted_iota(jnp.int32, (1, LANES), 1)
    terms = [
        jnp.sum(forward[0:1, :]),
        jnp.sum(forward[1:2, :]),
        0.0,
        0.0,
        jnp.sum(norm1[2:3, :]),
        jnp.sum(forward[2:3, :]) * (1.0 / D),
        jnp.sum(jnp.where(row < 3 * D, squares, 0.0)),
        jnp.sum(jnp.where((row >= 3 * D) & (row < 4 * D), squares, 0.0)),
        expert[1:2, 0:1],
        expert[2:3, 0:1],
        expert[3:4, 0:1],
    ]
    scalars = jnp.zeros((1, LANES), F32)
    for index, term in enumerate(terms):
        scalars = jnp.where(lane == index, term, scalars)
    lines[at : at + 1, :] = scalars
    lines[small - 8 : small - 8 + D // LANES, :] = as_lines(back_bias[0:1, :])
    values = lines[...]
    high = values.astype(BF16)
    low = (values - high.astype(F32)).astype(BF16)
    for chunk in range(chunks):
        message[chunk, 0:share, :] = total.astype(BF16)
        message[chunk, share : share + small, :] = high
        message[chunk, share + small :, :] = low


def spread_kernel(dims, s_ref, messages, outputs, qkv_out, out_out, sums, total):
    chunks, groups, width, small = dims
    share = messages.shape[1] - 2 * small
    summed = jnp.zeros((small, LANES), F32)
    at = small - 8
    for chunk in range(chunks):
        total[chunk * share : (chunk + 1) * share, :] = messages[chunk, 0:share, :].astype(F32)
        lines = messages[chunk, share : share + small, :].astype(F32) + messages[
            chunk, share + small :, :
        ].astype(F32)
        summed += lines
        sums[at : at + D // LANES, :] = lines[small - 8 : small - 8 + D // LANES]
        at += D // LANES
    sums[0 : small - 8, :] = summed[0 : small - 8]
    scalars = 5 * D // LANES + 2 * groups
    sums[scalars : scalars + 1, :] += outputs[0:1, :]
    per = EXPERTS // groups * (D // LANES)
    sums[at : at + per, :] = total[4 * D : 4 * D + per, :]
    qkv_out[...] = total[0 : 3 * D, :]
    for block in range(D // width):
        out_out[:, block * width : (block + 1) * width] = total[
            3 * D + block * width : 3 * D + (block + 1) * width, :
        ]


def finish_kernel(dims, s_ref, mine_ref, came_ref, *refs):
    chunks, groups, half, small, shared = dims
    gain1, shift1, gain2, shift2, out_bias, bias_out, router_out, back_out, norms_out, rms_out = refs
    per = D // LANES
    top = small - 8
    summed = mine_ref[0:top, :] + came_ref[0:top, :]
    squares = []
    for index, out in enumerate((gain1, shift1, gain2, shift2, out_bias)):
        block = summed[index * per : (index + 1) * per]
        squares.append(jnp.sum(block * block))
        out[...] = as_rows(block)
    at = 5 * per
    biases = summed[at : at + 2 * groups]
    place = lax.broadcasted_iota(jnp.int32, (groups, 1), 0) == s_ref[0]
    for part in range(2):
        lines = biases[part * groups : (part + 1) * groups]
        bias_out[part : part + 1, :] = jnp.sum(
            jnp.where(place, lines, 0.0), axis=0, keepdims=True
        )
    scalars = summed[at + 2 * groups : at + 2 * groups + 1]
    lane = lax.broadcasted_iota(jnp.int32, (1, LANES), 1)

    def scalar(index):
        return jnp.sum(jnp.where(lane == index, scalars, 0.0))

    share = EXPERTS // groups
    size = chunks * per + share * per
    for group in range(groups):
        source = mine_ref if group < half else came_ref
        start = top + (group if group < half else group - half) * size
        owner = jnp.bitwise_xor(s_ref[0], group)
        lane_expert = owner if shared else 0
        for chunk in range(chunks):
            line = as_rows(source[start + chunk * per : start + (chunk + 1) * per, :])
            back_out[pl.ds(chunk * s_ref[4] + lane_expert, 1), :] = line
        start += chunks * per
        router_rows = as_rows(source[start : start + share * per, :])
        for g in range(groups):
            @pl.when(owner == g)
            def _():
                router_out[g * share : (g + 1) * share, :] = router_rows
    router, back_bias = router_out[...], back_out[...]
    ordered = [
        squares[0], squares[1], scalar(6), jnp.sum(biases * biases), scalar(7), squares[4],
        squares[2], squares[3], jnp.sum(router * router), scalar(8), scalar(9), scalar(10),
        jnp.sum(back_bias * back_bias),
    ]
    norms = jnp.zeros((1, LANES), F32)
    for index, value in enumerate(ordered):
        norms = jnp.where(lane == index, value, norms)
    norms_out[...] = jnp.sqrt(norms)[:, :13]
    rms_out[...] = jnp.sqrt(scalars / (scalar(5) * D))[:, :5]


def shards(
    inputs, valid_mask, expert_ids, slot_ids, norm1_gain, norm1_bias, w_qkv, b_qv, w_out, b_out,
    norm2_gain, norm2_bias, w_router, w_in, b_in, w_back, b_back, cotangent, dp_size, tensor_size,
):
    count = inputs.shape[0]
    groups = tensor_size
    images = count // groups
    local_width = w_qkv.shape[2]
    heads = local_width // HD
    width = -(-local_width // LANES) * LANES
    local_experts, _, hidden_width = w_in.shape
    shared = local_experts == groups == 4
    pieces = groups if shared else 1
    chunks = dp_size
    rows = chunks * CAP
    own_tokens = images * PAD
    half = groups // 2
    data_at = lax.axis_index("dp").astype(jnp.int32)
    head_at = lax.axis_index("tensor").astype(jnp.int32)
    lane_expert = head_at if shared else jnp.int32(0)
    expert_at = data_at * local_experts + lane_expert
    first = jnp.int32(1) if shared else (head_at == 0).astype(jnp.int32)
    scalars = jnp.stack(
        [head_at, expert_at, first, data_at, jnp.int32(local_experts), lane_expert]
    )
    x_lines = jnp.transpose(inputs, (1, 0, 2)).reshape(SEQ * count, D)
    cot_lines = jnp.transpose(cotangent, (1, 0, 2)).reshape(SEQ * count, D)
    ids = jnp.transpose(expert_ids, (0, 2, 1))
    slots = jnp.transpose(slot_ids, (0, 2, 1))
    norms = jnp.stack([norm1_gain, norm1_bias, norm2_gain, norm2_bias, b_out]).astype(F32)
    router = jnp.transpose(w_router)
    last = [None]

    def call(kernel, ins, outs, **options):
        at = scalars if last[0] is None else after(scalars, last[0])
        got = run(kernel, at, ins, outs, **options)
        last[0] = got[0]
        return got

    def over(axis, size, value, by, *others):
        return swap(after(value, *others) if others else value, axis, size, by)

    def core(value, *others):
        return over("tensor", groups, value, 1, *others)

    def gather(value):
        parts = [value] + [None] * (groups - 1)
        for r in range(2, groups, 2):
            parts[r] = over("tensor", groups, value, r)
        for r in range(1, groups, 2):
            parts[r] = core(parts[r - 1])
        return parts

    def exchange(value, *others):
        value = after(value, *others) if others else value
        return lax.all_to_all(value.reshape(chunks, CAP, -1), "dp", 0, 0).reshape(rows, -1)

    fill = width - local_width
    qkv = jnp.pad(jnp.transpose(w_qkv, (1, 0, 2)), [(0, 0), (0, 0), (0, fill)])
    qkv = qkv.reshape(3 * D, width)
    out_rows = jnp.pad(w_out, [(0, fill), (0, 0)])
    qv_bias = jnp.pad(b_qv, [(0, 0), (0, fill)])
    bias_at = 4 * D + 16
    bias_lines = -(-(local_experts * hidden_width // width) // 16) * 16
    pack = call(
        functools.partial(pack_kernel, width),
        [qkv, out_rows, qv_bias, b_in], [((bias_at + bias_lines, width), BF16)], mib=58,
    )[0]
    packs = [pack, core(pack)] + [None] * (groups - 2)
    for r in range(2, groups, 2):
        packs[r] = over("tensor", groups, pack, r)

    block = D + hidden_width
    tall = D // LANES, SEQ * count, LANES
    got = call(
        functools.partial(start_kernel, (count, images, chunks, shared)),
        [ids, slots, cot_lines] + ([w_in, w_back] if shared else []),
        [((own_tokens, D), BF16)] + [((CAP, D + LANES), BF16)] * (chunks // 2)
        + [((rows // 2, D + LANES), BF16)]
        + ([((block, D), BF16)] * (pieces - 1) if shared else []),
        left=(3, 4), mib=58,
        scratch=[
            pltpu.VMEM(tall, F32), pltpu.VMEM((own_tokens, D), F32),
            pltpu.VMEM((rows, D + LANES), F32), pltpu.VMEM((rows, D + LANES), F32),
            pltpu.SemaphoreType.DMA((6,)),
        ],
    )
    cot_own, ups, up_far = got[0], got[1 : 1 + chunks // 2], got[1 + chunks // 2]
    up_far = over("dp", chunks, up_far, chunks // 2)
    if shared:
        weights = [None, got[-3], over("tensor", groups, got[-2], 2), got[-1]]
    for r in range(2, groups, 2):
        packs[r + 1] = core(packs[r], cot_own)

    mask_pad = pltpu.VMEM((8, WIDE), jnp.int32)
    x_own, normed1, normed2, middle, forward_sums, projected, attended = call(
        functools.partial(heads_kernel, count, images, heads, width, groups),
        [x_lines, norms, valid_mask, *packs],
        [((own_tokens, D), BF16)] * 4 + [((8, D), F32)]
        + [((own_tokens, groups * 3 * width), BF16), ((own_tokens, groups * width), BF16)],
        scratch=[pltpu.VMEM(tall, F32), pltpu.VMEM((own_tokens, D), F32), mask_pad], mib=MIB_HEADS,
        stream=True,
    )
    half_heads = {
        which: [
            pl.BlockSpec((own_tokens, half * size * width), lambda step, s, at=which: (0, at))
            for size in (3, 1)
        ]
        for which in (0, 1)
    }

    tokens = [normed2, core(normed2)] + [None] * (groups - 2)
    early = chunks // 2 - 1
    ups = list(ups)
    for r in range(1, early):
        ups[r] = over("dp", chunks, ups[r], r, normed2)
    for r in range(2, groups, 2):
        tokens[r] = over("tensor", groups, normed2, r)
    turn = [up_far, *ups[1:early]]
    if shared:
        turn.append(weights[2])
    for r in range(2, groups, 2):
        tokens[r + 1] = core(tokens[r], *turn)
    if shared:
        weights[3] = over("tensor", groups, weights[3], 3, tokens[2])
        weights[1] = core(weights[1], tokens[2])
    flat_pad = pltpu.VMEM((8, WIDE), jnp.int32)
    sent, *passed = call(
        functools.partial(dispatch_kernel, groups, images, chunks),
        [ids, slots, *tokens, up_far, ups[early]],
        [((rows, D), BF16)] + [((CAP, D + LANES), BF16)] * (early - 1)
        + [((2 * CAP, D + LANES), BF16)],
        scratch=[flat_pad],
    )
    dispatched = exchange(sent)
    passed = [over("dp", chunks, value, r) for r, value in enumerate(passed, 1)]
    ups = [*ups[:early], up_far, *passed]

    by_piece = pl.BlockSpec((1, rows, hidden_width), lambda step, s: (step, 0, 0))
    bias_spec = pl.BlockSpec((bias_lines, width), lambda step, s: (bias_at // bias_lines, 0))
    first_rows = pl.BlockSpec((CAP, D + LANES), lambda step, s: (0, 0))
    before = chunks
    hidden, d_pre, d_results, d_sent, mixed_sent, router_part, back_bias = call(
        functools.partial(expert_kernel, (chunks, pieces, hidden_width, width)),
        [dispatched, *ups, *packs[:pieces], router, b_back, w_in, w_back]
        + (weights[1:] if shared else []),
        [((pieces, rows, hidden_width), BF16)] * 2 + [((rows, D), BF16)] * 3
        + [((EXPERTS, D), F32), ((8, D), F32)],
        grid=(pieces,),
        in_specs={chunks // 2: first_rows, **{before + k: bias_spec for k in range(pieces)}},
        out_specs={0: by_piece, 1: by_piece},
        scratch=[
            pltpu.VMEM((rows, D + LANES), F32),
            pltpu.VMEM((rows, LANES), F32),
            pltpu.VMEM((2, D, hidden_width), BF16),
            pltpu.VMEM((2, hidden_width, D), BF16),
            pltpu.VMEM((8, hidden_width), F32),
            pltpu.VMEM((rows, D), F32),
            pltpu.VMEM((rows, D), F32),
            pltpu.SemaphoreType.DMA((2, 2)),
        ],
        left=range(before + pieces + 2, before + pieces + 4 + pieces), mib=61,
    )
    d_back = exchange(d_sent)
    tall_grad = D + 16 + hidden_width
    first_cut = -(-2 * tall_grad // 48) * 16
    plans = [((3,), (first_cut, tall_grad - first_cut)), ((2, 0, 1), (tall_grad,))]
    if not shared:
        plans = [((0,), (D + 16, hidden_width))]
    lane_counts = (D, D) if shared else (hidden_width, D)
    grads, expert_sums = {}, []
    for kept, cuts in plans:
        part = pl.BlockSpec(
            (1 if len(kept) == 1 else 3, rows, hidden_width),
            lambda step, s, at=kept[0] if len(kept) == 1 else 0: (at, 0, 0),
        )
        held = tuple(range(len(kept))) if len(kept) == 1 else kept
        *some, sums = call(
            functools.partial(expert_grads_kernel, held, cuts),
            [dispatched, d_results, hidden, d_pre],
            [((cut, wide), BF16) for cut, wide in zip(cuts, lane_counts)] * len(kept)
            + [((8, LANES), F32)],
            in_specs={2: part, 3: part}, mib=58,
        )
        for index, piece in enumerate(kept):
            grads[piece] = some[index * len(cuts) : (index + 1) * len(cuts)]
        expert_sums.append(sums)

    def combine(value):
        return call(
            functools.partial(combine_kernel, groups, images, chunks),
            [ids, slots, value],
            [((half * own_tokens, D), BF16)] * 2, scratch=[flat_pad],
        )

    def reduce_own(keep, send, size, *others):
        came = core(send)
        far = [None, None]
        for r in range(2, groups, 2):
            for part in range(2):
                start = r // 2 * size + part * (size // 2)
                span = slice(start, start + size // 2)
                out = (keep[span].astype(F32) + came[span].astype(F32)).astype(BF16)
                term = over("tensor", groups, out, r, *others)
                if far[part] is not None:
                    term = far[part].astype(F32) + term.astype(F32)
                far[part] = term
        return keep, came, far

    if shared:
        last_top = over("tensor", groups, grads[3][0], 2)
        d_back = after(d_back, last_top)
    d_keep, d_near, d_far = reduce_own(*combine(d_back), own_tokens)
    if shared:
        last_rest = over("tensor", groups, grads[3][1], 2, *d_far)
    mixed = exchange(mixed_sent, d_back)

    router_lines = EXPERTS // groups * (D // LANES)
    share = -(-(4 * D + router_lines) // (16 * chunks)) * 16

    def grads_out(parts):
        return [((8, parts * 3 * width), F32)] + [((chunks * share, width), BF16)] * parts

    first_half = pl.BlockSpec((own_tokens, D), lambda step, s: (0, 0))
    got = call(
        functools.partial(
            middle_pull_kernel, (images, heads, width, groups - half, half, groups)
        ),
        [cot_own, d_keep, d_near, *d_far, middle, norms, normed1, valid_mask, projected,
         attended, router_part, *packs[half:]],
        [((own_tokens, D), BF16), ((8, D), F32), ((own_tokens, D), BF16)]
        + grads_out(groups - half),
        scratch=[mask_pad], mib=MIB_PULL, in_specs={**dict(zip((9, 10), half_heads[1])), 1: first_half, 2: first_half},
    )
    d_low, norm2_sums, d_branch, far_bias = got[:4]
    far_grads = list(got[4:])

    def add_odd(grads):
        return (grads[0].astype(F32) + core(grads[1]).astype(F32)).astype(BF16)

    if shared:
        far_grads[1] = after(far_grads[1], last_rest)
    far = None
    for r in range(0, groups - half, 2):
        out = add_odd(far_grads[r : r + 2])
        d_low = after(d_low, out)
        term = over("tensor", groups, out, half + r)
        far = term if far is None else far.astype(F32) + term.astype(F32)
    got = call(
        functools.partial(input_pull_kernel, (images, heads, width, half, 0, groups)),
        [x_own, d_low, d_branch, norms, normed1, valid_mask, projected, attended,
         router_part, *packs[:half]],
        [((own_tokens, D), BF16), ((8, D), F32)] + grads_out(half),
        scratch=[mask_pad], mib=MIB_PULL, in_specs=dict(zip((6, 7), half_heads[0])),
    )
    d_own, norm1_sums, near_bias = got[:3]
    head_grads = list(got[3:])
    for r in range(2, half, 2):
        term = over("tensor", groups, add_odd(head_grads[r : r + 2]), r)
        far = far.astype(F32) + term.astype(F32)
    near = core(head_grads[1], far)
    split = call(
        functools.partial(split_kernel, chunks),
        [head_grads[0], near, far], [((chunks, share, width), BF16)],
    )[0]
    d_tokens = [d_own, core(d_own)] + [None] * (groups - 2)
    for r in range(2, groups, 2):
        d_tokens[r] = over("tensor", groups, d_own, r)
    pieces_in = lax.all_to_all(after(split, d_tokens[2]), "dp", 0, 0)
    mix_keep, mix_send = combine(mixed)
    mix_near = core(mix_send)

    def place_tokens(parts, places):
        placed = call(
            functools.partial(place_tokens_kernel, count, images, places),
            parts, [((SEQ * count, D), F32)],
            scratch=[pltpu.VMEM(tall, F32)],
        )[0]
        return jnp.transpose(placed.reshape(SEQ, count, D), (1, 0, 2))

    for r in range(2, groups, 2):
        d_tokens[r + 1] = core(d_tokens[r], split)

    def place_experts(came, pieces_here, first_row, shape, before=()):
        steps = len(pieces_here)

        def piece_at(step):
            place = jnp.int32(0)
            for index, piece in enumerate(pieces_here):
                place = jnp.where(step == index, piece, place)
            return place

        spec = pl.BlockSpec((1, *shape), lambda step, s: (jnp.bitwise_xor(s[0], piece_at(step)), 0, 0))
        lines = pl.BlockSpec((1, 8, hidden_width), lambda step, s: (step, 0, 0))
        parts = [a for piece in came for a in piece]
        bias = [] if first_row else [((steps, 8, hidden_width), F32)]
        return call(
            functools.partial(
                place_experts_kernel, tuple(len(piece) for piece in came), first_row
            ),
            [*parts, *before], [((local_experts, *shape), F32)] + bias,
            grid=(steps,), out_specs={0: spec, 1: lines}, left=range(len(parts), len(parts) + 1),
            aliases={len(parts): 0} if before else None,
        )

    mix = call(
        mixture_kernel, [middle, mix_keep, mix_near], [((half * own_tokens, D), BF16)]
    )[0]
    mix_far = [over("tensor", groups, mix, r) for r in range(2, groups, 2)]
    d_inputs = place_tokens(d_tokens, [(r, 0) for r in range(groups)])
    if shared:
        whole = (0, 1, 3), [grads[0], [core(grads[1][0])], [core(last_top), core(last_rest)]]
        g_w_in, lines_in = place_experts(whole[1], whole[0], 0, (D, hidden_width))
        (g_w_back,) = place_experts(whole[1], whole[0], D + 16, (hidden_width, D))
    small = -(-(5 * D // LANES + 2 * groups + 1) // 8) * 8 + 8
    small = -(-small // 16) * 16
    message = call(
        functools.partial(join_kernel, (chunks, groups, half, width, small)),
        [pieces_in, norm1_sums, norm2_sums, forward_sums, sum(expert_sums), back_bias, near_bias,
         far_bias],
        [((chunks, share + 2 * small, width), BF16)], scratch=[pltpu.VMEM((small, LANES), F32)],
        mib=58,
    )[0]
    messages = lax.all_to_all(message, "dp", 0, 0)
    output_own, output_sums = call(
        functools.partial(output_kernel, images, groups),
        [middle, mix, valid_mask, *mix_far],
        [((half * own_tokens, D), BF16), ((8, LANES), F32)], scratch=[mask_pad],
    )
    by = 1
    while by < chunks:
        output_sums = output_sums + over("dp", chunks, output_sums, by)
        by *= 2
    out_near = core(output_own)

    output = place_tokens([output_own, out_near], [(r % 2, r // 2) for r in range(groups)])
    top = small - 8
    qkv_sum, out_sum, sums = call(
        functools.partial(spread_kernel, (chunks, groups, width, small)),
        [messages, output_sums],
        [((3 * D, width), F32), ((width, D), F32),
         ((top + chunks * (D // LANES) + router_lines, LANES), F32)],
        scratch=[pltpu.VMEM((chunks * share, width), F32)],
    )
    by = 1
    while True:
        came = over("tensor", groups, sums, by)
        by *= 2
        if by == groups:
            break
        sums = jnp.concatenate([sums[:top] + came[:top], sums[top:], came[top:]], axis=0)

    if shared:
        last_piece = [[over("tensor", groups, grads[2][0], 2, mix_far[0])]]
        g_w_in, line_in = place_experts(last_piece, (2,), 0, (D, hidden_width), [g_w_in])
        (g_w_back,) = place_experts(last_piece, (2,), D + 16, (hidden_width, D), [g_w_back])
        by_piece = jnp.concatenate([lines_in[:2, 0], line_in[:, 0], lines_in[2:, 0]], axis=0)
        order = jnp.bitwise_xor(head_at, jnp.arange(groups, dtype=jnp.int32))
        g_b_in = jnp.take(by_piece, order, axis=0)
    else:
        g_w_in = grads[0][0][None, :D].astype(F32)
        g_w_back = grads[0][1][None].astype(F32)
        g_b_in = grads[0][0][D : D + 1].astype(F32)

    vector = [((1, D), F32)]
    (
        g_norm1_gain, g_norm1_bias, g_norm2_gain, g_norm2_bias, g_b_out, g_b_qv, router_grad,
        g_b_back, grad_norms, rms_values,
    ) = call(
        functools.partial(finish_kernel, (chunks, groups, half, small, shared)),
        [sums, came],
        vector * 5
        + [((2, LANES), F32), ((EXPERTS, D), F32), ((EXPERTS, D), F32)]
        + [((1, 13), F32), ((1, 5), F32)],
    )
    g_w_qkv = jnp.transpose(qkv_sum.reshape(3, D, width), (1, 0, 2))[:, :, :local_width]
    return (
        output, d_inputs, g_norm1_gain[0], g_norm1_bias[0], g_w_qkv, g_b_qv[:, :local_width],
        out_sum[:local_width], g_b_out[0], g_norm2_gain[0], g_norm2_bias[0],
        jnp.transpose(router_grad), g_w_in, g_b_in, g_w_back, g_b_back,
        grad_norms[0], rms_values[0],
    )


def solution(mesh):
    placed = (
        P("dp", None, None),
        P("dp", None),
        P("dp", None, None),
        P("dp", None, None),
        P(),
        P(),
        P(None, None, "tensor"),
        P(None, "tensor"),
        P("tensor", None),
        P(),
        P(),
        P(),
        P(),
        P("dp", None, "tensor"),
        P("dp", "tensor"),
        P("dp", "tensor", None),
        P(),
        P("dp", None, None),
    )
    return jax.shard_map(
        functools.partial(shards, dp_size=mesh.shape["dp"], tensor_size=mesh.shape["tensor"]),
        mesh=mesh,
        in_specs=placed,
        out_specs=(
            P("dp", None, None),
            P("dp", None, None),
            P(),
            P(),
            P(None, None, "tensor"),
            P(None, "tensor"),
            P("tensor", None),
            P(),
            P(),
            P(),
            P(),
            P("dp", None, "tensor"),
            P("dp", "tensor"),
            P("dp", "tensor", None),
            P(),
            P(),
            P(),
        ),
        check_vma=False,
    )
```

```python
import functools

import jax
import jax.numpy as jnp
from jax import lax
from jax.experimental import pallas as pl
from jax.experimental.pallas import tpu as pltpu
from jax.sharding import PartitionSpec as P

D = 512
HD = 64
EXPERTS = 32
SEQ = 197
CAP = 104
PAD = 208
UPS = CAP + 8
WIDE = 256
MIB_HEADS = 58
MIB_EXPERT = 58
MIB_GRADS = 58
MIB_PULL = 58
LANES = 128
F32 = jnp.float32
BF16 = jnp.bfloat16


def nn(a, b):
    return lax.dot_general(a, b, (((1,), (0,)), ((), ())), preferred_element_type=F32)


def nt(a, b):
    return lax.dot_general(a, b, (((1,), (1,)), ((), ())), preferred_element_type=F32)


def tn(a, b):
    return lax.dot_general(a, b, (((0,), (0,)), ((), ())), preferred_element_type=F32)


def swap(value, axis, size, by):
    return lax.ppermute(value, axis, [(at, at ^ by) for at in range(size)])


def after(value, *others):
    return lax.optimization_barrier((value, *others))[0]


class Held:
    def __init__(self, ref, copy):
        self.ref, self.copy, self.there = ref, copy, False
        self.shape, self.dtype = ref.shape, ref.dtype

    def __getitem__(self, index):
        if not self.there:
            self.copy.wait()
            self.there = True
        return self.ref[index]


class Sent:
    def __init__(self, ref, copy):
        self.ref, self.copy, self.left = ref, copy, False
        self.shape, self.dtype = ref.shape, ref.dtype

    def __getitem__(self, index):
        return self.ref[index]

    def __setitem__(self, index, value):
        self.ref[index] = value

    def send(self):
        if not self.left:
            self.copy.start()
            self.left = True


def streamed(kernel, ins, outs, scratch):
    shapes = [(a.shape, a.dtype) for a in ins] + list(outs)

    def body(s_ref, *refs):
        far, refs = refs[: len(shapes)], refs[len(shapes) :]
        near, refs, sems = refs[: len(shapes)], refs[len(shapes) : -1], refs[-1]
        held = []
        for i in range(len(ins)):
            copy = pltpu.make_async_copy(far[i], near[i], sems.at[i])
            copy.start()
            held.append(Held(near[i], copy))
        sent = [
            Sent(near[i], pltpu.make_async_copy(near[i], far[i], sems.at[i]))
            for i in range(len(ins), len(shapes))
        ]
        kernel(s_ref, *held, *sent, *refs)
        for value in held:
            if not value.there:
                value.copy.wait()
        for value in sent:
            value.send()
        for value in sent:
            value.copy.wait()

    buffers = [pltpu.VMEM(shape, dtype) for shape, dtype in shapes]
    return body, [*buffers, *scratch, pltpu.SemaphoreType.DMA((len(shapes),))]


def run(
    kernel, scalars, ins, outs, scratch=(), grid=(1,), in_specs=None, out_specs=None, mib=28, left=(),
    stream=False, aliases=None,
):
    in_specs, out_specs = in_specs or {}, out_specs or {}
    if stream:
        kernel, scratch = streamed(kernel, ins, outs, scratch)
        left = range(len(ins))
        out_specs = {i: pl.BlockSpec(memory_space=pl.ANY) for i in range(len(outs))}

    def whole(shape, stays=False):
        if stays:
            return pl.BlockSpec(memory_space=pl.ANY)
        return pl.BlockSpec(shape, lambda step, s, nd=len(shape): (0,) * nd)

    return pl.pallas_call(
        kernel,
        grid_spec=pltpu.PrefetchScalarGridSpec(
            num_scalar_prefetch=1,
            grid=grid,
            in_specs=[
                in_specs[i] if i in in_specs else whole(a.shape, i in left)
                for i, a in enumerate(ins)
            ],
            out_specs=[out_specs[i] if i in out_specs else whole(o[0]) for i, o in enumerate(outs)],
            scratch_shapes=list(scratch),
        ),
        out_shape=[jax.ShapeDtypeStruct(shape, dtype) for shape, dtype in outs],
        input_output_aliases={i + 1: o for i, o in (aliases or {}).items()},
        compiler_params=pltpu.CompilerParams(vmem_limit_bytes=mib * 2**20),
        cost_estimate=pl.CostEstimate(flops=0, bytes_accessed=0, transcendentals=0),
    )(scalars, *ins)


def route_rows(ids_ref, slots_ref, image):
    ids, slots = ids_ref[image], slots_ref[image]
    return jnp.where(slots < CAP, ids * CAP + slots, -1)


def block_start(s_ref, chunk):
    return (chunk * s_ref[4] + s_ref[5]) * CAP


def target_column(s_ref, chunks):
    rows = lax.broadcasted_iota(jnp.int32, (CAP, 1), 0)
    starts = [block_start(s_ref, chunk) for chunk in range(chunks)]
    return jnp.concatenate([rows + start for start in starts], axis=0)


def target_row(s_ref, chunks):
    lanes = lax.broadcasted_iota(jnp.int32, (1, chunks * CAP), 1)
    target = lanes
    for chunk in range(chunks):
        here = (lanes >= chunk * CAP) & (lanes < (chunk + 1) * CAP)
        target = jnp.where(here, lanes + (block_start(s_ref, chunk) - chunk * CAP), target)
    return target


def spread(source_ref, wide_ref, count):
    for k in range(D // LANES):
        wide_ref[k] = source_ref[:, k * LANES : (k + 1) * LANES].astype(F32)

    def image_rows(image):
        return jnp.concatenate(
            [wide_ref[k, pl.ds(image, SEQ, stride=count), :] for k in range(D // LANES)], axis=1
        )

    return image_rows


def own_rows(images, me, image_rows, out_ref, padded):
    padded[...] = jnp.zeros_like(padded)
    for image in range(images):
        padded[image * PAD : image * PAD + SEQ, :] = image_rows(me * images + image)
    out_ref[...] = padded[...].astype(BF16)


def pack_kernel(width, s_ref, qkv_ref, out_ref, bias_ref, in_bias_ref, pack):
    pack[0 : 3 * D, :] = qkv_ref[...]
    for block in range(D // width):
        at = 3 * D + block * width
        pack[at : at + width, :] = out_ref[:, block * width : (block + 1) * width]
    bias = bias_ref[...].astype(F32)
    experts, hidden = in_bias_ref.shape
    lines = in_bias_ref[...].astype(F32)
    lines = [
        lines[e : e + 1, k * width : (k + 1) * width]
        for e in range(experts)
        for k in range(hidden // width)
    ]
    fill = -len(lines) % 16
    if fill:
        lines.append(jnp.zeros((fill, width), F32))
    pack[4 * D :, :] = jnp.concatenate(
        [bias[0:1], bias[1:2], jnp.zeros((14, width), F32), *lines], axis=0
    ).astype(BF16)


def start_kernel(dims, s_ref, ids_ref, slots_ref, cot_ref, *refs):
    count, images, chunks, shared = dims
    copies = []
    if shared:
        w_in, w_back, *refs = refs
    own, *refs = refs
    near_outs, far_out, refs = refs[: chunks // 2], refs[chunks // 2], refs[chunks // 2 + 1 :]
    if shared:
        *laid, refs = *refs[:3], refs[3:]
    wide, padded, blocks, marks, square, wholes, sems = refs
    if shared:
        hidden = w_back.shape[1]
        for r, target in enumerate(laid, 1):
            expert = jnp.bitwise_xor(s_ref[0], r)
            for side, (source, place) in enumerate(
                ((w_in, pl.ds(0, D)), (w_back, pl.ds(D, hidden)))
            ):
                copies.append(
                    pltpu.make_async_copy(
                        source.at[expert], target.at[place], sems.at[2 * r - 2 + side]
                    )
                )
    for copy in copies:
        copy.start()
    image_rows = spread(cot_ref, wide, count)
    target = target_column(s_ref, chunks)
    rows = chunks * CAP
    blocks[...] = jnp.zeros_like(blocks)
    marks[...] = jnp.zeros_like(marks)

    def step(pair, carry):
        total = jnp.zeros((rows, D), F32)
        others = jnp.zeros((rows, SEQ), F32)
        for image in (2 * pair, 2 * pair + 1):
            flat = route_rows(ids_ref, slots_ref, image)
            ids = ids_ref[image].astype(F32)
            first = target == flat[0:1, :]
            second = target == flat[1:2, :]
            hit = (first | second).astype(F32).astype(BF16)
            total += nn(hit, image_rows(image).astype(BF16))
            others += jnp.where(first, ids[1:2, :], 0.0) + jnp.where(second, ids[0:1, :], 0.0)
        blocks[...] += total
        marks[...] += jnp.broadcast_to(jnp.sum(others, axis=1, keepdims=True), marks.shape)
        return carry

    lax.fori_loop(0, count // 2, step, 0)
    square[...] = jnp.zeros_like(square)
    wholes[...] = jnp.zeros_like(wholes)
    for chunk in range(chunks):
        at = pl.multiple_of(jnp.bitwise_xor(s_ref[3], chunk) * CAP, 8)
        place = chunk * UPS
        wholes[place : place + CAP, :] = blocks[pl.ds(at, CAP), :]
        square[0:CAP, :] = marks[pl.ds(at, CAP), :]
        wholes[place + CAP : place + UPS, 0:LANES] = jnp.transpose(square[...])[0:8, :]
    for chunk, near_out in enumerate(near_outs):
        near_out[...] = wholes[chunk * UPS : (chunk + 1) * UPS, :].astype(BF16)
    far_out[...] = wholes[chunks // 2 * UPS :, :].astype(BF16)
    own_rows(images, s_ref[0], image_rows, own, padded)
    for copy in copies:
        copy.wait()


def padded_routes(ids_ref, slots_ref, image, flat_ref):
    flat_ref[...] = jnp.full(flat_ref.shape, -1, jnp.int32)
    flat_ref[0:2, 0:SEQ] = route_rows(ids_ref, slots_ref, image)
    return flat_ref[...]


def dispatch_kernel(groups, images, chunks, s_ref, ids_ref, slots_ref, *refs):
    tokens, (far, late, out, *passed, flat_ref) = refs[:groups], refs[groups:]
    for chunk, on in enumerate(passed, 1):
        on[0:UPS, :] = far[chunk * UPS : (chunk + 1) * UPS, :]
    passed[-1][UPS:, :] = late[...]
    me = s_ref[0]
    target = target_column(s_ref, chunks)
    total = jnp.zeros((chunks * CAP, D), F32)
    for group in range(groups):
        for image in range(images):
            at = jnp.bitwise_xor(me, group) * images + image
            flat = padded_routes(ids_ref, slots_ref, at, flat_ref)[:, :PAD]
            hit = (target == flat[0:1, :]) | (target == flat[1:2, :])
            total += nn(
                hit.astype(F32).astype(BF16), tokens[group][image * PAD : (image + 1) * PAD, :]
            )
    out[...] = total.astype(BF16)


def combine_kernel(groups, images, chunks, s_ref, ids_ref, slots_ref, rows_ref, *refs):
    outs, flat_ref = refs[:2], refs[2]
    me = s_ref[0]
    rows = rows_ref[...]
    target = target_row(s_ref, chunks)

    def step(pair, carry):
        for odd in range(2):
            for image in range(images):
                at = jnp.bitwise_xor(me, 2 * pair + odd) * images + image
                flat = jnp.transpose(padded_routes(ids_ref, slots_ref, at, flat_ref))[:PAD, :]
                hit = (flat[:, 0:1] == target) | (flat[:, 1:2] == target)
                place = pl.multiple_of((pair * images + image) * PAD, 16)
                outs[odd][pl.ds(place, PAD), :] = nn(
                    hit.astype(F32).astype(BF16), rows
                ).astype(BF16)
        return carry

    lax.fori_loop(0, groups // 2, step, 0)


def chunk_weights(packs, width):
    qkv = [p[part * D : (part + 1) * D, :] for p in packs for part in range(3)]
    biases = []
    for p in packs:
        lines = p[3 * D + D : 3 * D + D + 16, :].astype(F32)
        biases += [lines[0:1], jnp.zeros((1, width), F32), lines[1:2]]
    outs = [
        jnp.concatenate(
            [p[3 * D + b * width : 3 * D + (b + 1) * width, :] for b in range(D // width)], axis=1
        )
        for p in packs
    ]
    return (
        jnp.concatenate(qkv, axis=1),
        jnp.concatenate(biases, axis=1),
        jnp.concatenate(outs, axis=0),
    )


def normalize(values):
    average = jnp.mean(values, axis=-1, keepdims=True)
    centered = values - average
    inv_std = lax.rsqrt(jnp.mean(centered * centered, axis=-1, keepdims=True) + 1e-06)
    return centered * inv_std, inv_std


def norm_pull(upstream, normal, inv_std, gain):
    scaled = upstream * gain
    inner = jnp.mean(scaled * normal, axis=-1, keepdims=True)
    return inv_std * (scaled - jnp.mean(scaled, axis=-1, keepdims=True) - normal * inner)


def key_masks(images, me, mask_ref, pad_ref):
    pad_ref[...] = jnp.full(pad_ref.shape, -1, jnp.int32)
    for image in range(images):
        pad_ref[image : image + 1, 0:SEQ] = mask_ref[pl.ds(me * images + image, 1), :]
    return pad_ref[...]


def valid_column(images, masks):
    columns = jnp.transpose(jnp.maximum(masks, 0).astype(F32))
    return jnp.concatenate([columns[:PAD, i : i + 1] for i in range(images)], axis=0)


def probabilities_of(queries, key_rows, key_mask):
    shift = jnp.where(key_mask > 0, 0.0, jnp.where(key_mask < 0, -2e30, -1e30))
    scores = nt(queries * jnp.asarray(HD ** (-0.5), BF16), key_rows) + shift
    exps = jnp.exp(scores - jnp.max(scores, axis=-1, keepdims=True))
    return exps * (1.0 / jnp.sum(exps, axis=-1, keepdims=True))


def by_head(rows, heads):
    zeros = jnp.zeros_like(rows)
    width = rows.shape[1]
    return jnp.concatenate(
        [jnp.where(head_lanes(width, head), rows, zeros) for head in range(heads)], axis=0
    )


def own_lanes(stacked, heads):
    result = stacked[:PAD]
    for head in range(1, heads):
        lanes = head_lanes(stacked.shape[1], head)
        result = jnp.where(lanes, stacked[head * PAD : (head + 1) * PAD], result)
    return result


def head_lanes(width, head):
    lane = lax.broadcasted_iota(jnp.int32, (1, width), 1)
    return (lane >= head * HD) & (lane < (head + 1) * HD)


def attend(images, heads, width, chunks, normed, weight, bias, masks, projected_ref):
    projected = (nn(normed, weight) + bias).astype(BF16)
    projected_ref[...] = projected
    projected_ref.send()
    parts = []
    for image in range(images):
        key_mask = masks[image : image + 1, :PAD]
        line = []
        for chunk in range(chunks):
            queries, key_rows, values = (
                projected[
                    image * PAD : (image + 1) * PAD,
                    (3 * chunk + part) * width : (3 * chunk + part + 1) * width,
                ]
                for part in range(3)
            )
            own = by_head(queries, heads)
            probabilities = probabilities_of(own, key_rows, key_mask)
            mixed = own_lanes(nn(probabilities.astype(BF16), values), heads)
            line.append(mixed.astype(BF16))
        parts.append(jnp.concatenate(line, axis=1))
    return projected, jnp.concatenate(parts, axis=0)


def heads_kernel(count, images, heads, width, chunks, s_ref, x_ref, norms_ref, mask_ref, *refs):
    packs, outs = refs[:chunks], refs[chunks : chunks + 7]
    wide, padded, mask_pad = refs[-3:]
    x_own, normed_ref, normed2_ref, middle_ref, sums, projected_ref, attended_ref = outs
    own_rows(images, s_ref[0], spread(x_ref, wide, count), x_own, padded)
    x_own.send()
    stream = padded[...]
    normal, _ = normalize(stream)
    normed = (normal * norms_ref[0:1, :] + norms_ref[1:2, :]).astype(BF16)
    normed_ref[...] = normed
    normed_ref.send()
    masks = key_masks(images, s_ref[0], mask_ref, mask_pad)
    weight, bias, out_weight = chunk_weights(packs, width)
    projected, attended = attend(
        images, heads, width, chunks, normed, weight, bias, masks, projected_ref
    )
    attended_ref[...] = attended
    attended_ref.send()
    branch = nn(attended, out_weight) + norms_ref[4:5, :]
    middle = stream + branch
    normal, _ = normalize(middle)
    normed2_ref[...] = (normal * norms_ref[2:3, :] + norms_ref[3:4, :]).astype(BF16)
    normed2_ref.send()
    middle_ref[...] = middle.astype(BF16)
    middle_ref.send()
    valid = valid_column(images, masks)
    sums[...] = jnp.concatenate(
        [
            jnp.sum(middle * middle * valid, axis=0, keepdims=True),
            jnp.sum(branch * branch * valid, axis=0, keepdims=True),
            jnp.broadcast_to(jnp.sum(valid, axis=0, keepdims=True), (1, D)),
            jnp.zeros((5, D), F32),
        ],
        axis=0,
    )


def as_lines(rows):
    return jnp.concatenate([rows[:, k * LANES : (k + 1) * LANES] for k in range(D // LANES)], axis=0)


def as_rows(lines):
    count = lines.shape[0] // (D // LANES)
    return jnp.concatenate(
        [lines[k * count : (k + 1) * count] for k in range(D // LANES)], axis=1
    )


def attend_pull(images, heads, width, chunks, projected_ref, d_attended, masks):
    parts = []
    for image in range(images):
        span = slice(image * PAD, (image + 1) * PAD)
        key_mask = masks[image : image + 1, :PAD]
        line = []
        for chunk in range(chunks):
            queries, key_rows, values = (
                projected_ref[span, (3 * chunk + part) * width : (3 * chunk + part + 1) * width]
                for part in range(3)
            )
            d_mixed = d_attended[span, chunk * width : (chunk + 1) * width]
            own = by_head(queries, heads)
            d_own = by_head(d_mixed, heads)
            probabilities = probabilities_of(own, key_rows, key_mask)
            d_probs = nt(d_own, values)
            row_dots = jnp.sum(d_probs * probabilities, axis=-1, keepdims=True)
            d_scores = probabilities * (d_probs - row_dots)
            d_scores = jnp.where(key_mask > 0, d_scores, 0.0).astype(BF16)
            d_values = tn(probabilities.astype(BF16), d_own)
            d_queries = own_lanes(nn(d_scores, key_rows), heads)
            d_keys = tn(d_scores, own)
            line += [d_queries * HD ** (-0.5), d_keys * HD ** (-0.5), d_values]
        parts.append(jnp.concatenate(line, axis=1).astype(BF16))
    return jnp.concatenate(parts, axis=0)


def heads_pull(
    dims, s_ref, normed, projected_ref, attended_ref, d_branch, packs, masks, router_ref, grads, biases
):
    images, heads, width, chunks, start, groups = dims
    weight, _, out_weight = chunk_weights(packs, width)
    d_attended = nt(d_branch, out_weight).astype(BF16)
    d_project = attend_pull(images, heads, width, chunks, projected_ref, d_attended, masks)
    grad = tn(normed, d_project)
    out_grad = tn(attended_ref[...], d_branch)
    for chunk in range(chunks):
        for part in range(3):
            at = (3 * chunk + part) * width
            grads[chunk][part * D : (part + 1) * D, :] = grad[:, at : at + width].astype(BF16)
        for block in range(D // width):
            at = 3 * D + block * width
            grads[chunk][at : at + width, :] = out_grad[
                chunk * width : (chunk + 1) * width, block * width : (block + 1) * width
            ].astype(BF16)
        per = EXPERTS // groups
        owner = jnp.bitwise_xor(s_ref[0], start + chunk)
        router = router_ref[0:per, :]
        for g in range(1, groups):
            router = jnp.where(owner == g, router_ref[g * per : (g + 1) * per, :], router)
        router = as_lines(router)
        grads[chunk][4 * D : 4 * D + router.shape[0], :] = router.astype(BF16)
        rest = grads[chunk].shape[0] - 4 * D - router.shape[0]
        if rest:
            grads[chunk][4 * D + router.shape[0] :, :] = jnp.zeros((rest, width), BF16)
    biases[...] = jnp.broadcast_to(
        jnp.sum(d_project.astype(F32), axis=0, keepdims=True), biases.shape
    )
    return nt(d_project, weight)


def middle_pull_kernel(
    dims, s_ref, cot_ref, part_ref, near_ref, top_ref, rest_ref, middle_ref, norms_ref, normed_ref, mask_ref,
    projected_ref, attended_ref, router_ref, *refs,
):
    images, chunks = dims[0], dims[3]
    packs, outs, mask_pad = refs[:chunks], refs[chunks:-1], refs[-1]
    d_low, sums, d_branch_ref, biases = outs[:4]
    tokens = images * PAD
    normal, inv_std = normalize(middle_ref[...].astype(F32))
    d_normed2 = part_ref[...][:tokens].astype(F32) + near_ref[...][:tokens].astype(F32)
    d_normed2 = d_normed2 + jnp.concatenate([top_ref[...], rest_ref[...]], axis=0).astype(F32)
    d_middle = cot_ref[...].astype(F32) + norm_pull(d_normed2, normal, inv_std, norms_ref[2:3, :])
    d_branch = d_middle.astype(BF16)
    d_branch_ref[...] = d_branch
    sums[...] = jnp.concatenate(
        [
            jnp.sum(d_normed2 * normal, axis=0, keepdims=True),
            jnp.sum(d_normed2, axis=0, keepdims=True),
            jnp.sum(d_branch.astype(F32), axis=0, keepdims=True),
            jnp.zeros((5, D), F32),
        ],
        axis=0,
    )
    masks = key_masks(images, s_ref[0], mask_ref, mask_pad)
    d_low[...] = heads_pull(
        dims, s_ref, normed_ref[...], projected_ref, attended_ref, d_branch, packs, masks, router_ref,
        outs[4:], biases,
    ).astype(BF16)


def input_pull_kernel(
    dims, s_ref, x_ref, d_normed_ref, d_branch_ref, norms_ref, normed_ref, mask_ref,
    projected_ref, attended_ref, router_ref, *refs,
):
    images, chunks = dims[0], dims[3]
    packs, outs, mask_pad = refs[:chunks], refs[chunks:-1], refs[-1]
    d_inputs_ref, sums, biases = outs[:3]
    masks = key_masks(images, s_ref[0], mask_ref, mask_pad)
    d_normed = d_normed_ref[...].astype(F32) + heads_pull(
        dims, s_ref, normed_ref[...], projected_ref, attended_ref, d_branch_ref[...], packs, masks,
        router_ref, outs[3:], biases,
    )
    normal, inv_std = normalize(x_ref[...].astype(F32))
    d_inputs = d_branch_ref[...].astype(F32) + norm_pull(d_normed, normal, inv_std, norms_ref[0:1, :])
    d_inputs_ref[...] = d_inputs.astype(BF16)
    sums[...] = jnp.concatenate(
        [
            jnp.sum(d_normed * normal, axis=0, keepdims=True),
            jnp.sum(d_normed, axis=0, keepdims=True),
            jnp.sum(d_inputs * d_inputs * valid_column(images, masks), axis=0, keepdims=True),
            jnp.zeros((5, D), F32),
        ],
        axis=0,
    )


def expert_kernel(dims, s_ref, rows_in, *refs):
    chunks, pieces, hidden_width, width = dims
    ups_in, refs = refs[: chunks - 1], refs[chunks - 1 :]
    biases, refs = refs[:pieces], refs[pieces:]
    half = chunks // 2
    router_ref, back_bias_ref, w_in, w_back, *refs = refs
    blocks, refs = refs[: pieces - 1], refs[pieces - 1 :]
    hidden_out, d_pre_out, d_results, d_rows_out, mixed_out, router_grad, back_bias_out = refs[:7]
    (
        ups_wide, marks, in_weight, back_weight, in_bias, results, d_rows, sems
    ) = refs[7:]
    piece = pl.program_id(0)

    def weight_copies_of(k):
        slot = k % 2
        if k == 0:
            sources = w_in.at[s_ref[5]], w_back.at[s_ref[5]]
        else:
            block = blocks[k - 1]
            sources = block.at[pl.ds(0, D)], block.at[pl.ds(D, hidden_width)]
        return [
            pltpu.make_async_copy(sources[0], in_weight.at[slot], sems.at[0, slot]),
            pltpu.make_async_copy(sources[1], back_weight.at[slot], sems.at[1, slot]),
        ]

    def start(k):
        for copy in weight_copies_of(k):
            copy.start()

    expert, first = s_ref[1], s_ref[2]
    rows = rows_in[...]
    label = lax.broadcasted_iota(jnp.int32, (1, EXPERTS), 1)
    mine = label == expert

    @pl.when(piece == 0)
    def _():
        start(0)
        for chunk in range(chunks):
            at = pl.multiple_of(jnp.bitwise_xor(s_ref[3], chunk) * CAP, 8)
            if chunk == half - 1:
                came = ups_in[-1][UPS:, :].astype(F32)
            else:
                came = ups_in[chunk if chunk < half else chunk - 1][0:UPS, :].astype(F32)
            ups_wide[pl.ds(at, CAP), :D] = came[:CAP]
            column = jnp.transpose(came[CAP:, :LANES])[:CAP, 0:1]
            ups_wide[pl.ds(at, CAP), D:] = jnp.broadcast_to(column, (CAP, LANES))
        lines = hidden_width // width
        for k in range(pieces):
            block = biases[k][...].astype(F32)
            bias_rows = block[0:lines]
            for e in range(1, block.shape[0] // lines):
                here = block[e * lines : (e + 1) * lines]
                bias_rows = jnp.where(s_ref[5] == e, here, bias_rows)
            for line in range(lines):
                in_bias[k : k + 1, line * width : (line + 1) * width] = bias_rows[line : line + 1]
        other = ups_wide[:, D : D + 1]
        logits = nt(rows, router_ref[...])
        others = label.astype(F32) == other
        own_logit = jnp.sum(jnp.where(mine, logits, 0.0), axis=1, keepdims=True)
        other_logit = jnp.sum(jnp.where(others, logits, 0.0), axis=1, keepdims=True)
        peak = jnp.maximum(own_logit, other_logit)
        own_exp, other_exp = jnp.exp(own_logit - peak), jnp.exp(other_logit - peak)
        gate = own_exp / (own_exp + other_exp)
        other_gate = other_exp / (own_exp + other_exp)
        lane = lax.broadcasted_iota(jnp.int32, (1, LANES), 1)
        marks[...] = jnp.where(lane == 0, gate, other_gate)
        d_results[...] = (gate * ups_wide[:, :D]).astype(BF16)
        results[...] = jnp.zeros_like(results)
        d_rows[...] = jnp.zeros_like(d_rows)

    for k in range(pieces):
        @pl.when(piece == k)
        def _():
            for copy in weight_copies_of(k):
                copy.wait()
            if k + 1 < pieces:
                start(k + 1)

    slot = lax.rem(piece, 2)
    in_now, back_now = in_weight[slot], back_weight[slot]
    pre_act = nn(rows, in_now) + in_bias[pl.ds(piece, 1), :]
    cdf = 0.5 * (1.0 + lax.erf(pre_act * (0.5**0.5)))
    hidden = (pre_act * cdf).astype(BF16)
    hidden_out[0] = hidden
    results[...] += nn(hidden, back_now)
    slope = cdf + pre_act * jnp.exp(-0.5 * pre_act * pre_act) * 0.3989422804014327
    d_pre = (slope * nt(d_results[...], back_now)).astype(BF16)
    d_pre_out[0] = d_pre
    d_rows[...] += nt(d_pre, in_now)

    @pl.when(piece == pieces - 1)
    def _():
        gate, other_gate = marks[:, 0:1], marks[:, 1:2]
        others = label.astype(F32) == ups_wide[:, D : D + 1]
        bias = jnp.where(first > 0, 1.0, 0.0) * back_bias_ref[...].astype(F32)
        pick = (lax.broadcasted_iota(jnp.int32, (EXPERTS, 1), 0) == expert).astype(F32)
        total = results[...] + jnp.sum(pick * bias, axis=0, keepdims=True)
        d_gate = jnp.sum(ups_wide[:, :D] * total, axis=1, keepdims=True)
        moved = gate * other_gate * d_gate
        d_logits = jnp.where(mine, moved, jnp.where(others, -moved, 0.0)).astype(BF16)
        router_grad[...] = tn(d_logits, rows)
        back_bias_out[...] = jnp.broadcast_to(
            jnp.sum(d_results[...].astype(F32), axis=0, keepdims=True), back_bias_out.shape
        )
        d_rows_out[...] = (d_rows[...] + nn(d_logits, router_ref[...])).astype(BF16)
        mixed_out[...] = (gate * total).astype(BF16)


def expert_grads_kernel(pieces, cuts, s_ref, rows_ref, d_ref, hiddens, d_pres, *refs):
    grads, sums = refs[:-1], refs[-1]
    hidden_width = hiddens.shape[2]
    sums[...] = jnp.zeros_like(sums)
    rows, d_results = rows_ref[...], d_ref[...]

    def step(index, carry):
        piece = jnp.int32(pieces[0])
        for k in range(1, len(pieces)):
            piece = jnp.where(index == k, pieces[k], piece)
        d_pre = d_pres[piece]
        in_grad = tn(rows, d_pre)
        back_grad = tn(hiddens[piece], d_results)
        bias_grad = jnp.sum(d_pre.astype(F32), axis=0, keepdims=True)
        sums[1:2, :] += jnp.sum(in_grad * in_grad)
        sums[2:3, :] += jnp.sum(bias_grad * bias_grad)
        sums[3:4, :] += jnp.sum(back_grad * back_grad)
        parts = (in_grad, jnp.broadcast_to(bias_grad, (16, hidden_width)), back_grad)
        for k in range(len(pieces)):
            @pl.when(index == k)
            def _():
                at = 0
                for part in parts:
                    done = 0
                    while done < part.shape[0]:
                        place, start = 0, at
                        while start >= cuts[place]:
                            start -= cuts[place]
                            place += 1
                        size = min(part.shape[0] - done, cuts[place] - start)
                        grads[k * len(cuts) + place][start : start + size, :] = part[
                            done : done + size
                        ].astype(BF16)
                        done += size
                        at += size

        return carry

    lax.fori_loop(0, len(pieces), step, 0)


def mixture_kernel(s_ref, middle_ref, part_ref, near_ref, out_ref):
    tokens = middle_ref.shape[0]
    total = part_ref[...].astype(F32) + near_ref[...].astype(F32)
    out_ref[0:tokens, :] = (total[0:tokens] + middle_ref[...].astype(F32)).astype(BF16)
    out_ref[tokens:, :] = total[tokens:].astype(BF16)


def output_kernel(images, groups, s_ref, middle_ref, part_ref, mask_ref, *refs):
    fars, (out_ref, sums, mask_pad) = refs[: groups // 2 - 1], refs[groups // 2 - 1 :]
    tokens = images * PAD
    for r in range(0, groups, 2):
        total = part_ref[r // 2 * tokens : (r // 2 + 1) * tokens, :].astype(F32)
        for far, ref in enumerate(fars, 1):
            at = ((r // 2) ^ far) * tokens
            total = total + ref[at : at + tokens, :].astype(F32)
        out_ref[r // 2 * tokens : (r // 2 + 1) * tokens, :] = total.astype(BF16)
        if r == 0:
            output = total
    mixture = output - middle_ref[...].astype(F32)
    valid = valid_column(images, key_masks(images, s_ref[0], mask_ref, mask_pad))
    lane = lax.broadcasted_iota(jnp.int32, sums.shape, 1)
    sums[...] = jnp.where(
        lane == 2, jnp.sum(mixture * mixture * valid),
        jnp.where(lane == 3, jnp.sum(output * output * valid), 0.0),
    )


def place_tokens_kernel(count, images, places, s_ref, *refs):
    out, wide = refs[-2:]
    for group, (index, place) in enumerate(places):
        for image in range(images):
            start = (place * images + image) * PAD
            rows = refs[index][start : start + PAD, :].astype(F32)[:SEQ]
            at = jnp.bitwise_xor(s_ref[0], group) * images + image
            for k in range(D // LANES):
                wide[k, pl.ds(at, SEQ, stride=count), :] = rows[:, k * LANES : (k + 1) * LANES]
    for k in range(D // LANES):
        out[:, k * LANES : (k + 1) * LANES] = wide[k]


def place_experts_kernel(counts, first_row, s_ref, *refs):
    ins, outs = refs[: sum(counts)], refs[-1 if first_row else -2 :]
    height = outs[0].shape[1]
    at = 0
    for step, count in enumerate(counts):
        parts, at = ins[at : at + count], at + count

        @pl.when(pl.program_id(0) == step)
        def _():
            row = 0
            for part in parts:
                begin, end = max(first_row, row), min(first_row + height, row + part.shape[0])
                if begin < end:
                    outs[0][0, begin - first_row : end - first_row, :] = part[
                        begin - row : end - row, :
                    ].astype(F32)
                row += part.shape[0]
            if not first_row:
                bias = parts[0][height : height + 16, :].astype(F32)[0:1, :]
                outs[1][...] = jnp.broadcast_to(bias, outs[1].shape)


def split_kernel(chunks, s_ref, part_ref, near_ref, far_ref, out_ref):
    total = part_ref[...].astype(F32) + near_ref[...].astype(F32) + far_ref[...].astype(F32)
    share = total.shape[0] // chunks
    for chunk in range(chunks):
        out_ref[chunk] = total[chunk * share : (chunk + 1) * share].astype(BF16)


def join_kernel(dims, s_ref, pieces_ref, *refs):
    chunks, groups, half, width, small = dims
    norm1, norm2, forward, expert, back_bias, near_bias, far_bias = refs[:7]
    message, lines = refs[7:]
    total = pieces_ref[0].astype(F32)
    for chunk in range(1, chunks):
        total += pieces_ref[chunk].astype(F32)
    share = total.shape[0]
    row = lax.broadcasted_iota(jnp.int32, (share, 1), 0) + s_ref[3] * share
    squares = total * total
    lines[...] = jnp.zeros_like(lines)
    at = 0
    for source, index in ((norm1, 0), (norm1, 1), (norm2, 0), (norm2, 1), (norm2, 2)):
        lines[at : at + D // LANES, :] = as_lines(source[index : index + 1, :])
        at += D // LANES
    for part in (0, 2):
        for group in range(groups):
            biases, chunk = (near_bias, group) if group < half else (far_bias, group - half)
            line = biases[0:1, (3 * chunk + part) * width : (3 * chunk + part) * width + LANES]
            lines[pl.ds(at + jnp.bitwise_xor(s_ref[0], group), 1), :] = line
        at += groups
    lane = lax.broadcasted_iota(jnp.int32, (1, LANES), 1)
    terms = [
        jnp.sum(forward[0:1, :]),
        jnp.sum(forward[1:2, :]),
        0.0,
        0.0,
        jnp.sum(norm1[2:3, :]),
        jnp.sum(forward[2:3, :]) * (1.0 / D),
        jnp.sum(jnp.where(row < 3 * D, squares, 0.0)),
        jnp.sum(jnp.where((row >= 3 * D) & (row < 4 * D), squares, 0.0)),
        expert[1:2, 0:1],
        expert[2:3, 0:1],
        expert[3:4, 0:1],
    ]
    scalars = jnp.zeros((1, LANES), F32)
    for index, term in enumerate(terms):
        scalars = jnp.where(lane == index, term, scalars)
    lines[at : at + 1, :] = scalars
    lines[small - 8 : small - 8 + D // LANES, :] = as_lines(back_bias[0:1, :])
    values = lines[...]
    high = values.astype(BF16)
    low = (values - high.astype(F32)).astype(BF16)
    for chunk in range(chunks):
        message[chunk, 0:share, :] = total.astype(BF16)
        message[chunk, share : share + small, :] = high
        message[chunk, share + small :, :] = low


def spread_kernel(dims, s_ref, messages, outputs, qkv_out, out_out, sums, total):
    chunks, groups, width, small = dims
    share = messages.shape[1] - 2 * small
    summed = jnp.zeros((small, LANES), F32)
    at = small - 8
    for chunk in range(chunks):
        total[chunk * share : (chunk + 1) * share, :] = messages[chunk, 0:share, :].astype(F32)
        lines = messages[chunk, share : share + small, :].astype(F32) + messages[
            chunk, share + small :, :
        ].astype(F32)
        summed += lines
        sums[at : at + D // LANES, :] = lines[small - 8 : small - 8 + D // LANES]
        at += D // LANES
    sums[0 : small - 8, :] = summed[0 : small - 8]
    scalars = 5 * D // LANES + 2 * groups
    sums[scalars : scalars + 1, :] += outputs[0:1, :]
    per = EXPERTS // groups * (D // LANES)
    sums[at : at + per, :] = total[4 * D : 4 * D + per, :]
    qkv_out[...] = total[0 : 3 * D, :]
    for block in range(D // width):
        out_out[:, block * width : (block + 1) * width] = total[
            3 * D + block * width : 3 * D + (block + 1) * width, :
        ]


def finish_kernel(dims, s_ref, mine_ref, came_ref, *refs):
    chunks, groups, half, small, shared = dims
    gain1, shift1, gain2, shift2, out_bias, bias_out, router_out, back_out, norms_out, rms_out = refs
    per = D // LANES
    top = small - 8
    summed = mine_ref[0:top, :] + came_ref[0:top, :]
    squares = []
    for index, out in enumerate((gain1, shift1, gain2, shift2, out_bias)):
        block = summed[index * per : (index + 1) * per]
        squares.append(jnp.sum(block * block))
        out[...] = as_rows(block)
    at = 5 * per
    biases = summed[at : at + 2 * groups]
    place = lax.broadcasted_iota(jnp.int32, (groups, 1), 0) == s_ref[0]
    for part in range(2):
        lines = biases[part * groups : (part + 1) * groups]
        bias_out[part : part + 1, :] = jnp.sum(
            jnp.where(place, lines, 0.0), axis=0, keepdims=True
        )
    scalars = summed[at + 2 * groups : at + 2 * groups + 1]
    lane = lax.broadcasted_iota(jnp.int32, (1, LANES), 1)

    def scalar(index):
        return jnp.sum(jnp.where(lane == index, scalars, 0.0))

    share = EXPERTS // groups
    size = chunks * per + share * per
    for group in range(groups):
        source = mine_ref if group < half else came_ref
        start = top + (group if group < half else group - half) * size
        owner = jnp.bitwise_xor(s_ref[0], group)
        lane_expert = owner if shared else 0
        for chunk in range(chunks):
            line = as_rows(source[start + chunk * per : start + (chunk + 1) * per, :])
            back_out[pl.ds(chunk * s_ref[4] + lane_expert, 1), :] = line
        start += chunks * per
        router_rows = as_rows(source[start : start + share * per, :])
        for g in range(groups):
            @pl.when(owner == g)
            def _():
                router_out[g * share : (g + 1) * share, :] = router_rows
    router, back_bias = router_out[...], back_out[...]
    ordered = [
        squares[0], squares[1], scalar(6), jnp.sum(biases * biases), scalar(7), squares[4],
        squares[2], squares[3], jnp.sum(router * router), scalar(8), scalar(9), scalar(10),
        jnp.sum(back_bias * back_bias),
    ]
    norms = jnp.zeros((1, LANES), F32)
    for index, value in enumerate(ordered):
        norms = jnp.where(lane == index, value, norms)
    norms_out[...] = jnp.sqrt(norms)[:, :13]
    rms_out[...] = jnp.sqrt(scalars / (scalar(5) * D))[:, :5]


def shards(
    inputs, valid_mask, expert_ids, slot_ids, norm1_gain, norm1_bias, w_qkv, b_qv, w_out, b_out,
    norm2_gain, norm2_bias, w_router, w_in, b_in, w_back, b_back, cotangent, dp_size, tensor_size,
):
    count = inputs.shape[0]
    groups = tensor_size
    images = count // groups
    local_width = w_qkv.shape[2]
    heads = local_width // HD
    width = -(-local_width // LANES) * LANES
    local_experts, _, hidden_width = w_in.shape
    shared = local_experts == groups == 4
    pieces = groups if shared else 1
    chunks = dp_size
    rows = chunks * CAP
    own_tokens = images * PAD
    half = groups // 2
    data_at = lax.axis_index("dp").astype(jnp.int32)
    head_at = lax.axis_index("tensor").astype(jnp.int32)
    lane_expert = head_at if shared else jnp.int32(0)
    expert_at = data_at * local_experts + lane_expert
    first = jnp.int32(1) if shared else (head_at == 0).astype(jnp.int32)
    scalars = jnp.stack(
        [head_at, expert_at, first, data_at, jnp.int32(local_experts), lane_expert]
    )
    x_lines = jnp.transpose(inputs, (1, 0, 2)).reshape(SEQ * count, D)
    cot_lines = jnp.transpose(cotangent, (1, 0, 2)).reshape(SEQ * count, D)
    ids = jnp.transpose(expert_ids, (0, 2, 1))
    slots = jnp.transpose(slot_ids, (0, 2, 1))
    norms = jnp.stack([norm1_gain, norm1_bias, norm2_gain, norm2_bias, b_out]).astype(F32)
    router = jnp.transpose(w_router)
    last = [None]

    def call(kernel, ins, outs, **options):
        at = scalars if last[0] is None else after(scalars, last[0])
        got = run(kernel, at, ins, outs, **options)
        last[0] = got[0]
        return got

    def over(axis, size, value, by, *others):
        return swap(after(value, *others) if others else value, axis, size, by)

    def core(value, *others):
        return over("tensor", groups, value, 1, *others)

    def gather(value):
        parts = [value] + [None] * (groups - 1)
        for r in range(2, groups, 2):
            parts[r] = over("tensor", groups, value, r)
        for r in range(1, groups, 2):
            parts[r] = core(parts[r - 1])
        return parts

    def exchange(value, *others):
        value = after(value, *others) if others else value
        return lax.all_to_all(value.reshape(chunks, CAP, -1), "dp", 0, 0).reshape(rows, -1)

    fill = width - local_width
    qkv = jnp.pad(jnp.transpose(w_qkv, (1, 0, 2)), [(0, 0), (0, 0), (0, fill)])
    qkv = qkv.reshape(3 * D, width)
    out_rows = jnp.pad(w_out, [(0, fill), (0, 0)])
    qv_bias = jnp.pad(b_qv, [(0, 0), (0, fill)])
    bias_at = 4 * D + 16
    bias_lines = -(-(local_experts * hidden_width // width) // 16) * 16
    pack = call(
        functools.partial(pack_kernel, width),
        [qkv, out_rows, qv_bias, b_in], [((bias_at + bias_lines, width), BF16)], mib=58,
    )[0]
    packs = [pack, core(pack)] + [None] * (groups - 2)
    for r in range(2, groups, 2):
        packs[r] = over("tensor", groups, pack, r)

    block = D + hidden_width
    tall = D // LANES, SEQ * count, LANES
    got = call(
        functools.partial(start_kernel, (count, images, chunks, shared)),
        [ids, slots, cot_lines] + ([w_in, w_back] if shared else []),
        [((own_tokens, D), BF16)] + [((UPS, D), BF16)] * (chunks // 2)
        + [((chunks // 2 * UPS, D), BF16)]
        + (
            [((block, D), BF16)] * (pieces - 1) if shared else []
        ),
        left=(3, 4), mib=58,
        scratch=[
            pltpu.VMEM(tall, F32), pltpu.VMEM((own_tokens, D), F32),
            pltpu.VMEM((rows, D), F32), pltpu.VMEM((rows, LANES), F32),
            pltpu.VMEM((LANES, LANES), F32), pltpu.VMEM((chunks * UPS, D), F32),
            pltpu.SemaphoreType.DMA((6,)),
        ],
    )
    cot_own, ups, up_far = got[0], got[1 : 1 + chunks // 2], got[1 + chunks // 2]
    up_far = over("dp", chunks, up_far, chunks // 2)
    if shared:
        weights = [got[-3], over("tensor", groups, got[-2], 2), got[-1]]
    else:
        weights = []
    for r in range(2, groups, 2):
        packs[r + 1] = core(packs[r], cot_own)

    mask_pad = pltpu.VMEM((8, WIDE), jnp.int32)
    x_own, normed1, normed2, middle, forward_sums, projected, attended = call(
        functools.partial(heads_kernel, count, images, heads, width, groups),
        [x_lines, norms, valid_mask, *packs],
        [((own_tokens, D), BF16)] * 4 + [((8, D), F32)]
        + [((own_tokens, groups * 3 * width), BF16), ((own_tokens, groups * width), BF16)],
        scratch=[pltpu.VMEM(tall, F32), pltpu.VMEM((own_tokens, D), F32), mask_pad], mib=MIB_HEADS,
        stream=True,
    )
    half_heads = {
        which: [
            pl.BlockSpec((own_tokens, half * size * width), lambda step, s, at=which: (0, at))
            for size in (3, 1)
        ]
        for which in (0, 1)
    }

    tokens = [normed2, core(normed2)] + [None] * (groups - 2)
    early = chunks // 2 - 1
    ups = list(ups)
    for r in range(1, early):
        ups[r] = over("dp", chunks, ups[r], r, normed2)
    for r in range(2, groups, 2):
        tokens[r] = over("tensor", groups, normed2, r)
    turn = [up_far, *ups[1:early]]
    if shared:
        turn.append(weights[1])
    for r in range(2, groups, 2):
        tokens[r + 1] = core(tokens[r], *turn)
    if shared:
        weights[2] = over("tensor", groups, weights[2], 3, tokens[2])
        weights[0] = core(weights[0], tokens[2])
    flat_pad = pltpu.VMEM((8, WIDE), jnp.int32)
    sent, *passed = call(
        functools.partial(dispatch_kernel, groups, images, chunks),
        [ids, slots, *tokens, up_far, ups[early]],
        [((rows, D), BF16)] + [((UPS, D), BF16)] * (early - 1) + [((2 * UPS, D), BF16)],
        scratch=[flat_pad],
    )
    dispatched = exchange(sent)
    passed = [over("dp", chunks, value, r) for r, value in enumerate(passed, 1)]
    ups = [*ups[:early], up_far, *passed]

    by_piece = pl.BlockSpec((1, rows, hidden_width), lambda step, s: (step, 0, 0))
    bias_spec = pl.BlockSpec((bias_lines, width), lambda step, s: (bias_at // bias_lines, 0))
    first_rows = pl.BlockSpec((UPS, D), lambda step, s: (0, 0))
    before = chunks
    hidden, d_pre, d_results, d_sent, mixed_sent, router_part, back_bias = call(
        functools.partial(expert_kernel, (chunks, pieces, hidden_width, width)),
        [dispatched, *ups, *packs[:pieces], router, b_back, w_in, w_back]
        + weights,
        [((pieces, rows, hidden_width), BF16)] * 2 + [((rows, D), BF16)] * 3
        + [((EXPERTS, D), F32), ((8, D), F32)],
        grid=(pieces,),
        in_specs={chunks // 2: first_rows, **{before + k: bias_spec for k in range(pieces)}},
        out_specs={0: by_piece, 1: by_piece},
        scratch=[
            pltpu.VMEM((rows, D + LANES), F32),
            pltpu.VMEM((rows, LANES), F32),
            pltpu.VMEM((2, D, hidden_width), BF16),
            pltpu.VMEM((2, hidden_width, D), BF16),
            pltpu.VMEM((8, hidden_width), F32),
            pltpu.VMEM((rows, D), F32),
            pltpu.VMEM((rows, D), F32),
            pltpu.SemaphoreType.DMA((2, 2)),
        ],
        left=range(before + pieces + 2, before + pieces + 4 + pieces), mib=61,
    )
    d_back = exchange(d_sent)
    tall_grad = D + 16 + hidden_width
    first_cut = -(-2 * tall_grad // 48) * 16
    plans = [((3,), (first_cut, tall_grad - first_cut)), ((2, 0, 1), (tall_grad,))]
    if not shared:
        plans = [((0,), (D + 16, hidden_width))]
    lane_counts = (D, D) if shared else (hidden_width, D)
    grads, expert_sums = {}, []
    for kept, cuts in plans:
        part = pl.BlockSpec(
            (1 if len(kept) == 1 else 3, rows, hidden_width),
            lambda step, s, at=kept[0] if len(kept) == 1 else 0: (at, 0, 0),
        )
        held = tuple(range(len(kept))) if len(kept) == 1 else kept
        *some, sums = call(
            functools.partial(expert_grads_kernel, held, cuts),
            [dispatched, d_results, hidden, d_pre],
            [((cut, wide), BF16) for cut, wide in zip(cuts, lane_counts)] * len(kept)
            + [((8, LANES), F32)],
            in_specs={2: part, 3: part}, mib=58,
        )
        for index, piece in enumerate(kept):
            grads[piece] = some[index * len(cuts) : (index + 1) * len(cuts)]
        expert_sums.append(sums)

    def combine(value):
        return call(
            functools.partial(combine_kernel, groups, images, chunks),
            [ids, slots, value],
            [((half * own_tokens, D), BF16)] * 2, scratch=[flat_pad],
        )

    def reduce_own(keep, send, size, *others):
        came = core(send)
        far = [None, None]
        for r in range(2, groups, 2):
            for part in range(2):
                start = r // 2 * size + part * (size // 2)
                span = slice(start, start + size // 2)
                out = (keep[span].astype(F32) + came[span].astype(F32)).astype(BF16)
                term = over("tensor", groups, out, r, *others)
                if far[part] is not None:
                    term = far[part].astype(F32) + term.astype(F32)
                far[part] = term
        return keep, came, far

    if shared:
        last_top = over("tensor", groups, grads[3][0], 2)
        d_back = after(d_back, last_top)
    d_keep, d_near, d_far = reduce_own(*combine(d_back), own_tokens)
    if shared:
        last_rest = over("tensor", groups, grads[3][1], 2, *d_far)
    mixed = exchange(mixed_sent, d_back)

    router_lines = EXPERTS // groups * (D // LANES)
    share = -(-(4 * D + router_lines) // (16 * chunks)) * 16

    def grads_out(parts):
        return [((8, parts * 3 * width), F32)] + [((chunks * share, width), BF16)] * parts

    first_half = pl.BlockSpec((own_tokens, D), lambda step, s: (0, 0))
    got = call(
        functools.partial(
            middle_pull_kernel, (images, heads, width, groups - half, half, groups)
        ),
        [cot_own, d_keep, d_near, *d_far, middle, norms, normed1, valid_mask, projected,
         attended, router_part, *packs[half:]],
        [((own_tokens, D), BF16), ((8, D), F32), ((own_tokens, D), BF16)]
        + grads_out(groups - half),
        scratch=[mask_pad], mib=MIB_PULL, in_specs={**dict(zip((9, 10), half_heads[1])), 1: first_half, 2: first_half},
    )
    d_low, norm2_sums, d_branch, far_bias = got[:4]
    far_grads = list(got[4:])

    def add_odd(grads):
        return (grads[0].astype(F32) + core(grads[1]).astype(F32)).astype(BF16)

    if shared:
        far_grads[1] = after(far_grads[1], last_rest)
    far = None
    for r in range(0, groups - half, 2):
        out = add_odd(far_grads[r : r + 2])
        d_low = after(d_low, out)
        term = over("tensor", groups, out, half + r)
        far = term if far is None else far.astype(F32) + term.astype(F32)
    got = call(
        functools.partial(input_pull_kernel, (images, heads, width, half, 0, groups)),
        [x_own, d_low, d_branch, norms, normed1, valid_mask, projected, attended,
         router_part, *packs[:half]],
        [((own_tokens, D), BF16), ((8, D), F32)] + grads_out(half),
        scratch=[mask_pad], mib=MIB_PULL, in_specs=dict(zip((6, 7), half_heads[0])),
    )
    d_own, norm1_sums, near_bias = got[:3]
    head_grads = list(got[3:])
    for r in range(2, half, 2):
        term = over("tensor", groups, add_odd(head_grads[r : r + 2]), r)
        far = far.astype(F32) + term.astype(F32)
    near = core(head_grads[1], far)
    split = call(
        functools.partial(split_kernel, chunks),
        [head_grads[0], near, far], [((chunks, share, width), BF16)],
    )[0]
    d_tokens = [d_own, core(d_own)] + [None] * (groups - 2)
    for r in range(2, groups, 2):
        d_tokens[r] = over("tensor", groups, d_own, r)
    pieces_in = lax.all_to_all(after(split, d_tokens[2]), "dp", 0, 0)
    mix_keep, mix_send = combine(mixed)
    mix_near = core(mix_send)

    def place_tokens(parts, places):
        placed = call(
            functools.partial(place_tokens_kernel, count, images, places),
            parts, [((SEQ * count, D), F32)],
            scratch=[pltpu.VMEM(tall, F32)],
        )[0]
        return jnp.transpose(placed.reshape(SEQ, count, D), (1, 0, 2))

    for r in range(2, groups, 2):
        d_tokens[r + 1] = core(d_tokens[r], split)

    def place_experts(came, pieces_here, first_row, shape, before=()):
        steps = len(pieces_here)

        def piece_at(step):
            place = jnp.int32(0)
            for index, piece in enumerate(pieces_here):
                place = jnp.where(step == index, piece, place)
            return place

        spec = pl.BlockSpec((1, *shape), lambda step, s: (jnp.bitwise_xor(s[0], piece_at(step)), 0, 0))
        lines = pl.BlockSpec((1, 8, hidden_width), lambda step, s: (step, 0, 0))
        parts = [a for piece in came for a in piece]
        bias = [] if first_row else [((steps, 8, hidden_width), F32)]
        return call(
            functools.partial(
                place_experts_kernel, tuple(len(piece) for piece in came), first_row
            ),
            [*parts, *before], [((local_experts, *shape), F32)] + bias,
            grid=(steps,), out_specs={0: spec, 1: lines}, left=range(len(parts), len(parts) + 1),
            aliases={len(parts): 0} if before else None,
        )

    mix = call(
        mixture_kernel, [middle, mix_keep, mix_near], [((half * own_tokens, D), BF16)]
    )[0]
    mix_far = [over("tensor", groups, mix, r) for r in range(2, groups, 2)]
    d_inputs = place_tokens(d_tokens, [(r, 0) for r in range(groups)])
    if shared:
        whole = (0, 1, 3), [grads[0], [core(grads[1][0])], [core(last_top), core(last_rest)]]
        g_w_in, lines_in = place_experts(whole[1], whole[0], 0, (D, hidden_width))
        (g_w_back,) = place_experts(whole[1], whole[0], D + 16, (hidden_width, D))
    small = -(-(5 * D // LANES + 2 * groups + 1) // 8) * 8 + 8
    small = -(-small // 16) * 16
    message = call(
        functools.partial(join_kernel, (chunks, groups, half, width, small)),
        [pieces_in, norm1_sums, norm2_sums, forward_sums, sum(expert_sums), back_bias, near_bias,
         far_bias],
        [((chunks, share + 2 * small, width), BF16)], scratch=[pltpu.VMEM((small, LANES), F32)],
        mib=58,
    )[0]
    messages = lax.all_to_all(message, "dp", 0, 0)
    output_own, output_sums = call(
        functools.partial(output_kernel, images, groups),
        [middle, mix, valid_mask, *mix_far],
        [((half * own_tokens, D), BF16), ((8, LANES), F32)], scratch=[mask_pad],
    )
    by = 1
    while by < chunks:
        output_sums = output_sums + over("dp", chunks, output_sums, by)
        by *= 2
    out_near = core(output_own)

    output = place_tokens([output_own, out_near], [(r % 2, r // 2) for r in range(groups)])
    top = small - 8
    qkv_sum, out_sum, sums = call(
        functools.partial(spread_kernel, (chunks, groups, width, small)),
        [messages, output_sums],
        [((3 * D, width), F32), ((width, D), F32),
         ((top + chunks * (D // LANES) + router_lines, LANES), F32)],
        scratch=[pltpu.VMEM((chunks * share, width), F32)],
    )
    by = 1
    while True:
        came = over("tensor", groups, sums, by)
        by *= 2
        if by == groups:
            break
        sums = jnp.concatenate([sums[:top] + came[:top], sums[top:], came[top:]], axis=0)

    if shared:
        last_piece = [[over("tensor", groups, grads[2][0], 2, mix_far[0])]]
        g_w_in, line_in = place_experts(last_piece, (2,), 0, (D, hidden_width), [g_w_in])
        (g_w_back,) = place_experts(last_piece, (2,), D + 16, (hidden_width, D), [g_w_back])
        by_piece = jnp.concatenate([lines_in[:2, 0], line_in[:, 0], lines_in[2:, 0]], axis=0)
        order = jnp.bitwise_xor(head_at, jnp.arange(groups, dtype=jnp.int32))
        g_b_in = jnp.take(by_piece, order, axis=0)
    else:
        g_w_in = grads[0][0][None, :D].astype(F32)
        g_w_back = grads[0][1][None].astype(F32)
        g_b_in = grads[0][0][D : D + 1].astype(F32)

    vector = [((1, D), F32)]
    (
        g_norm1_gain, g_norm1_bias, g_norm2_gain, g_norm2_bias, g_b_out, g_b_qv, router_grad,
        g_b_back, grad_norms, rms_values,
    ) = call(
        functools.partial(finish_kernel, (chunks, groups, half, small, shared)),
        [sums, came],
        vector * 5
        + [((2, LANES), F32), ((EXPERTS, D), F32), ((EXPERTS, D), F32)]
        + [((1, 13), F32), ((1, 5), F32)],
    )
    g_w_qkv = jnp.transpose(qkv_sum.reshape(3, D, width), (1, 0, 2))[:, :, :local_width]
    return (
        output, d_inputs, g_norm1_gain[0], g_norm1_bias[0], g_w_qkv, g_b_qv[:, :local_width],
        out_sum[:local_width], g_b_out[0], g_norm2_gain[0], g_norm2_bias[0],
        jnp.transpose(router_grad), g_w_in, g_b_in, g_w_back, g_b_back,
        grad_norms[0], rms_values[0],
    )


def solution(mesh):
    placed = (
        P("dp", None, None),
        P("dp", None),
        P("dp", None, None),
        P("dp", None, None),
        P(),
        P(),
        P(None, None, "tensor"),
        P(None, "tensor"),
        P("tensor", None),
        P(),
        P(),
        P(),
        P(),
        P("dp", None, "tensor"),
        P("dp", "tensor"),
        P("dp", "tensor", None),
        P(),
        P("dp", None, None),
    )
    return jax.shard_map(
        functools.partial(shards, dp_size=mesh.shape["dp"], tensor_size=mesh.shape["tensor"]),
        mesh=mesh,
        in_specs=placed,
        out_specs=(
            P("dp", None, None),
            P("dp", None, None),
            P(),
            P(),
            P(None, None, "tensor"),
            P(None, "tensor"),
            P("tensor", None),
            P(),
            P(),
            P(),
            P(),
            P("dp", None, "tensor"),
            P("dp", "tensor"),
            P("dp", "tensor", None),
            P(),
            P(),
            P(),
        ),
        check_vma=False,
    )
```

```python
import functools

import jax
import jax.numpy as jnp
from jax import lax
from jax.experimental import pallas as pl
from jax.experimental.pallas import tpu as pltpu
from jax.sharding import PartitionSpec as P

D = 512
HD = 64
EXPERTS = 32
SEQ = 197
CAP = 104
PAD = 208
UPS = CAP + 8
WIDE = 256
MIB_HEADS = 52
MIB_EXPERT = 58
MIB_GRADS = 58
MIB_PULL = 58
LANES = 128
F32 = jnp.float32
BF16 = jnp.bfloat16


def nn(a, b):
    return lax.dot_general(a, b, (((1,), (0,)), ((), ())), preferred_element_type=F32)


def nt(a, b):
    return lax.dot_general(a, b, (((1,), (1,)), ((), ())), preferred_element_type=F32)


def tn(a, b):
    return lax.dot_general(a, b, (((0,), (0,)), ((), ())), preferred_element_type=F32)


def swap(value, axis, size, by):
    return lax.ppermute(value, axis, [(at, at ^ by) for at in range(size)])


def after(value, *others):
    return lax.optimization_barrier((value, *others))[0]


class Held:
    def __init__(self, ref, copy):
        self.ref, self.copy, self.there = ref, copy, False
        self.shape, self.dtype = ref.shape, ref.dtype

    def __getitem__(self, index):
        if not self.there:
            self.copy.wait()
            self.there = True
        return self.ref[index]


class Sent:
    def __init__(self, ref, copy):
        self.ref, self.copy, self.left = ref, copy, False
        self.shape, self.dtype = ref.shape, ref.dtype

    def __getitem__(self, index):
        return self.ref[index]

    def __setitem__(self, index, value):
        self.ref[index] = value

    def send(self):
        if not self.left:
            self.copy.start()
            self.left = True


def streamed(kernel, ins, outs, scratch):
    shapes = [(a.shape, a.dtype) for a in ins] + list(outs)

    def body(s_ref, *refs):
        far, refs = refs[: len(shapes)], refs[len(shapes) :]
        near, refs, sems = refs[: len(shapes)], refs[len(shapes) : -1], refs[-1]
        held = []
        for i in range(len(ins)):
            copy = pltpu.make_async_copy(far[i], near[i], sems.at[i])
            copy.start()
            held.append(Held(near[i], copy))
        sent = [
            Sent(near[i], pltpu.make_async_copy(near[i], far[i], sems.at[i]))
            for i in range(len(ins), len(shapes))
        ]
        kernel(s_ref, *held, *sent, *refs)
        for value in held:
            if not value.there:
                value.copy.wait()
        for value in sent:
            value.send()
        for value in sent:
            value.copy.wait()

    buffers = [pltpu.VMEM(shape, dtype) for shape, dtype in shapes]
    return body, [*buffers, *scratch, pltpu.SemaphoreType.DMA((len(shapes),))]


def run(
    kernel, scalars, ins, outs, scratch=(), grid=(1,), in_specs=None, out_specs=None, mib=28, left=(),
    stream=False, aliases=None, near=(),
):
    in_specs, out_specs = in_specs or {}, out_specs or {}
    if len(near) == len(outs):
        ins = [pltpu.with_memory_space_constraint(a, pltpu.HBM) for a in ins]
    if stream:
        kernel, scratch = streamed(kernel, ins, outs, scratch)
        left = range(len(ins))
        out_specs = {i: pl.BlockSpec(memory_space=pl.ANY) for i in range(len(outs))}

    def whole(shape, stays=False):
        if stays:
            return pl.BlockSpec(memory_space=pl.ANY)
        return pl.BlockSpec(shape, lambda step, s, nd=len(shape): (0,) * nd)

    return pl.pallas_call(
        kernel,
        grid_spec=pltpu.PrefetchScalarGridSpec(
            num_scalar_prefetch=1,
            grid=grid,
            in_specs=[
                in_specs[i] if i in in_specs else whole(a.shape, i in left)
                for i, a in enumerate(ins)
            ],
            out_specs=[out_specs[i] if i in out_specs else whole(o[0]) for i, o in enumerate(outs)],
            scratch_shapes=list(scratch),
        ),
        out_shape=[
            (pltpu.VMEM if i in near else pltpu.HBM if near else jax.ShapeDtypeStruct)(*out)
            for i, out in enumerate(outs)
        ],
        input_output_aliases={i + 1: o for i, o in (aliases or {}).items()},
        compiler_params=pltpu.CompilerParams(vmem_limit_bytes=mib * 2**20),
        cost_estimate=pl.CostEstimate(flops=0, bytes_accessed=0, transcendentals=0),
    )(scalars, *ins)


def route_rows(ids_ref, slots_ref, image):
    ids, slots = ids_ref[image], slots_ref[image]
    return jnp.where(slots < CAP, ids * CAP + slots, -1)


def block_start(s_ref, chunk):
    return (chunk * s_ref[4] + s_ref[5]) * CAP


def target_column(s_ref, chunks):
    rows = lax.broadcasted_iota(jnp.int32, (CAP, 1), 0)
    starts = [block_start(s_ref, chunk) for chunk in range(chunks)]
    return jnp.concatenate([rows + start for start in starts], axis=0)


def target_row(s_ref, chunks):
    lanes = lax.broadcasted_iota(jnp.int32, (1, chunks * CAP), 1)
    target = lanes
    for chunk in range(chunks):
        here = (lanes >= chunk * CAP) & (lanes < (chunk + 1) * CAP)
        target = jnp.where(here, lanes + (block_start(s_ref, chunk) - chunk * CAP), target)
    return target


def spread(source_ref, wide_ref, count):
    for k in range(D // LANES):
        wide_ref[k] = source_ref[:, k * LANES : (k + 1) * LANES].astype(F32)

    def image_rows(image):
        return jnp.concatenate(
            [wide_ref[k, pl.ds(image, SEQ, stride=count), :] for k in range(D // LANES)], axis=1
        )

    return image_rows


def own_rows(images, me, image_rows, out_ref, padded):
    padded[...] = jnp.zeros_like(padded)
    for image in range(images):
        padded[image * PAD : image * PAD + SEQ, :] = image_rows(me * images + image)
    out_ref[...] = padded[...].astype(BF16)


def pack_kernel(width, s_ref, qkv_ref, out_ref, bias_ref, in_bias_ref, pack):
    pack[0 : 3 * D, :] = qkv_ref[...]
    for block in range(D // width):
        at = 3 * D + block * width
        pack[at : at + width, :] = out_ref[:, block * width : (block + 1) * width]
    bias = bias_ref[...].astype(F32)
    experts, hidden = in_bias_ref.shape
    lines = in_bias_ref[...].astype(F32)
    lines = [
        lines[e : e + 1, k * width : (k + 1) * width]
        for e in range(experts)
        for k in range(hidden // width)
    ]
    fill = -len(lines) % 16
    if fill:
        lines.append(jnp.zeros((fill, width), F32))
    pack[4 * D :, :] = jnp.concatenate(
        [bias[0:1], bias[1:2], jnp.zeros((14, width), F32), *lines], axis=0
    ).astype(BF16)


def start_kernel(dims, s_ref, ids_ref, slots_ref, cot_ref, *refs):
    count, images, chunks, shared = dims
    copies = []
    if shared:
        w_in, w_back, *refs = refs
    own, *refs = refs
    near_outs, far_out, refs = refs[: chunks // 2], refs[chunks // 2], refs[chunks // 2 + 1 :]
    if shared:
        *laid, refs = *refs[:3], refs[3:]
    wide, padded, blocks, marks, square, wholes, sems = refs
    if shared:
        hidden = w_back.shape[1]
        for r, target in enumerate(laid, 1):
            expert = jnp.bitwise_xor(s_ref[0], r)
            for side, (source, place) in enumerate(
                ((w_in, pl.ds(0, D)), (w_back, pl.ds(D, hidden)))
            ):
                copies.append(
                    pltpu.make_async_copy(
                        source.at[expert], target.at[place], sems.at[2 * r - 2 + side]
                    )
                )
    for copy in copies:
        copy.start()
    image_rows = spread(cot_ref, wide, count)
    target = target_column(s_ref, chunks)
    rows = chunks * CAP
    blocks[...] = jnp.zeros_like(blocks)
    marks[...] = jnp.zeros_like(marks)

    def step(pair, carry):
        total = jnp.zeros((rows, D), F32)
        others = jnp.zeros((rows, SEQ), F32)
        for image in (2 * pair, 2 * pair + 1):
            flat = route_rows(ids_ref, slots_ref, image)
            ids = ids_ref[image].astype(F32)
            first = target == flat[0:1, :]
            second = target == flat[1:2, :]
            hit = (first | second).astype(F32).astype(BF16)
            total += nn(hit, image_rows(image).astype(BF16))
            others += jnp.where(first, ids[1:2, :], 0.0) + jnp.where(second, ids[0:1, :], 0.0)
        blocks[...] += total
        marks[...] += jnp.broadcast_to(jnp.sum(others, axis=1, keepdims=True), marks.shape)
        return carry

    lax.fori_loop(0, count // 2, step, 0)
    square[...] = jnp.zeros_like(square)
    wholes[...] = jnp.zeros_like(wholes)
    for chunk in range(chunks):
        at = pl.multiple_of(jnp.bitwise_xor(s_ref[3], chunk) * CAP, 8)
        place = chunk * UPS
        wholes[place : place + CAP, :] = blocks[pl.ds(at, CAP), :]
        square[0:CAP, :] = marks[pl.ds(at, CAP), :]
        wholes[place + CAP : place + UPS, 0:LANES] = jnp.transpose(square[...])[0:8, :]
    for chunk, near_out in enumerate(near_outs):
        near_out[...] = wholes[chunk * UPS : (chunk + 1) * UPS, :].astype(BF16)
    far_out[...] = wholes[chunks // 2 * UPS :, :].astype(BF16)
    own_rows(images, s_ref[0], image_rows, own, padded)
    for copy in copies:
        copy.wait()


def padded_routes(ids_ref, slots_ref, image, flat_ref):
    flat_ref[...] = jnp.full(flat_ref.shape, -1, jnp.int32)
    flat_ref[0:2, 0:SEQ] = route_rows(ids_ref, slots_ref, image)
    return flat_ref[...]


def dispatch_kernel(groups, images, chunks, s_ref, ids_ref, slots_ref, *refs):
    tokens, (far, late, out, *passed, flat_ref) = refs[:groups], refs[groups:]
    for chunk, on in enumerate(passed, 1):
        on[0:UPS, :] = far[chunk * UPS : (chunk + 1) * UPS, :]
    passed[-1][UPS:, :] = late[...]
    me = s_ref[0]
    target = target_column(s_ref, chunks)
    total = jnp.zeros((chunks * CAP, D), F32)
    for group in range(groups):
        for image in range(images):
            at = jnp.bitwise_xor(me, group) * images + image
            flat = padded_routes(ids_ref, slots_ref, at, flat_ref)[:, :PAD]
            hit = (target == flat[0:1, :]) | (target == flat[1:2, :])
            total += nn(
                hit.astype(F32).astype(BF16), tokens[group][image * PAD : (image + 1) * PAD, :]
            )
    out[...] = total.astype(BF16)


def combine_kernel(groups, images, chunks, s_ref, ids_ref, slots_ref, rows_ref, *refs):
    outs, flat_ref = refs[:2], refs[2]
    me = s_ref[0]
    rows = rows_ref[...]
    target = target_row(s_ref, chunks)

    def step(pair, carry):
        for odd in range(2):
            for image in range(images):
                at = jnp.bitwise_xor(me, 2 * pair + odd) * images + image
                flat = jnp.transpose(padded_routes(ids_ref, slots_ref, at, flat_ref))[:PAD, :]
                hit = (flat[:, 0:1] == target) | (flat[:, 1:2] == target)
                place = pl.multiple_of((pair * images + image) * PAD, 16)
                outs[odd][pl.ds(place, PAD), :] = nn(
                    hit.astype(F32).astype(BF16), rows
                ).astype(BF16)
        return carry

    lax.fori_loop(0, groups // 2, step, 0)


def chunk_weights(packs, width):
    qkv = [p[part * D : (part + 1) * D, :] for p in packs for part in range(3)]
    biases = []
    for p in packs:
        lines = p[3 * D + D : 3 * D + D + 16, :].astype(F32)
        biases += [lines[0:1], jnp.zeros((1, width), F32), lines[1:2]]
    outs = [
        jnp.concatenate(
            [p[3 * D + b * width : 3 * D + (b + 1) * width, :] for b in range(D // width)], axis=1
        )
        for p in packs
    ]
    return (
        jnp.concatenate(qkv, axis=1),
        jnp.concatenate(biases, axis=1),
        jnp.concatenate(outs, axis=0),
    )


def normalize(values):
    average = jnp.mean(values, axis=-1, keepdims=True)
    centered = values - average
    inv_std = lax.rsqrt(jnp.mean(centered * centered, axis=-1, keepdims=True) + 1e-06)
    return centered * inv_std, inv_std


def norm_pull(upstream, normal, inv_std, gain):
    scaled = upstream * gain
    inner = jnp.mean(scaled * normal, axis=-1, keepdims=True)
    return inv_std * (scaled - jnp.mean(scaled, axis=-1, keepdims=True) - normal * inner)


def key_masks(images, me, mask_ref, pad_ref):
    pad_ref[...] = jnp.full(pad_ref.shape, -1, jnp.int32)
    for image in range(images):
        pad_ref[image : image + 1, 0:SEQ] = mask_ref[pl.ds(me * images + image, 1), :]
    return pad_ref[...]


def valid_column(images, masks):
    columns = jnp.transpose(jnp.maximum(masks, 0).astype(F32))
    return jnp.concatenate([columns[:PAD, i : i + 1] for i in range(images)], axis=0)


def probabilities_of(queries, key_rows, key_mask):
    shift = jnp.where(key_mask > 0, 0.0, jnp.where(key_mask < 0, -2e30, -1e30))
    scores = nt(queries * jnp.asarray(HD ** (-0.5), BF16), key_rows) + shift
    exps = jnp.exp(scores - jnp.max(scores, axis=-1, keepdims=True))
    return exps * (1.0 / jnp.sum(exps, axis=-1, keepdims=True))


def by_head(rows, heads):
    zeros = jnp.zeros_like(rows)
    width = rows.shape[1]
    return jnp.concatenate(
        [jnp.where(head_lanes(width, head), rows, zeros) for head in range(heads)], axis=0
    )


def own_lanes(stacked, heads):
    result = stacked[:PAD]
    for head in range(1, heads):
        lanes = head_lanes(stacked.shape[1], head)
        result = jnp.where(lanes, stacked[head * PAD : (head + 1) * PAD], result)
    return result


def head_lanes(width, head):
    lane = lax.broadcasted_iota(jnp.int32, (1, width), 1)
    return (lane >= head * HD) & (lane < (head + 1) * HD)


def attend(images, heads, width, chunks, normed, weight, bias, masks, projected_ref):
    projected = (nn(normed, weight) + bias).astype(BF16)
    projected_ref[...] = projected
    projected_ref.send()
    parts = []
    for image in range(images):
        key_mask = masks[image : image + 1, :PAD]
        line = []
        for chunk in range(chunks):
            queries, key_rows, values = (
                projected[
                    image * PAD : (image + 1) * PAD,
                    (3 * chunk + part) * width : (3 * chunk + part + 1) * width,
                ]
                for part in range(3)
            )
            own = by_head(queries, heads)
            probabilities = probabilities_of(own, key_rows, key_mask)
            mixed = own_lanes(nn(probabilities.astype(BF16), values), heads)
            line.append(mixed.astype(BF16))
        parts.append(jnp.concatenate(line, axis=1))
    return projected, jnp.concatenate(parts, axis=0)


def heads_kernel(count, images, heads, width, chunks, s_ref, x_ref, norms_ref, mask_ref, *refs):
    packs, outs = refs[:chunks], refs[chunks : chunks + 7]
    wide, padded, mask_pad = refs[-3:]
    x_own, normed_ref, normed2_ref, middle_ref, sums, projected_ref, attended_ref = outs
    own_rows(images, s_ref[0], spread(x_ref, wide, count), x_own, padded)
    x_own.send()
    stream = padded[...]
    normal, _ = normalize(stream)
    normed = (normal * norms_ref[0:1, :] + norms_ref[1:2, :]).astype(BF16)
    normed_ref[...] = normed
    normed_ref.send()
    masks = key_masks(images, s_ref[0], mask_ref, mask_pad)
    weight, bias, out_weight = chunk_weights(packs, width)
    projected, attended = attend(
        images, heads, width, chunks, normed, weight, bias, masks, projected_ref
    )
    attended_ref[...] = attended
    attended_ref.send()
    branch = nn(attended, out_weight) + norms_ref[4:5, :]
    middle = stream + branch
    normal, _ = normalize(middle)
    normed2_ref[...] = (normal * norms_ref[2:3, :] + norms_ref[3:4, :]).astype(BF16)
    normed2_ref.send()
    middle_ref[...] = middle.astype(BF16)
    middle_ref.send()
    valid = valid_column(images, masks)
    sums[...] = jnp.concatenate(
        [
            jnp.sum(middle * middle * valid, axis=0, keepdims=True),
            jnp.sum(branch * branch * valid, axis=0, keepdims=True),
            jnp.broadcast_to(jnp.sum(valid, axis=0, keepdims=True), (1, D)),
            jnp.zeros((5, D), F32),
        ],
        axis=0,
    )


def as_lines(rows):
    return jnp.concatenate([rows[:, k * LANES : (k + 1) * LANES] for k in range(D // LANES)], axis=0)


def as_rows(lines):
    count = lines.shape[0] // (D // LANES)
    return jnp.concatenate(
        [lines[k * count : (k + 1) * count] for k in range(D // LANES)], axis=1
    )


def attend_pull(images, heads, width, chunks, projected_ref, d_attended, masks):
    parts = []
    for image in range(images):
        span = slice(image * PAD, (image + 1) * PAD)
        key_mask = masks[image : image + 1, :PAD]
        line = []
        for chunk in range(chunks):
            queries, key_rows, values = (
                projected_ref[span, (3 * chunk + part) * width : (3 * chunk + part + 1) * width]
                for part in range(3)
            )
            d_mixed = d_attended[span, chunk * width : (chunk + 1) * width]
            own = by_head(queries, heads)
            d_own = by_head(d_mixed, heads)
            probabilities = probabilities_of(own, key_rows, key_mask)
            d_probs = nt(d_own, values)
            row_dots = jnp.sum(d_probs * probabilities, axis=-1, keepdims=True)
            d_scores = probabilities * (d_probs - row_dots)
            d_scores = jnp.where(key_mask > 0, d_scores, 0.0).astype(BF16)
            d_values = tn(probabilities.astype(BF16), d_own)
            d_queries = own_lanes(nn(d_scores, key_rows), heads)
            d_keys = tn(d_scores, own)
            line += [d_queries * HD ** (-0.5), d_keys * HD ** (-0.5), d_values]
        parts.append(jnp.concatenate(line, axis=1).astype(BF16))
    return jnp.concatenate(parts, axis=0)


def heads_pull(
    dims, s_ref, normed, projected_ref, attended_ref, d_branch, packs, masks, router_ref, grads, biases
):
    images, heads, width, chunks, start, groups = dims
    weight, _, out_weight = chunk_weights(packs, width)
    d_attended = nt(d_branch, out_weight).astype(BF16)
    d_project = attend_pull(images, heads, width, chunks, projected_ref, d_attended, masks)
    grad = tn(normed, d_project)
    out_grad = tn(attended_ref[...], d_branch)
    for chunk in range(chunks):
        for part in range(3):
            at = (3 * chunk + part) * width
            grads[chunk][part * D : (part + 1) * D, :] = grad[:, at : at + width].astype(BF16)
        for block in range(D // width):
            at = 3 * D + block * width
            grads[chunk][at : at + width, :] = out_grad[
                chunk * width : (chunk + 1) * width, block * width : (block + 1) * width
            ].astype(BF16)
        per = EXPERTS // groups
        owner = jnp.bitwise_xor(s_ref[0], start + chunk)
        router = router_ref[0:per, :]
        for g in range(1, groups):
            router = jnp.where(owner == g, router_ref[g * per : (g + 1) * per, :], router)
        router = as_lines(router)
        grads[chunk][4 * D : 4 * D + router.shape[0], :] = router.astype(BF16)
        rest = grads[chunk].shape[0] - 4 * D - router.shape[0]
        if rest:
            grads[chunk][4 * D + router.shape[0] :, :] = jnp.zeros((rest, width), BF16)
    biases[...] = jnp.broadcast_to(
        jnp.sum(d_project.astype(F32), axis=0, keepdims=True), biases.shape
    )
    return nt(d_project, weight)


def middle_pull_kernel(
    dims, s_ref, cot_ref, part_ref, near_ref, top_ref, rest_ref, middle_ref, norms_ref, normed_ref, mask_ref,
    projected_ref, attended_ref, router_ref, *refs,
):
    images, chunks = dims[0], dims[3]
    packs, outs, mask_pad = refs[:chunks], refs[chunks:-1], refs[-1]
    d_low, sums, d_branch_ref, biases = outs[:4]
    tokens = images * PAD
    normal, inv_std = normalize(middle_ref[...].astype(F32))
    d_normed2 = part_ref[...][:tokens].astype(F32) + near_ref[...][:tokens].astype(F32)
    d_normed2 = d_normed2 + jnp.concatenate([top_ref[...], rest_ref[...]], axis=0).astype(F32)
    d_middle = cot_ref[...].astype(F32) + norm_pull(d_normed2, normal, inv_std, norms_ref[2:3, :])
    d_branch = d_middle.astype(BF16)
    d_branch_ref[...] = d_branch
    sums[...] = jnp.concatenate(
        [
            jnp.sum(d_normed2 * normal, axis=0, keepdims=True),
            jnp.sum(d_normed2, axis=0, keepdims=True),
            jnp.sum(d_branch.astype(F32), axis=0, keepdims=True),
            jnp.zeros((5, D), F32),
        ],
        axis=0,
    )
    masks = key_masks(images, s_ref[0], mask_ref, mask_pad)
    d_low[...] = heads_pull(
        dims, s_ref, normed_ref[...], projected_ref, attended_ref, d_branch, packs, masks, router_ref,
        outs[4:], biases,
    ).astype(BF16)


def input_pull_kernel(
    dims, s_ref, x_ref, d_normed_ref, d_branch_ref, norms_ref, normed_ref, mask_ref,
    projected_ref, attended_ref, router_ref, *refs,
):
    images, chunks = dims[0], dims[3]
    packs, outs, mask_pad = refs[:chunks], refs[chunks:-1], refs[-1]
    d_inputs_ref, sums, biases = outs[:3]
    masks = key_masks(images, s_ref[0], mask_ref, mask_pad)
    d_normed = d_normed_ref[...].astype(F32) + heads_pull(
        dims, s_ref, normed_ref[...], projected_ref, attended_ref, d_branch_ref[...], packs, masks,
        router_ref, outs[3:], biases,
    )
    normal, inv_std = normalize(x_ref[...].astype(F32))
    d_inputs = d_branch_ref[...].astype(F32) + norm_pull(d_normed, normal, inv_std, norms_ref[0:1, :])
    d_inputs_ref[...] = d_inputs.astype(BF16)
    sums[...] = jnp.concatenate(
        [
            jnp.sum(d_normed * normal, axis=0, keepdims=True),
            jnp.sum(d_normed, axis=0, keepdims=True),
            jnp.sum(d_inputs * d_inputs * valid_column(images, masks), axis=0, keepdims=True),
            jnp.zeros((5, D), F32),
        ],
        axis=0,
    )


def expert_kernel(dims, s_ref, rows_in, *refs):
    chunks, pieces, hidden_width, width = dims
    ups_in, refs = refs[: chunks - 1], refs[chunks - 1 :]
    biases, refs = refs[:pieces], refs[pieces:]
    half = chunks // 2
    router_ref, back_bias_ref, w_in, w_back, *refs = refs
    blocks, refs = refs[: pieces - 1], refs[pieces - 1 :]
    hidden_out, d_pre_out, d_results, d_rows_out, mixed_out, router_grad, back_bias_out = refs[:7]
    (
        ups_wide, marks, in_weight, back_weight, in_bias, results, d_rows, sems
    ) = refs[7:]
    piece = pl.program_id(0)

    def weight_copies_of(k):
        slot = k % 2
        if k == 0:
            sources = w_in.at[s_ref[5]], w_back.at[s_ref[5]]
        else:
            block = blocks[k - 1]
            sources = block.at[pl.ds(0, D)], block.at[pl.ds(D, hidden_width)]
        return [
            pltpu.make_async_copy(sources[0], in_weight.at[slot], sems.at[0, slot]),
            pltpu.make_async_copy(sources[1], back_weight.at[slot], sems.at[1, slot]),
        ]

    def start(k):
        for copy in weight_copies_of(k):
            copy.start()

    expert, first = s_ref[1], s_ref[2]
    rows = rows_in[...]
    label = lax.broadcasted_iota(jnp.int32, (1, EXPERTS), 1)
    mine = label == expert

    @pl.when(piece == 0)
    def _():
        start(0)
        for chunk in range(chunks):
            at = pl.multiple_of(jnp.bitwise_xor(s_ref[3], chunk) * CAP, 8)
            if chunk == half - 1:
                came = ups_in[-1][UPS:, :].astype(F32)
            else:
                came = ups_in[chunk if chunk < half else chunk - 1][0:UPS, :].astype(F32)
            ups_wide[pl.ds(at, CAP), :D] = came[:CAP]
            column = jnp.transpose(came[CAP:, :LANES])[:CAP, 0:1]
            ups_wide[pl.ds(at, CAP), D:] = jnp.broadcast_to(column, (CAP, LANES))
        lines = hidden_width // width
        for k in range(pieces):
            block = biases[k][...].astype(F32)
            bias_rows = block[0:lines]
            for e in range(1, block.shape[0] // lines):
                here = block[e * lines : (e + 1) * lines]
                bias_rows = jnp.where(s_ref[5] == e, here, bias_rows)
            for line in range(lines):
                in_bias[k : k + 1, line * width : (line + 1) * width] = bias_rows[line : line + 1]
        other = ups_wide[:, D : D + 1]
        logits = nt(rows, router_ref[...])
        others = label.astype(F32) == other
        own_logit = jnp.sum(jnp.where(mine, logits, 0.0), axis=1, keepdims=True)
        other_logit = jnp.sum(jnp.where(others, logits, 0.0), axis=1, keepdims=True)
        peak = jnp.maximum(own_logit, other_logit)
        own_exp, other_exp = jnp.exp(own_logit - peak), jnp.exp(other_logit - peak)
        gate = own_exp / (own_exp + other_exp)
        other_gate = other_exp / (own_exp + other_exp)
        lane = lax.broadcasted_iota(jnp.int32, (1, LANES), 1)
        marks[...] = jnp.where(lane == 0, gate, other_gate)
        d_results[...] = (gate * ups_wide[:, :D]).astype(BF16)
        results[...] = jnp.zeros_like(results)
        d_rows[...] = jnp.zeros_like(d_rows)

    for k in range(pieces):
        @pl.when(piece == k)
        def _():
            for copy in weight_copies_of(k):
                copy.wait()
            if k + 1 < pieces:
                start(k + 1)

    slot = lax.rem(piece, 2)
    in_now, back_now = in_weight[slot], back_weight[slot]
    pre_act = nn(rows, in_now) + in_bias[pl.ds(piece, 1), :]
    cdf = 0.5 * (1.0 + lax.erf(pre_act * (0.5**0.5)))
    hidden = (pre_act * cdf).astype(BF16)
    hidden_out[0] = hidden
    results[...] += nn(hidden, back_now)
    slope = cdf + pre_act * jnp.exp(-0.5 * pre_act * pre_act) * 0.3989422804014327
    d_pre = (slope * nt(d_results[...], back_now)).astype(BF16)
    d_pre_out[0] = d_pre
    d_rows[...] += nt(d_pre, in_now)

    @pl.when(piece == pieces - 1)
    def _():
        gate, other_gate = marks[:, 0:1], marks[:, 1:2]
        others = label.astype(F32) == ups_wide[:, D : D + 1]
        bias = jnp.where(first > 0, 1.0, 0.0) * back_bias_ref[...].astype(F32)
        pick = (lax.broadcasted_iota(jnp.int32, (EXPERTS, 1), 0) == expert).astype(F32)
        total = results[...] + jnp.sum(pick * bias, axis=0, keepdims=True)
        d_gate = jnp.sum(ups_wide[:, :D] * total, axis=1, keepdims=True)
        moved = gate * other_gate * d_gate
        d_logits = jnp.where(mine, moved, jnp.where(others, -moved, 0.0)).astype(BF16)
        router_grad[...] = tn(d_logits, rows)
        back_bias_out[...] = jnp.broadcast_to(
            jnp.sum(d_results[...].astype(F32), axis=0, keepdims=True), back_bias_out.shape
        )
        d_rows_out[...] = (d_rows[...] + nn(d_logits, router_ref[...])).astype(BF16)
        mixed_out[...] = (gate * total).astype(BF16)


def expert_grads_kernel(pieces, cuts, s_ref, rows_ref, d_ref, hiddens, d_pres, *refs):
    grads, sums = refs[:-1], refs[-1]
    hidden_width = hiddens.shape[2]
    sums[...] = jnp.zeros_like(sums)
    rows, d_results = rows_ref[...], d_ref[...]

    def step(index, carry):
        piece = jnp.int32(pieces[0])
        for k in range(1, len(pieces)):
            piece = jnp.where(index == k, pieces[k], piece)
        d_pre = d_pres[piece]
        in_grad = tn(rows, d_pre)
        back_grad = tn(hiddens[piece], d_results)
        bias_grad = jnp.sum(d_pre.astype(F32), axis=0, keepdims=True)
        sums[1:2, :] += jnp.sum(in_grad * in_grad)
        sums[2:3, :] += jnp.sum(bias_grad * bias_grad)
        sums[3:4, :] += jnp.sum(back_grad * back_grad)
        parts = (in_grad, jnp.broadcast_to(bias_grad, (16, hidden_width)), back_grad)
        first = 0
        for k, heights in enumerate(cuts):
            arrays, first = grads[first : first + len(heights)], first + len(heights)

            @pl.when(index == k)
            def _():
                at = 0
                for part in parts:
                    done = 0
                    while done < part.shape[0]:
                        place, start = 0, at
                        while start >= heights[place]:
                            start -= heights[place]
                            place += 1
                        size = min(part.shape[0] - done, heights[place] - start)
                        arrays[place][start : start + size, :] = part[done : done + size].astype(BF16)
                        done += size
                        at += size

        return carry

    lax.fori_loop(0, len(pieces), step, 0)


def mixture_kernel(s_ref, middle_ref, part_ref, near_ref, out_ref):
    tokens = middle_ref.shape[0]
    total = part_ref[...].astype(F32) + near_ref[...].astype(F32)
    out_ref[0:tokens, :] = (total[0:tokens] + middle_ref[...].astype(F32)).astype(BF16)
    out_ref[tokens:, :] = total[tokens:].astype(BF16)


def output_kernel(images, groups, s_ref, middle_ref, part_ref, mask_ref, *refs):
    fars, (out_ref, sums, mask_pad) = refs[: groups // 2 - 1], refs[groups // 2 - 1 :]
    tokens = images * PAD
    for r in range(0, groups, 2):
        total = part_ref[r // 2 * tokens : (r // 2 + 1) * tokens, :].astype(F32)
        for far, ref in enumerate(fars, 1):
            at = ((r // 2) ^ far) * tokens
            total = total + ref[at : at + tokens, :].astype(F32)
        out_ref[r // 2 * tokens : (r // 2 + 1) * tokens, :] = total.astype(BF16)
        if r == 0:
            output = total
    mixture = output - middle_ref[...].astype(F32)
    valid = valid_column(images, key_masks(images, s_ref[0], mask_ref, mask_pad))
    lane = lax.broadcasted_iota(jnp.int32, sums.shape, 1)
    sums[...] = jnp.where(
        lane == 2, jnp.sum(mixture * mixture * valid),
        jnp.where(lane == 3, jnp.sum(output * output * valid), 0.0),
    )


def place_tokens_kernel(count, images, places, s_ref, *refs):
    out, wide = refs[-2:]
    for group, (index, place) in enumerate(places):
        for image in range(images):
            start = (place * images + image) * PAD
            rows = refs[index][start : start + PAD, :].astype(F32)[:SEQ]
            at = jnp.bitwise_xor(s_ref[0], group) * images + image
            for k in range(D // LANES):
                wide[k, pl.ds(at, SEQ, stride=count), :] = rows[:, k * LANES : (k + 1) * LANES]
    for k in range(D // LANES):
        out[:, k * LANES : (k + 1) * LANES] = wide[k]


def place_experts_kernel(counts, first_row, s_ref, *refs):
    ins, outs = refs[: sum(counts)], refs[-1 if first_row else -2 :]
    lines = None if first_row or len(counts) > 1 else refs[sum(counts)]
    height = outs[0].shape[1]
    at = 0
    for step, count in enumerate(counts):
        parts, at = ins[at : at + count], at + count

        @pl.when(pl.program_id(0) == step)
        def _():
            row = 0
            for part in parts:
                begin, end = max(first_row, row), min(first_row + height, row + part.shape[0])
                if begin < end:
                    outs[0][0, begin - first_row : end - first_row, :] = part[
                        begin - row : end - row, :
                    ].astype(F32)
                row += part.shape[0]
            if not first_row:
                bias = parts[0][height : height + 16, :].astype(F32)[0:1, :]
                if lines is None:
                    outs[1][...] = jnp.broadcast_to(bias, outs[1].shape)
                else:
                    for index, piece in enumerate((0, 1, 3)):
                        owner = jnp.bitwise_xor(s_ref[0], piece)
                        outs[1][pl.ds(owner, 1), :] = lines[index, 0:1, :]
                    outs[1][pl.ds(jnp.bitwise_xor(s_ref[0], 2), 1), :] = bias


def split_kernel(chunks, s_ref, part_ref, near_ref, far_ref, out_ref):
    total = part_ref[...].astype(F32) + near_ref[...].astype(F32) + far_ref[...].astype(F32)
    share = total.shape[0] // chunks
    for chunk in range(chunks):
        out_ref[chunk] = total[chunk * share : (chunk + 1) * share].astype(BF16)


def join_kernel(dims, s_ref, pieces_ref, *refs):
    chunks, groups, half, width, small = dims
    norm1, norm2, forward, expert, back_bias, near_bias, far_bias = refs[:7]
    message, lines = refs[7:]
    total = pieces_ref[0].astype(F32)
    for chunk in range(1, chunks):
        total += pieces_ref[chunk].astype(F32)
    share = total.shape[0]
    row = lax.broadcasted_iota(jnp.int32, (share, 1), 0) + s_ref[3] * share
    squares = total * total
    lines[...] = jnp.zeros_like(lines)
    at = 0
    for source, index in ((norm1, 0), (norm1, 1), (norm2, 0), (norm2, 1), (norm2, 2)):
        lines[at : at + D // LANES, :] = as_lines(source[index : index + 1, :])
        at += D // LANES
    for part in (0, 2):
        for group in range(groups):
            biases, chunk = (near_bias, group) if group < half else (far_bias, group - half)
            line = biases[0:1, (3 * chunk + part) * width : (3 * chunk + part) * width + LANES]
            lines[pl.ds(at + jnp.bitwise_xor(s_ref[0], group), 1), :] = line
        at += groups
    lane = lax.broadcasted_iota(jnp.int32, (1, LANES), 1)
    terms = [
        jnp.sum(forward[0:1, :]),
        jnp.sum(forward[1:2, :]),
        0.0,
        0.0,
        jnp.sum(norm1[2:3, :]),
        jnp.sum(forward[2:3, :]) * (1.0 / D),
        jnp.sum(jnp.where(row < 3 * D, squares, 0.0)),
        jnp.sum(jnp.where((row >= 3 * D) & (row < 4 * D), squares, 0.0)),
        expert[1:2, 0:1],
        expert[2:3, 0:1],
        expert[3:4, 0:1],
    ]
    scalars = jnp.zeros((1, LANES), F32)
    for index, term in enumerate(terms):
        scalars = jnp.where(lane == index, term, scalars)
    lines[at : at + 1, :] = scalars
    lines[small - 8 : small - 8 + D // LANES, :] = as_lines(back_bias[0:1, :])
    values = lines[...]
    high = values.astype(BF16)
    low = (values - high.astype(F32)).astype(BF16)
    for chunk in range(chunks):
        message[chunk, 0:share, :] = total.astype(BF16)
        message[chunk, share : share + small, :] = high
        message[chunk, share + small :, :] = low


def spread_kernel(dims, s_ref, messages, outputs, qkv_out, out_out, sums, total):
    chunks, groups, width, small = dims
    share = messages.shape[1] - 2 * small
    summed = jnp.zeros((small, LANES), F32)
    at = small - 8
    for chunk in range(chunks):
        total[chunk * share : (chunk + 1) * share, :] = messages[chunk, 0:share, :].astype(F32)
        lines = messages[chunk, share : share + small, :].astype(F32) + messages[
            chunk, share + small :, :
        ].astype(F32)
        summed += lines
        sums[at : at + D // LANES, :] = lines[small - 8 : small - 8 + D // LANES]
        at += D // LANES
    sums[0 : small - 8, :] = summed[0 : small - 8]
    scalars = 5 * D // LANES + 2 * groups
    sums[scalars : scalars + 1, :] += outputs[0:1, :]
    per = EXPERTS // groups * (D // LANES)
    sums[at : at + per, :] = total[4 * D : 4 * D + per, :]
    qkv_out[...] = total[0 : 3 * D, :]
    for block in range(D // width):
        out_out[:, block * width : (block + 1) * width] = total[
            3 * D + block * width : 3 * D + (block + 1) * width, :
        ]


def finish_kernel(dims, s_ref, mine_ref, came_ref, *refs):
    chunks, groups, half, small, shared = dims
    gain1, shift1, gain2, shift2, out_bias, bias_out, router_out, back_out, norms_out, rms_out = refs
    per = D // LANES
    top = small - 8
    summed = mine_ref[0:top, :] + came_ref[0:top, :]
    squares = []
    for index, out in enumerate((gain1, shift1, gain2, shift2, out_bias)):
        block = summed[index * per : (index + 1) * per]
        squares.append(jnp.sum(block * block))
        out[...] = as_rows(block)
    at = 5 * per
    biases = summed[at : at + 2 * groups]
    place = lax.broadcasted_iota(jnp.int32, (groups, 1), 0) == s_ref[0]
    for part in range(2):
        lines = biases[part * groups : (part + 1) * groups]
        bias_out[part : part + 1, :] = jnp.sum(
            jnp.where(place, lines, 0.0), axis=0, keepdims=True
        )
    scalars = summed[at + 2 * groups : at + 2 * groups + 1]
    lane = lax.broadcasted_iota(jnp.int32, (1, LANES), 1)

    def scalar(index):
        return jnp.sum(jnp.where(lane == index, scalars, 0.0))

    share = EXPERTS // groups
    size = chunks * per + share * per
    for group in range(groups):
        source = mine_ref if group < half else came_ref
        start = top + (group if group < half else group - half) * size
        owner = jnp.bitwise_xor(s_ref[0], group)
        lane_expert = owner if shared else 0
        for chunk in range(chunks):
            line = as_rows(source[start + chunk * per : start + (chunk + 1) * per, :])
            back_out[pl.ds(chunk * s_ref[4] + lane_expert, 1), :] = line
        start += chunks * per
        router_rows = as_rows(source[start : start + share * per, :])
        for g in range(groups):
            @pl.when(owner == g)
            def _():
                router_out[g * share : (g + 1) * share, :] = router_rows
    router, back_bias = router_out[...], back_out[...]
    ordered = [
        squares[0], squares[1], scalar(6), jnp.sum(biases * biases), scalar(7), squares[4],
        squares[2], squares[3], jnp.sum(router * router), scalar(8), scalar(9), scalar(10),
        jnp.sum(back_bias * back_bias),
    ]
    norms = jnp.zeros((1, LANES), F32)
    for index, value in enumerate(ordered):
        norms = jnp.where(lane == index, value, norms)
    norms_out[...] = jnp.sqrt(norms)[:, :13]
    rms_out[...] = jnp.sqrt(scalars / (scalar(5) * D))[:, :5]


def shards(
    inputs, valid_mask, expert_ids, slot_ids, norm1_gain, norm1_bias, w_qkv, b_qv, w_out, b_out,
    norm2_gain, norm2_bias, w_router, w_in, b_in, w_back, b_back, cotangent, dp_size, tensor_size,
):
    count = inputs.shape[0]
    groups = tensor_size
    images = count // groups
    local_width = w_qkv.shape[2]
    heads = local_width // HD
    width = -(-local_width // LANES) * LANES
    local_experts, _, hidden_width = w_in.shape
    shared = local_experts == groups == 4
    pieces = groups if shared else 1
    chunks = dp_size
    rows = chunks * CAP
    own_tokens = images * PAD
    half = groups // 2
    data_at = lax.axis_index("dp").astype(jnp.int32)
    head_at = lax.axis_index("tensor").astype(jnp.int32)
    lane_expert = head_at if shared else jnp.int32(0)
    expert_at = data_at * local_experts + lane_expert
    first = jnp.int32(1) if shared else (head_at == 0).astype(jnp.int32)
    scalars = jnp.stack(
        [head_at, expert_at, first, data_at, jnp.int32(local_experts), lane_expert]
    )
    x_lines = jnp.transpose(inputs, (1, 0, 2)).reshape(SEQ * count, D)
    cot_lines = jnp.transpose(cotangent, (1, 0, 2)).reshape(SEQ * count, D)
    ids = jnp.transpose(expert_ids, (0, 2, 1))
    slots = jnp.transpose(slot_ids, (0, 2, 1))
    norms = jnp.stack([norm1_gain, norm1_bias, norm2_gain, norm2_bias, b_out]).astype(F32)
    router = jnp.transpose(w_router)
    last = [None]

    def call(kernel, ins, outs, **options):
        at = scalars if last[0] is None else after(scalars, last[0])
        got = run(kernel, at, ins, outs, **options)
        last[0] = got[0]
        return got

    def over(axis, size, value, by, *others):
        return swap(after(value, *others) if others else value, axis, size, by)

    def core(value, *others):
        return over("tensor", groups, value, 1, *others)

    def gather(value):
        parts = [value] + [None] * (groups - 1)
        for r in range(2, groups, 2):
            parts[r] = over("tensor", groups, value, r)
        for r in range(1, groups, 2):
            parts[r] = core(parts[r - 1])
        return parts

    def exchange(value, *others):
        value = after(value, *others) if others else value
        return lax.all_to_all(value.reshape(chunks, CAP, -1), "dp", 0, 0).reshape(rows, -1)

    fill = width - local_width
    qkv = jnp.pad(jnp.transpose(w_qkv, (1, 0, 2)), [(0, 0), (0, 0), (0, fill)])
    qkv = qkv.reshape(3 * D, width)
    out_rows = jnp.pad(w_out, [(0, fill), (0, 0)])
    qv_bias = jnp.pad(b_qv, [(0, 0), (0, fill)])
    bias_at = 4 * D + 16
    bias_lines = -(-(local_experts * hidden_width // width) // 16) * 16
    pack = call(
        functools.partial(pack_kernel, width),
        [qkv, out_rows, qv_bias, b_in], [((bias_at + bias_lines, width), BF16)], mib=48, near=(0,),
    )[0]
    packs = [pack, core(pack)] + [None] * (groups - 2)
    for r in range(2, groups, 2):
        packs[r] = over("tensor", groups, pack, r)

    block = D + hidden_width
    tall = D // LANES, SEQ * count, LANES
    got = call(
        functools.partial(start_kernel, (count, images, chunks, shared)),
        [ids, slots, cot_lines] + ([w_in, w_back] if shared else []),
        [((own_tokens, D), BF16)] + [((UPS, D), BF16)] * (chunks // 2)
        + [((chunks // 2 * UPS, D), BF16)]
        + (
            [((block, D), BF16)] * (pieces - 1) if shared else []
        ),
        left=(3, 4), mib=58,
        scratch=[
            pltpu.VMEM(tall, F32), pltpu.VMEM((own_tokens, D), F32),
            pltpu.VMEM((rows, D), F32), pltpu.VMEM((rows, LANES), F32),
            pltpu.VMEM((LANES, LANES), F32), pltpu.VMEM((chunks * UPS, D), F32),
            pltpu.SemaphoreType.DMA((6,)),
        ],
    )
    cot_own, ups, up_far = got[0], got[1 : 1 + chunks // 2], got[1 + chunks // 2]
    up_far = over("dp", chunks, up_far, chunks // 2)
    if shared:
        weights = [got[-3], over("tensor", groups, got[-2], 2), got[-1]]
    else:
        weights = []
    for r in range(2, groups, 2):
        packs[r + 1] = core(packs[r], cot_own)

    mask_pad = pltpu.VMEM((8, WIDE), jnp.int32)
    x_own, normed1, normed2, middle, forward_sums, projected, attended = call(
        functools.partial(heads_kernel, count, images, heads, width, groups),
        [x_lines, norms, valid_mask, *packs],
        [((own_tokens, D), BF16)] * 4 + [((8, D), F32)]
        + [((own_tokens, groups * 3 * width), BF16), ((own_tokens, groups * width), BF16)],
        scratch=[pltpu.VMEM(tall, F32), pltpu.VMEM((own_tokens, D), F32), mask_pad], mib=MIB_HEADS,
        stream=True, near=(2,),
    )
    half_heads = {
        which: [
            pl.BlockSpec((own_tokens, half * size * width), lambda step, s, at=which: (0, at))
            for size in (3, 1)
        ]
        for which in (0, 1)
    }

    tokens = [normed2, core(normed2)] + [None] * (groups - 2)
    early = chunks // 2 - 1
    ups = list(ups)
    for r in range(1, early):
        ups[r] = over("dp", chunks, ups[r], r, normed2)
    for r in range(2, groups, 2):
        tokens[r] = over("tensor", groups, normed2, r)
    turn = [up_far, *ups[1:early]]
    if shared:
        turn.append(weights[1])
    for r in range(2, groups, 2):
        tokens[r + 1] = core(tokens[r], *turn)
    if shared:
        weights[2] = over("tensor", groups, weights[2], 3, tokens[2])
        weights[0] = core(weights[0], tokens[2])
    flat_pad = pltpu.VMEM((8, WIDE), jnp.int32)
    sent, *passed = call(
        functools.partial(dispatch_kernel, groups, images, chunks),
        [ids, slots, *tokens, up_far, ups[early]],
        [((rows, D), BF16)] + [((UPS, D), BF16)] * (early - 1) + [((2 * UPS, D), BF16)],
        scratch=[flat_pad],
    )
    dispatched = exchange(sent)
    passed = [over("dp", chunks, value, r) for r, value in enumerate(passed, 1)]
    ups = [*ups[:early], up_far, *passed]

    by_piece = pl.BlockSpec((1, rows, hidden_width), lambda step, s: (step, 0, 0))
    bias_spec = pl.BlockSpec((bias_lines, width), lambda step, s: (bias_at // bias_lines, 0))
    first_rows = pl.BlockSpec((UPS, D), lambda step, s: (0, 0))
    before = chunks
    hidden, d_pre, d_results, d_sent, mixed_sent, router_part, back_bias = call(
        functools.partial(expert_kernel, (chunks, pieces, hidden_width, width)),
        [dispatched, *ups, *packs[:pieces], router, b_back, w_in, w_back]
        + weights,
        [((pieces, rows, hidden_width), BF16)] * 2 + [((rows, D), BF16)] * 3
        + [((EXPERTS, D), F32), ((8, D), F32)],
        grid=(pieces,),
        in_specs={chunks // 2: first_rows, **{before + k: bias_spec for k in range(pieces)}},
        out_specs={0: by_piece, 1: by_piece},
        scratch=[
            pltpu.VMEM((rows, D + LANES), F32),
            pltpu.VMEM((rows, LANES), F32),
            pltpu.VMEM((2, D, hidden_width), BF16),
            pltpu.VMEM((2, hidden_width, D), BF16),
            pltpu.VMEM((8, hidden_width), F32),
            pltpu.VMEM((rows, D), F32),
            pltpu.VMEM((rows, D), F32),
            pltpu.SemaphoreType.DMA((2, 2)),
        ],
        left=range(before + pieces + 2, before + pieces + 4 + pieces), mib=61,
    )
    d_back = exchange(d_sent)
    tall_grad = D + 16 + hidden_width
    first_cut = -(-2 * tall_grad // 48) * 16
    two = first_cut, tall_grad - first_cut
    most = tall_grad - 160, 160
    plans = [((3,), (two,)), ((2, 0, 1), (most, (tall_grad,), (tall_grad,)))]
    if not shared:
        plans = [((0,), ((D + 16, hidden_width),))]
    lane_counts = (D, D) if shared else (hidden_width, D)
    grads, expert_sums = {}, []
    for kept, cuts in plans:
        part = pl.BlockSpec(
            (1 if len(kept) == 1 else 3, rows, hidden_width),
            lambda step, s, at=kept[0] if len(kept) == 1 else 0: (at, 0, 0),
        )
        held = tuple(range(len(kept))) if len(kept) == 1 else kept
        *some, sums = call(
            functools.partial(expert_grads_kernel, held, cuts),
            [dispatched, d_results, hidden, d_pre],
            [((cut, wide), BF16) for heights in cuts for cut, wide in zip(heights, lane_counts)]
            + [((8, LANES), F32)],
            in_specs={2: part, 3: part}, mib=58,
        )
        for piece, heights in zip(kept, cuts):
            grads[piece], some = some[: len(heights)], some[len(heights) :]
        expert_sums.append(sums)

    def combine(value):
        return call(
            functools.partial(combine_kernel, groups, images, chunks),
            [ids, slots, value],
            [((half * own_tokens, D), BF16)] * 2, scratch=[flat_pad],
        )

    def reduce_own(keep, send, size, *others):
        came = core(send)
        far = [None, None]
        for r in range(2, groups, 2):
            for part in range(2):
                start = r // 2 * size + part * (size // 2)
                span = slice(start, start + size // 2)
                out = (keep[span].astype(F32) + came[span].astype(F32)).astype(BF16)
                term = over("tensor", groups, out, r, *others)
                if far[part] is not None:
                    term = far[part].astype(F32) + term.astype(F32)
                far[part] = term
        return keep, came, far

    if shared:
        last_top = over("tensor", groups, grads[3][0], 2)
        d_back = after(d_back, last_top)
    d_keep, d_near, d_far = reduce_own(*combine(d_back), own_tokens)
    if shared:
        last_rest = over("tensor", groups, grads[3][1], 2, *d_far)
    mixed = exchange(mixed_sent, d_back)

    router_lines = EXPERTS // groups * (D // LANES)
    share = -(-(4 * D + router_lines) // (16 * chunks)) * 16

    def grads_out(parts):
        return [((8, parts * 3 * width), F32)] + [((chunks * share, width), BF16)] * parts

    first_half = pl.BlockSpec((own_tokens, D), lambda step, s: (0, 0))
    got = call(
        functools.partial(
            middle_pull_kernel, (images, heads, width, groups - half, half, groups)
        ),
        [cot_own, d_keep, d_near, *d_far, middle, norms, normed1, valid_mask, projected,
         attended, router_part, *packs[half:]],
        [((own_tokens, D), BF16), ((8, D), F32), ((own_tokens, D), BF16)]
        + grads_out(groups - half),
        scratch=[mask_pad], mib=MIB_PULL, in_specs={**dict(zip((9, 10), half_heads[1])), 1: first_half, 2: first_half},
    )
    d_low, norm2_sums, d_branch, far_bias = got[:4]
    far_grads = list(got[4:])

    def add_odd(grads):
        return (grads[0].astype(F32) + core(grads[1]).astype(F32)).astype(BF16)

    if shared:
        far_grads[1] = after(far_grads[1], last_rest)
    far = None
    for r in range(0, groups - half, 2):
        out = add_odd(far_grads[r : r + 2])
        d_low = after(d_low, out)
        term = over("tensor", groups, out, half + r)
        far = term if far is None else far.astype(F32) + term.astype(F32)
    got = call(
        functools.partial(input_pull_kernel, (images, heads, width, half, 0, groups)),
        [x_own, d_low, d_branch, norms, normed1, valid_mask, projected, attended,
         router_part, *packs[:half]],
        [((own_tokens, D), BF16), ((8, D), F32)] + grads_out(half),
        scratch=[mask_pad], mib=MIB_PULL, in_specs=dict(zip((6, 7), half_heads[0])),
    )
    d_own, norm1_sums, near_bias = got[:3]
    head_grads = list(got[3:])
    for r in range(2, half, 2):
        term = over("tensor", groups, add_odd(head_grads[r : r + 2]), r)
        far = far.astype(F32) + term.astype(F32)
    near = core(head_grads[1], far)
    split = call(
        functools.partial(split_kernel, chunks),
        [head_grads[0], near, far], [((chunks, share, width), BF16)], mib=58,
    )[0]
    d_tokens = [d_own, core(d_own)] + [None] * (groups - 2)
    for r in range(2, groups, 2):
        d_tokens[r] = over("tensor", groups, d_own, r)
    pieces_in = lax.all_to_all(after(split, d_tokens[2]), "dp", 0, 0)
    mix_keep, mix_send = combine(mixed)
    mix_near = core(mix_send)

    def place_tokens(parts, places):
        placed = call(
            functools.partial(place_tokens_kernel, count, images, places),
            parts, [((SEQ * count, D), F32)],
            scratch=[pltpu.VMEM(tall, F32)],
        )[0]
        return jnp.transpose(placed.reshape(SEQ, count, D), (1, 0, 2))

    for r in range(2, groups, 2):
        d_tokens[r + 1] = core(d_tokens[r], split)

    def place_experts(came, pieces_here, first_row, shape, before=[]):
        steps = len(pieces_here)

        def piece_at(step):
            place = jnp.int32(0)
            for index, piece in enumerate(pieces_here):
                place = jnp.where(step == index, piece, place)
            return place

        spec = pl.BlockSpec((1, *shape), lambda step, s: (jnp.bitwise_xor(s[0], piece_at(step)), 0, 0))
        lines = pl.BlockSpec((1, 8, hidden_width), lambda step, s: (step, 0, 0))
        parts = [a for piece in came for a in piece]
        bias = [] if first_row else [((steps, 8, hidden_width), F32)]
        out_specs = {0: spec, 1: lines}
        if not first_row and steps == 1:
            bias, out_specs = [((local_experts, hidden_width), F32)], {0: spec}
        return call(
            functools.partial(
                place_experts_kernel, tuple(len(piece) for piece in came), first_row
            ),
            [*parts, *before], [((local_experts, *shape), F32)] + bias,
            grid=(steps,), out_specs=out_specs, left=[len(parts + before) - 1] if before else (),
            aliases={len(parts + before) - 1: 0} if before else None,
        )

    mix = call(
        mixture_kernel, [middle, mix_keep, mix_near], [((half * own_tokens, D), BF16)], mib=58,
    )[0]
    if shared:
        piece_rest = over("tensor", groups, grads[2][1], 2, d_tokens[2])
        mix = after(mix, piece_rest)
    mix_far = [over("tensor", groups, mix, r) for r in range(2, groups, 2)]
    d_inputs = place_tokens(d_tokens, [(r, 0) for r in range(groups)])
    if shared:
        whole = (0, 1, 3), [grads[0], [core(grads[1][0])], [core(last_top), core(last_rest)]]
        g_w_in, lines_in = place_experts(whole[1], whole[0], 0, (D, hidden_width))
        (g_w_back,) = place_experts(whole[1], whole[0], D + 16, (hidden_width, D))
    small = -(-(5 * D // LANES + 2 * groups + 1) // 8) * 8 + 8
    small = -(-small // 16) * 16
    message = call(
        functools.partial(join_kernel, (chunks, groups, half, width, small)),
        [pieces_in, norm1_sums, norm2_sums, forward_sums, sum(expert_sums), back_bias, near_bias,
         far_bias],
        [((chunks, share + 2 * small, width), BF16)], scratch=[pltpu.VMEM((small, LANES), F32)],
        mib=58,
    )[0]
    messages = lax.all_to_all(message, "dp", 0, 0)
    output_own, output_sums = call(
        functools.partial(output_kernel, images, groups),
        [middle, mix, valid_mask, *mix_far],
        [((half * own_tokens, D), BF16), ((8, LANES), F32)], scratch=[mask_pad],
    )
    out_near = core(output_own)
    output_sums = output_sums + over("dp", chunks, output_sums, 1)
    output = place_tokens([output_own, out_near], [(r % 2, r // 2) for r in range(groups)])
    output_sums = after(output_sums, output)
    by = 2
    while by < chunks:
        output_sums = output_sums + over("dp", chunks, output_sums, by)
        by *= 2
    top = small - 8
    qkv_sum, out_sum, sums = call(
        functools.partial(spread_kernel, (chunks, groups, width, small)),
        [messages, output_sums],
        [((3 * D, width), F32), ((width, D), F32),
         ((top + chunks * (D // LANES) + router_lines, LANES), F32)],
        scratch=[pltpu.VMEM((chunks * share, width), F32)],
    )
    by = 1
    while True:
        came = over("tensor", groups, sums, by)
        by *= 2
        if by == groups:
            break
        sums = jnp.concatenate([sums[:top] + came[:top], sums[top:], came[top:]], axis=0)

    if shared:
        last_piece = [[over("tensor", groups, grads[2][0], 2, mix_far[0]), piece_rest]]
        g_w_in, g_b_in = place_experts(
            last_piece, (2,), 0, (D, hidden_width), [lines_in, g_w_in]
        )
        (g_w_back,) = place_experts(last_piece, (2,), D + 16, (hidden_width, D), [g_w_back])
    else:
        g_w_in = grads[0][0][None, :D].astype(F32)
        g_w_back = grads[0][1][None].astype(F32)
        g_b_in = grads[0][0][D : D + 1].astype(F32)

    vector = [((1, D), F32)]
    (
        g_norm1_gain, g_norm1_bias, g_norm2_gain, g_norm2_bias, g_b_out, g_b_qv, router_grad,
        g_b_back, grad_norms, rms_values,
    ) = call(
        functools.partial(finish_kernel, (chunks, groups, half, small, shared)),
        [sums, came],
        vector * 5
        + [((2, LANES), F32), ((EXPERTS, D), F32), ((EXPERTS, D), F32)]
        + [((1, 13), F32), ((1, 5), F32)],
    )
    g_w_qkv = jnp.transpose(qkv_sum.reshape(3, D, width), (1, 0, 2))[:, :, :local_width]
    return (
        output, d_inputs, g_norm1_gain[0], g_norm1_bias[0], g_w_qkv, g_b_qv[:, :local_width],
        out_sum[:local_width], g_b_out[0], g_norm2_gain[0], g_norm2_bias[0],
        jnp.transpose(router_grad), g_w_in, g_b_in, g_w_back, g_b_back,
        grad_norms[0], rms_values[0],
    )


def solution(mesh):
    placed = (
        P("dp", None, None),
        P("dp", None),
        P("dp", None, None),
        P("dp", None, None),
        P(),
        P(),
        P(None, None, "tensor"),
        P(None, "tensor"),
        P("tensor", None),
        P(),
        P(),
        P(),
        P(),
        P("dp", None, "tensor"),
        P("dp", "tensor"),
        P("dp", "tensor", None),
        P(),
        P("dp", None, None),
    )
    return jax.shard_map(
        functools.partial(shards, dp_size=mesh.shape["dp"], tensor_size=mesh.shape["tensor"]),
        mesh=mesh,
        in_specs=placed,
        out_specs=(
            P("dp", None, None),
            P("dp", None, None),
            P(),
            P(),
            P(None, None, "tensor"),
            P(None, "tensor"),
            P("tensor", None),
            P(),
            P(),
            P(),
            P(),
            P("dp", None, "tensor"),
            P("dp", "tensor"),
            P("dp", "tensor", None),
            P(),
            P(),
            P(),
        ),
        check_vma=False,
    )
```
